32 devices in a mesh: rep: 2 (over x), fsdp: 4 (over z), seq: 4 (over y, core).
Axes of the slice: x: 2, y: 2, z: 4, core: 2. Of those that a mesh axis runs over, the one named last changes fastest.
Arguments:
- frames: bfloat16 [16, 1536, 768], P(('rep', 'fsdp'), 'seq'), may hold values from -6 to 6
- lengths: int32 [16], P(('rep', 'fsdp')), may hold values from 1152 to 1536, as said below
- cotangent: bfloat16 [16, 1536, 768], P(('rep', 'fsdp'), 'seq')
- dense_in: float32 [2, 768, 6144], P(None, ('fsdp', 'seq'))
- dense_out: float32 [2, 3072, 768], P(None, ('fsdp', 'seq')), may hold values from -0.109375 to 0.109375
- small_params: float32 [2, 12, 768], P(None, None, ('fsdp', 'seq'))
- first_in: float32 [2, 768, 6144], P(None, ('fsdp', 'seq'))
- first_out: float32 [2, 3072, 768], P(None, ('fsdp', 'seq'))
- first_small: float32 [2, 12, 768], P(None, None, ('fsdp', 'seq'))
- second_in: float32 [2, 768, 6144], P(None, ('fsdp', 'seq')), as said below
- second_out: float32 [2, 3072, 768], P(None, ('fsdp', 'seq')), as said below
- second_small: float32 [2, 12, 768], P(None, None, ('fsdp', 'seq')), as said below
Outputs:
- encoded: bfloat16 [16, 1536, 768], P(('rep', 'fsdp'), 'seq')
- frames_grad: float32 [16, 1536, 768], P(('rep', 'fsdp'), 'seq')
- grad_in: float32 [2, 768, 6144], P(None, ('fsdp', 'seq'))
- grad_out: float32 [2, 3072, 768], P(None, ('fsdp', 'seq'))
- grad_small: float32 [2, 12, 768], P(None, None, ('fsdp', 'seq'))
- moment_in: float32 [2, 768, 6144], P(None, ('fsdp', 'seq'))
- moment_out: float32 [2, 3072, 768], P(None, ('fsdp', 'seq'))
- moment_small: float32 [2, 12, 768], P(None, None, ('fsdp', 'seq'))
- square_in: float32 [2, 768, 6144], P(None, ('fsdp', 'seq'))
- square_out: float32 [2, 3072, 768], P(None, ('fsdp', 'seq'))
- square_small: float32 [2, 12, 768], P(None, None, ('fsdp', 'seq'))
- updated_in: float32 [2, 768, 6144], P(None, ('fsdp', 'seq'))
- updated_out: float32 [2, 3072, 768], P(None, ('fsdp', 'seq'))
- updated_small: float32 [2, 12, 768], P(None, None, ('fsdp', 'seq'))
The draws below stay inside these ranges and needn't reach their ends.
Inputs may be any that keep to these rules, and one draw needn't show every extreme that they name: `lengths`: counted from the start of the clip; of the 2 clips of each (rep, fsdp) pair one has exactly 1536. `second_in`: positive. `second_out`: positive. `second_small`: positive.
All inputs are finite; a program needn't handle non-finite values.
Results may differ from the reference program's by a relative error of at most 0.017.
The reference program's roundings to bfloat16 on the way count: a program that leaves them out, or rounds other values in their place, can miss the bound.
Values may be sent and summed in bfloat16 or wider, within the bound.
No kernel may reach another device: no remote copies, remote signals or barrier semaphores. Data moves between devices by JAX's collectives and lax.ppermute only.
A program may use at most 576 MiB of HBM per device.

```python
import math
import jax
import jax.numpy as jnp
from jax import lax

D = 768
FF = 3072
HEADS = 12
HDIM = 64
LAYERS = 2
FRAMES = 1536
CLIPS = 2
STEP = 10
GROUPS = 8
ALLCLIPS = 16
TOKENS = 24576
SMALL_ROWS = 12


def bell_noise(key, full_shape):
    return jnp.clip(jax.random.normal(key, full_shape, jnp.float32), -4.0, 4.0)


def spread_factor(key, full_shape):
    return jnp.exp(jax.random.uniform(key, full_shape, jnp.float32, math.log(0.5), math.log(2.0)))


def column_scale(scale_qk, scale_value, scale_wide, scale_ff):
    columns = jnp.arange(4 * D + FF)
    return jnp.where(columns < 2 * D, scale_qk, jnp.where(columns < 3 * D, scale_value, jnp.where(columns < 4 * D, scale_wide, scale_ff))).astype(jnp.float32)


def dense_grad_scale():
    return column_scale(0.6, 0.9, 1.6 * FRAMES ** (-0.5), 0.3) * math.sqrt(TOKENS)


def draw_lengths(key, part):
    key = jax.random.fold_in(key, 3)
    first_key, second_key = jax.random.split(key)
    drawn = jax.random.randint(first_key, (GROUPS, CLIPS), FRAMES - FRAMES // 4, FRAMES + 1)
    chosen = jax.random.randint(second_key, (GROUPS, 1), 0, CLIPS)
    slots = jnp.arange(CLIPS)[None, :]
    return jnp.where(slots == chosen, FRAMES, drawn).reshape(ALLCLIPS).astype(jnp.int32)


def draw_cotangent(key, part):
    key = jax.random.fold_in(key, 31)
    noise_key = jax.random.fold_in(key, 0)
    full_shape = (ALLCLIPS, FRAMES, D)
    return jnp.clip(jax.random.normal(noise_key, full_shape, jnp.float32), -6.0, 6.0).astype(jnp.bfloat16)


def draw_dense_in(key, part):
    key = jax.random.fold_in(key, 5)
    full_shape = (LAYERS, D, 4 * D + FF)
    base = bell_noise(key, full_shape)
    return base * column_scale(D ** (-0.5), D ** (-0.5), math.sqrt(FRAMES / (3.0 * D)), D ** (-0.5))


def draw_small_params(key, part):
    key = jax.random.fold_in(key, 7)
    full_shape = (LAYERS, SMALL_ROWS, D)
    base = bell_noise(key, full_shape)
    rows_index = jnp.arange(SMALL_ROWS)[None, :, None]
    gains = (rows_index == 0) | (rows_index == 5)
    return jnp.where(gains, 1.0 + 0.15 * base, 0.2 * base)


def draw_first_in(key, part):
    key = jax.random.fold_in(key, 11)
    full_shape = (LAYERS, D, 4 * D + FF)
    base = bell_noise(key, full_shape)
    return 0.1 * base * dense_grad_scale()


def draw_first_out(key, part):
    key = jax.random.fold_in(key, 13)
    full_shape = (LAYERS, FF, D)
    base = bell_noise(key, full_shape)
    return 0.1 * 0.65 * math.sqrt(TOKENS) * base


def draw_first_small(key, part):
    key = jax.random.fold_in(key, 17)
    full_shape = (LAYERS, SMALL_ROWS, D)
    base = bell_noise(key, full_shape)
    return 0.1 * 0.7 * math.sqrt(TOKENS) * base


def draw_second_in(key, part):
    key = jax.random.fold_in(key, 19)
    full_shape = (LAYERS, D, 4 * D + FF)
    grad_scale = dense_grad_scale()
    return 0.002 * grad_scale * grad_scale * spread_factor(key, full_shape)


def draw_second_out(key, part):
    key = jax.random.fold_in(key, 23)
    full_shape = (LAYERS, FF, D)
    return 0.002 * 0.65 * 0.65 * TOKENS * spread_factor(key, full_shape)


def draw_second_small(key, part):
    key = jax.random.fold_in(key, 29)
    full_shape = (LAYERS, SMALL_ROWS, D)
    return 0.002 * 0.7 * 0.7 * TOKENS * spread_factor(key, full_shape)


def level_of(key, shape, cuts, smallest, largest):
    factor_of = 1.0
    for position, blocks in cuts:
        steps = jax.random.uniform(jax.random.fold_in(jax.random.fold_in(key, 6), position), (blocks,), jnp.float32, smallest / len(cuts), largest / len(cuts))
        factor_of = factor_of * jnp.repeat(jnp.exp(steps), shape[position] // blocks).reshape((-1,) + (1,) * (len(shape) - 1 - position))
    return factor_of


def bell_draw(stream_key, extent, deviation, most, pieces=(), kind=jnp.bfloat16):
    values = deviation * jax.random.normal(stream_key, extent, jnp.float32)
    if pieces:
        values = values * level_of(stream_key, extent, pieces, -0.22, 0.18)
    return jnp.clip(values, -most, most).astype(kind)


def setup_inputs(seed: int = 0) -> dict:
    key_list = jax.random.split(jax.random.key(seed), 13)
    frames = bell_draw(key_list[0], (ALLCLIPS, FRAMES, D), 1.0, 6.0, ((0, 8), (1, 4)))
    lengths = draw_lengths(jax.random.fold_in(key_list[12], 71), 0)
    cotangent = draw_cotangent(jax.random.fold_in(key_list[12], 71), 0)
    dense_in = draw_dense_in(jax.random.fold_in(key_list[12], 71), 0)
    dense_out = bell_draw(key_list[4], (LAYERS, FF, D), FF ** -0.5, 0.109375, ((1, 16),), jnp.float32)
    small_params = draw_small_params(jax.random.fold_in(key_list[12], 71), 0)
    first_in = draw_first_in(jax.random.fold_in(key_list[12], 71), 0)
    first_out = draw_first_out(jax.random.fold_in(key_list[12], 71), 0)
    first_small = draw_first_small(jax.random.fold_in(key_list[12], 71), 0)
    second_in = draw_second_in(jax.random.fold_in(key_list[12], 71), 0)
    second_out = draw_second_out(jax.random.fold_in(key_list[12], 71), 0)
    second_small = draw_second_small(jax.random.fold_in(key_list[12], 71), 0)
    return {"frames": frames, "lengths": lengths, "cotangent": cotangent, "dense_in": dense_in, "dense_out": dense_out, "small_params": small_params, "first_in": first_in, "first_out": first_out, "first_small": first_small, "second_in": second_in, "second_out": second_out, "second_small": second_small}


@jax.custom_vjp
def low(v):
    return lax.optimization_barrier(v.astype(jnp.bfloat16)).astype(jnp.float32)

@jax.custom_vjp
def low_back(v):
    return v

def low_keep(v):
    return (low(v), None)

def low_pass(kept, grad):
    return (grad,)

def back_keep(v):
    return (v, None)

def back_low(kept, grad):
    return (low(grad),)
low.defvjp(low_keep, low_pass)
low_back.defvjp(back_keep, back_low)
HIGHEST_PRECISION = lax.Precision.HIGHEST
NORM_EPSILON = 1e-05
BETA_ONE = 0.9
BETA_TWO = 0.999
ADAM_EPSILON = 1e-08
DECAY_RATE = 0.01
RATE_DENSE = 0.1
RATE_OUTER = 0.05
RATE_SMALL = 0.5

def layer_norm(values_in, gain_row, shift_row):
    centred = values_in - lax.optimization_barrier(jnp.mean(values_in, axis=-1, keepdims=True))
    spread = lax.optimization_barrier(jnp.mean(centred * centred, axis=-1, keepdims=True))
    return centred * lax.rsqrt(spread + NORM_EPSILON) * gain_row + shift_row

def matmul(left_side, right_side):
    return jnp.dot(left_side, right_side, precision=HIGHEST_PRECISION, preferred_element_type=jnp.float32)

def encoder_layer(hidden, w_dense, w_outer, params, key_valid):
    w_dense = low(w_dense)
    w_outer = low(w_outer)
    params = low(params)
    model_width = hidden.shape[-1]
    frame_count = hidden.shape[0]
    zero_bias = jnp.zeros((model_width,), jnp.float32)
    normed = low(layer_norm(hidden, params[0], params[1]))
    projected = low(low_back(matmul(normed, w_dense[:, :3 * model_width]) + jnp.concatenate([params[2], zero_bias, params[3]])))
    queries = projected[:, :model_width].reshape(frame_count, HEADS, HDIM)
    key_heads = projected[:, model_width:2 * model_width].reshape(frame_count, HEADS, HDIM)
    value_heads = projected[:, 2 * model_width:].reshape(frame_count, HEADS, HDIM)
    logits = low_back(jnp.einsum('qhd,khd->hqk', queries, key_heads, precision=HIGHEST_PRECISION) * 0.125)
    logits = jnp.where(key_valid[None, None, :], logits, -1e+30)
    row_top = lax.optimization_barrier(jnp.max(logits, axis=-1, keepdims=True))
    weights_exp = jnp.exp(logits - row_top)
    chances = weights_exp / lax.optimization_barrier(jnp.sum(weights_exp, axis=-1, keepdims=True))
    mixed_out = jnp.einsum('hqk,khd->qhd', low(chances), value_heads, precision=HIGHEST_PRECISION).reshape(frame_count, model_width)
    mixed_out = low(low_back(mixed_out))
    branch = low_back(matmul(mixed_out, w_dense[:, 3 * model_width:4 * model_width]) + params[4])
    middle = hidden + branch
    second = low(layer_norm(middle, params[5], params[6]))
    inner_pre = low_back(matmul(second, w_dense[:, 4 * model_width:]) + params[8:].reshape(-1))
    active = low(jax.nn.gelu(inner_pre, approximate=False))
    outer = low_back(matmul(active, w_outer) + params[7])
    return middle + outer

def encoder(hidden, w_dense, w_outer, params, key_valid):
    for layer_index in range(LAYERS):
        hidden = encoder_layer(hidden, w_dense[layer_index], w_outer[layer_index], params[layer_index], key_valid)
    return hidden

def adam_step(weight, gradient, first, second, rate):
    moment = BETA_ONE * first + (1.0 - BETA_ONE) * gradient
    square = BETA_TWO * second + (1.0 - BETA_TWO) * gradient * gradient
    moment_hat = moment / (1.0 - BETA_ONE ** STEP)
    square_hat = square / (1.0 - BETA_TWO ** STEP)
    updated = weight - rate * (moment_hat / (jnp.sqrt(square_hat) + ADAM_EPSILON) + DECAY_RATE * weight)
    return (moment, square, updated)

def dense_rates(model_width, column_total, frame_total):
    columns = jnp.arange(column_total, dtype=jnp.int32)
    wide_rate = RATE_DENSE * math.sqrt(frame_total / 3.0)
    return jnp.where((columns >= 3 * model_width) & (columns < 4 * model_width), wide_rate, RATE_DENSE)

def reference(frames, lengths, cotangent, dense_in, dense_out, small_params, first_in, first_out, first_small, second_in, second_out, second_small):
    positions = jnp.arange(FRAMES, dtype=jnp.int32)

    def one_clip(totals, inputs):
        clip, length, upstream = inputs
        key_valid = positions < length

        def run(hidden, w_dense, w_outer, params):
            return encoder(hidden, w_dense, w_outer, params, key_valid)
        result, pullback = jax.vjp(run, clip.astype(jnp.float32), dense_in, dense_out, small_params)
        grads = pullback(upstream.astype(jnp.float32))
        totals = (totals[0] + grads[1], totals[1] + grads[2], totals[2] + grads[3])
        return (totals, (result.astype(jnp.bfloat16), grads[0]))
    zeros = (jnp.zeros_like(dense_in), jnp.zeros_like(dense_out), jnp.zeros_like(small_params))
    totals, outputs = lax.scan(one_clip, zeros, (frames, lengths, cotangent))
    encoded, frames_grad = outputs
    grad_in, grad_out, grad_small = totals
    rates = dense_rates(D, dense_in.shape[2], FRAMES)
    moment_in, square_in, updated_in = adam_step(dense_in, grad_in, first_in, second_in, rates)
    moment_out, square_out, updated_out = adam_step(dense_out, grad_out, first_out, second_out, RATE_OUTER)
    moment_small, square_small, updated_small = adam_step(small_params, grad_small, first_small, second_small, RATE_SMALL)
    return (encoded, frames_grad, grad_in, grad_out, grad_small, moment_in, moment_out, moment_small, square_in, square_out, square_small, updated_in, updated_out, updated_small)
```

```python
import functools
import math

import jax
import jax.numpy as jnp
from jax import lax
from jax.experimental import pallas as pl
from jax.experimental.pallas import tpu as pltpu
from jax.sharding import PartitionSpec as P

HDIM = 64
STEP = 10

NORM_EPSILON = 1e-05
BETA_ONE = 0.9
BETA_TWO = 0.999
ADAM_EPSILON = 1e-08
DECAY_RATE = 0.01
RATE_DENSE = 0.1
RATE_OUTER = 0.05
RATE_SMALL = 0.5
INV_ROOT_TWO = 0.7071067811865476
INV_ROOT_TAU = 0.3989422804014327
LOGIT_SCALE = 0.125
MASKED = -1e30
LANES = 128
VMEM_LIMIT = 56 * 2**20

F32 = jnp.float32
LOW = jnp.bfloat16


def norm_forward(values_in, gain_row, shift_row):
    centred = values_in - jnp.mean(values_in, axis=-1, keepdims=True)
    scale_inv = lax.rsqrt(jnp.mean(centred * centred, axis=-1, keepdims=True) + NORM_EPSILON)
    normal = centred * scale_inv
    return (normal * gain_row + shift_row, normal, scale_inv)


def norm_backward(upstream, gain_row, normal, scale_inv):
    scaled = upstream * gain_row
    inside = (
        scaled
        - jnp.mean(scaled, axis=-1, keepdims=True)
        - normal * jnp.mean(scaled * normal, axis=-1, keepdims=True)
    )
    return (scale_inv * inside, jnp.sum(upstream * normal, axis=0), jnp.sum(upstream, axis=0))


def gelu_slope(values_in):
    cumulative = 0.5 * (1.0 + lax.erf(values_in * INV_ROOT_TWO))
    return cumulative + values_in * jnp.exp(-0.5 * values_in * values_in) * INV_ROOT_TAU


def product(left_side, right_side):
    return jnp.dot(left_side, right_side, preferred_element_type=F32)


def outer_sum(left_side, right_side):
    return jnp.einsum("rf,rd->fd", left_side, right_side, preferred_element_type=F32)


def back_product(left_side, right_side):
    return jnp.einsum("rd,fd->rf", left_side, right_side, preferred_element_type=F32)


def adam_step(weight, gradient, first, second, rate):
    moment = BETA_ONE * first + (1.0 - BETA_ONE) * gradient
    square = BETA_TWO * second + (1.0 - BETA_TWO) * gradient * gradient
    moment_hat = moment / (1.0 - BETA_ONE**STEP)
    square_hat = square / (1.0 - BETA_TWO**STEP)
    updated = weight - rate * (
        moment_hat / (jnp.sqrt(square_hat) + ADAM_EPSILON) + DECAY_RATE * weight
    )
    return (moment, square, updated)


def query_block(rows):
    return next(size for size in (384, 256, 128) if rows % size == 0)


def attend_kernel(parts, block, bias_ref, q_ref, *refs):
    k_refs, v_refs = refs[:parts], refs[parts : 2 * parts]
    o_ref, lse_ref = refs[2 * parts :]
    rows = q_ref.shape[0]
    q_side = (q_ref[...] * jnp.bfloat16(LOGIT_SCALE)).T
    v_side = [ref[...].T for ref in v_refs]
    head_of = lax.broadcasted_iota(jnp.int32, (LANES, block), 0) // HDIM
    for start in range(0, rows, block):
        q_block = q_side[:, start : start + block]
        both = []
        for head in range(2):
            q_head = jnp.where(head_of == head, q_block, jnp.zeros_like(q_block))
            scores = []
            for part in range(parts):
                score = product(k_refs[part][...], q_head)
                lower, upper = score[: rows // 2], score[rows // 2 :]
                bias = jnp.tile(bias_ref[part], (1, block // LANES))
                scores.append(jnp.concatenate([lower, upper + bias], axis=0))
            top = functools.reduce(
                jnp.maximum, [jnp.max(score, axis=0, keepdims=True) for score in scores]
            )
            weights = [jnp.exp(score - top) for score in scores]
            total = sum(jnp.sum(weight, axis=0, keepdims=True) for weight in weights)
            mixed = sum(
                product(v_side[part][head * HDIM : (head + 1) * HDIM], weights[part].astype(LOW))
                for part in range(parts)
            )
            both.append(mixed / total)
            lse_ref[0, head : head + 1, start : start + block] = top + jnp.log(total)
        o_ref[start : start + block, :] = jnp.concatenate(both, axis=0).T.astype(LOW)


def attend(projected, others, bias):
    rows = projected.shape[0]
    width = projected.shape[1] // 3
    pairs = width // LANES
    parts = len(others) + 1

    def columns(base):
        return pl.BlockSpec((rows, LANES), lambda pair: (0, base * pairs + pair))

    return pl.pallas_call(
        functools.partial(attend_kernel, parts, query_block(rows)),
        grid=(pairs,),
        in_specs=[pl.BlockSpec(bias.shape, lambda pair: (0, 0, 0)), columns(0)]
        + [columns(1)]
        + [columns(0)] * (parts - 1)
        + [columns(2)]
        + [columns(1)] * (parts - 1),
        out_specs=[columns(0), pl.BlockSpec((1, 2, rows), lambda pair: (pair, 0, 0))],
        out_shape=[
            jax.ShapeDtypeStruct((rows, width), LOW),
            jax.ShapeDtypeStruct((pairs, 2, rows), F32),
        ],
        compiler_params=pltpu.CompilerParams(vmem_limit_bytes=VMEM_LIMIT),
        cost_estimate=pl.CostEstimate(
            flops=16 * rows * rows * parts * width,
            bytes_accessed=4 * rows * width * (1 + parts),
            transcendentals=rows * rows * parts * width // HDIM,
        ),
        name="attend",
    )(bias, projected, projected, *others, projected, *others)


def attend_back_kernel(parts, block, bias_ref, q_ref, *refs):
    k_refs, v_refs = refs[:parts], refs[parts : 2 * parts]
    o_ref, do_ref, lse_ref = refs[2 * parts : 2 * parts + 3]
    dq_ref = refs[2 * parts + 3]
    dk_refs = refs[2 * parts + 4 : 3 * parts + 4]
    dv_refs = refs[3 * parts + 4 :]
    rows = q_ref.shape[0]
    q_rows = q_ref[...] * jnp.bfloat16(LOGIT_SCALE)
    do_rows = do_ref[...]
    q_side, do_side = q_rows.T, do_rows.T
    shared = (do_rows.astype(F32) * o_ref[...].astype(F32)).T
    delta = [
        jnp.sum(shared[head * HDIM : (head + 1) * HDIM], axis=0, keepdims=True)
        for head in range(2)
    ]
    head_of = lax.broadcasted_iota(jnp.int32, (LANES, rows), 0) // HDIM
    zeros = jnp.zeros_like(q_side)
    q_heads = [jnp.where(head_of == head, q_side, zeros) for head in range(2)]
    do_heads = [jnp.where(head_of == head, do_side, zeros) for head in range(2)]
    lane = lax.broadcasted_iota(jnp.int32, (block, LANES), 1)
    dq_sides = [jnp.zeros((HDIM, rows), F32)] * 2
    for part in range(parts):
        for start in range(0, rows, block):
            here = slice(start, start + block)
            k_block, v_block = k_refs[part][here], v_refs[part][here]
            k_side = k_block.T
            dk_heads, dv_heads = [], []
            for head in range(2):
                score = product(k_block, q_heads[head])
                if start + block > rows // 2:
                    skip = max(rows // 2 - start, 0)
                    upper = bias_ref[part][start + skip - rows // 2 : start + block - rows // 2]
                    raised = score[skip:] + jnp.tile(upper, (1, rows // LANES))
                    score = jnp.concatenate([score[:skip], raised], axis=0) if skip else raised
                chances = jnp.exp(score - lse_ref[0, head : head + 1])
                chance_grad = product(v_block, do_heads[head])
                score_grad = (chances * (chance_grad - delta[head])).astype(LOW)
                dq_sides[head] = dq_sides[head] + product(
                    k_side[head * HDIM : (head + 1) * HDIM], score_grad
                )
                dk_heads.append(product(score_grad, q_rows))
                dv_heads.append(product(chances.astype(LOW), do_rows))
            dk_refs[part][here] = jnp.where(lane < HDIM, *dk_heads).astype(LOW)
            dv_refs[part][here] = jnp.where(lane < HDIM, *dv_heads).astype(LOW)
    dq_ref[...] = (jnp.concatenate(dq_sides, axis=0) * LOGIT_SCALE).T.astype(LOW)


def attend_back(projected, others, mixed_out, mixed_grad, log_total, bias):
    rows = projected.shape[0]
    width = projected.shape[1] // 3
    pairs = width // LANES
    parts = len(others) + 1

    def columns(base):
        return pl.BlockSpec((rows, LANES), lambda pair: (0, base * pairs + pair))

    out = pl.pallas_call(
        functools.partial(attend_back_kernel, parts, query_block(rows)),
        grid=(pairs,),
        in_specs=[pl.BlockSpec(bias.shape, lambda pair: (0, 0, 0)), columns(0)]
        + [columns(1)]
        + [columns(0)] * (parts - 1)
        + [columns(2)]
        + [columns(1)] * (parts - 1)
        + [columns(0), columns(0), pl.BlockSpec((1, 2, rows), lambda pair: (pair, 0, 0))],
        out_specs=[columns(0)] * (2 * parts + 1),
        out_shape=[jax.ShapeDtypeStruct((rows, width), LOW)] * (2 * parts + 1),
        compiler_params=pltpu.CompilerParams(vmem_limit_bytes=VMEM_LIMIT),
        cost_estimate=pl.CostEstimate(
            flops=40 * rows * rows * parts * width,
            bytes_accessed=8 * rows * width * (1 + parts),
            transcendentals=rows * rows * parts * width // HDIM,
        ),
        name="attend_back",
    )(bias, projected, projected, *others, projected, *others, mixed_out, mixed_grad, log_total)
    return out[0], out[1 : parts + 1], out[parts + 1 :]


def on_device(
    frames,
    lengths,
    cotangent,
    dense_in,
    dense_out,
    small_params,
    first_in,
    first_out,
    first_small,
    second_in,
    second_out,
    second_small,
):
    clip_count, local_frames, model_width = frames.shape
    layer_count = dense_in.shape[0]
    seq = lax.axis_size("seq")
    half = seq // clip_count
    total_frames = local_frames * seq
    place = lax.axis_index("seq")
    owners = seq * lax.axis_size("fsdp")
    my_clip, my_member = place // half, place % half
    in_lower = my_clip == 0
    swap = [(source, (source + half) % seq) for source in range(seq)]

    def to_clips(whole):
        kept = lax.dynamic_index_in_dim(whole, my_clip, 0, keepdims=False)
        given = lax.dynamic_index_in_dim(whole, 1 - my_clip, 0, keepdims=False)
        taken = lax.ppermute(given, "seq", swap)
        return jnp.concatenate(
            [jnp.where(in_lower, kept, taken), jnp.where(in_lower, taken, kept)], axis=0
        )

    def from_clips(rows):
        lower, upper = rows[:local_frames], rows[local_frames:]
        kept = jnp.where(in_lower, lower, upper)
        given = jnp.where(in_lower, upper, lower).astype(LOW)
        taken = lax.ppermute(given, "seq", swap).astype(rows.dtype)
        return jnp.stack([jnp.where(in_lower, kept, taken), jnp.where(in_lower, taken, kept)])

    def around(step):
        return [
            (source, source - source % half + (source % half + step) % half)
            for source in range(seq)
        ]

    length = lax.dynamic_index_in_dim(lengths, my_clip, 0, keepdims=False)
    bias = jnp.stack(
        [
            jnp.broadcast_to(
                jnp.where(
                    (half + (my_member - step) % half) * local_frames
                    + jnp.arange(local_frames, dtype=jnp.int32)
                    < length,
                    0.0,
                    MASKED,
                )[:, None],
                (local_frames, LANES),
            )
            for step in range(half)
        ]
    ).astype(F32)

    hidden = to_clips(frames).astype(F32)
    upstream = to_clips(cotangent).astype(F32)
    zero_bias = jnp.zeros((model_width,), F32)
    packed = lax.all_gather(small_params.astype(LOW), ("fsdp", "seq"), axis=2, tiled=True)
    stored = []
    for layer_index in range(layer_count):
        w_dense, w_outer = (
            lax.all_gather(
                dense_in[layer_index].astype(LOW), ("fsdp", "seq"), axis=0, tiled=True
            ),
            lax.all_gather(
                dense_out[layer_index].astype(LOW), ("fsdp", "seq"), axis=0, tiled=True
            ),
        )
        params = packed[layer_index].astype(F32)
        normed, normal_one, inv_one = norm_forward(hidden, params[0], params[1])
        normed_low = normed.astype(LOW)
        projected = (
            product(normed_low, w_dense[:, : 3 * model_width])
            + jnp.concatenate([params[2], zero_bias, params[3]])
        ).astype(LOW)
        pairs_out = projected[:, model_width:]
        others = [lax.ppermute(pairs_out, "seq", around(step)) for step in range(1, half)]
        mixed_out, log_total = attend(projected, others, bias)
        middle = hidden + (
            product(mixed_out, w_dense[:, 3 * model_width : 4 * model_width]) + params[4]
        )
        second, normal_two, inv_two = norm_forward(middle, params[5], params[6])
        second_low = second.astype(LOW)
        inner_pre = product(second_low, w_dense[:, 4 * model_width :]) + params[8:].reshape(-1)
        active = jax.nn.gelu(inner_pre, approximate=False).astype(LOW)
        hidden = middle + (product(active, w_outer) + params[7])
        stored.append(
            (
                w_dense,
                w_outer,
                params,
                normed_low,
                normal_one,
                inv_one,
                projected,
                others,
                log_total,
                mixed_out,
                normal_two,
                inv_two,
                second_low,
                inner_pre,
                active,
            )
        )
    encoded = from_clips(hidden.astype(LOW))
    owned_dense = []
    owned_outer = []
    small_grads = []
    for layer_index in reversed(range(layer_count)):
        (
            w_dense,
            w_outer,
            params,
            normed_low,
            normal_one,
            inv_one,
            projected,
            others,
            log_total,
            mixed_out,
            normal_two,
            inv_two,
            second_low,
            inner_pre,
            active,
        ) = stored[layer_index]
        outer_grad = upstream.astype(LOW)
        grad_w_outer = outer_sum(active, outer_grad)
        grad_b_outer = jnp.sum(outer_grad.astype(F32), axis=0)
        inner_grad = (back_product(outer_grad, w_outer) * gelu_slope(inner_pre)).astype(LOW)
        grad_w_inner = outer_sum(second_low, inner_grad)
        grad_b_inner = jnp.sum(inner_grad.astype(F32), axis=0)
        second_grad = back_product(inner_grad, w_dense[:, 4 * model_width :])
        lifted, grad_gain_two, grad_shift_two = norm_backward(
            second_grad, params[5], normal_two, inv_two
        )
        middle_grad = upstream + lifted
        branch_grad = middle_grad.astype(LOW)
        grad_w_mix = outer_sum(mixed_out, branch_grad)
        grad_b_mix = jnp.sum(branch_grad.astype(F32), axis=0)
        mixed_grad = back_product(
            branch_grad, w_dense[:, 3 * model_width : 4 * model_width]
        ).astype(LOW)
        query_grad, key_terms, value_terms = attend_back(
            projected, others, mixed_out, mixed_grad, log_total, bias
        )
        key_grad, value_grad = key_terms[0].astype(F32), value_terms[0].astype(F32)
        for step in range(1, half):
            key_grad += lax.ppermute(key_terms[step], "seq", around(half - step)).astype(F32)
            value_grad += lax.ppermute(value_terms[step], "seq", around(half - step)).astype(F32)
        projected_grad = jnp.concatenate(
            [query_grad, key_grad.astype(LOW), value_grad.astype(LOW)], axis=1
        )
        grad_w_qkv = outer_sum(normed_low, projected_grad)
        column_sums = jnp.sum(projected_grad.astype(F32), axis=0)
        first_grad = back_product(projected_grad, w_dense[:, : 3 * model_width])
        lowered, grad_gain_one, grad_shift_one = norm_backward(
            first_grad, params[0], normal_one, inv_one
        )
        upstream = middle_grad + lowered
        grad_dense_layer = jnp.concatenate([grad_w_qkv, grad_w_mix, grad_w_inner], axis=1)
        small_grads.insert(
            0,
            jnp.concatenate(
                [
                    jnp.stack(
                        [
                            grad_gain_one,
                            grad_shift_one,
                            column_sums[:model_width],
                            column_sums[2 * model_width :],
                            grad_b_mix,
                            grad_gain_two,
                            grad_shift_two,
                            grad_b_outer,
                        ]
                    ),
                    grad_b_inner.reshape(-1, model_width),
                ],
                axis=0,
            ),
        )
        part_dense, part_outer = (
            lax.psum_scatter(
                grad_dense_layer.astype(LOW), ("fsdp", "seq"), scatter_dimension=0, tiled=True
            ),
            lax.psum_scatter(
                grad_w_outer.astype(LOW), ("fsdp", "seq"), scatter_dimension=0, tiled=True
            ),
        )
        owned_dense.insert(0, part_dense)
        owned_outer.insert(0, part_outer)
    frames_grad = from_clips(upstream)
    small_all = jnp.stack(small_grads)
    small_all = small_all.reshape(small_all.shape[:2] + (owners, -1)).transpose(2, 0, 1, 3)
    owned_small = lax.psum_scatter(
        small_all, ("fsdp", "seq"), scatter_dimension=0, tiled=True
    ).reshape(small_params.shape)
    grad_in, grad_out, grad_small = (
        lax.psum(jnp.stack(owned_dense), "rep").astype(F32),
        lax.psum(jnp.stack(owned_outer), "rep").astype(F32),
        lax.psum(owned_small.astype(LOW), "rep").astype(F32),
    )
    columns = jnp.arange(dense_in.shape[2], dtype=jnp.int32)
    rates = jnp.where(
        (columns >= 3 * model_width) & (columns < 4 * model_width),
        RATE_DENSE * math.sqrt(total_frames / 3.0),
        RATE_DENSE,
    )
    moment_in, square_in, updated_in = adam_step(dense_in, grad_in, first_in, second_in, rates)
    moment_out, square_out, updated_out = adam_step(
        dense_out, grad_out, first_out, second_out, RATE_OUTER
    )
    moment_small, square_small, updated_small = adam_step(
        small_params, grad_small, first_small, second_small, RATE_SMALL
    )
    return (
        encoded,
        frames_grad,
        grad_in,
        grad_out,
        grad_small,
        moment_in,
        moment_out,
        moment_small,
        square_in,
        square_out,
        square_small,
        updated_in,
        updated_out,
        updated_small,
    )


def solution(mesh):
    clips = P(("rep", "fsdp"), "seq", None)
    rows = P(None, ("fsdp", "seq"), None)
    lanes = P(None, None, ("fsdp", "seq"))
    return jax.shard_map(
        on_device,
        mesh=mesh,
        in_specs=(clips, P(("rep", "fsdp")), clips) + (rows, rows, lanes) * 3,
        out_specs=(clips, clips) + (rows, rows, lanes) * 4,
        check_vma=False,
    )
```

```python
import functools
import math

import jax
import jax.numpy as jnp
from jax import lax
from jax.experimental import pallas as pl
from jax.experimental.pallas import tpu as pltpu
from jax.sharding import PartitionSpec as P

HDIM = 64
STEP = 10

NORM_EPSILON = 1e-05
BETA_ONE = 0.9
BETA_TWO = 0.999
ADAM_EPSILON = 1e-08
DECAY_RATE = 0.01
RATE_DENSE = 0.1
RATE_OUTER = 0.05
RATE_SMALL = 0.5
INV_ROOT_TWO = 0.7071067811865476
INV_ROOT_TAU = 0.3989422804014327
LOGIT_SCALE = 0.125
MASKED = -1e30
LANES = 128
VMEM_LIMIT = 60 * 2**20

F32 = jnp.float32
LOW = jnp.bfloat16


def adam_step(weight, gradient, first, second, rate):
    moment = BETA_ONE * first + (1.0 - BETA_ONE) * gradient
    square = BETA_TWO * second + (1.0 - BETA_TWO) * gradient * gradient
    moment_hat = moment / (1.0 - BETA_ONE**STEP)
    square_hat = square / (1.0 - BETA_TWO**STEP)
    updated = weight - rate * (
        moment_hat / (jnp.sqrt(square_hat) + ADAM_EPSILON) + DECAY_RATE * weight
    )
    return (moment, square, updated)


def product(left_side, right_side):
    return jnp.dot(left_side, right_side, preferred_element_type=F32)


def back_product(left_side, right_side):
    return lax.dot_general(
        left_side, right_side, (((1,), (1,)), ((), ())), preferred_element_type=F32
    )


def outer_sum(left_side, right_side):
    return lax.dot_general(
        left_side, right_side, (((0,), (0,)), ((), ())), preferred_element_type=F32
    )


def normalise(values_in):
    centred = values_in - jnp.mean(values_in, axis=-1, keepdims=True)
    scale_inv = lax.rsqrt(jnp.mean(centred * centred, axis=-1, keepdims=True) + NORM_EPSILON)
    return centred * scale_inv, scale_inv


def norm_backward(upstream, gain_row, normal, scale_inv):
    scaled = upstream * gain_row
    inside = (
        scaled
        - jnp.mean(scaled, axis=-1, keepdims=True)
        - normal * jnp.mean(scaled * normal, axis=-1, keepdims=True)
    )
    return (
        scale_inv * inside,
        jnp.sum(upstream * normal, axis=0, keepdims=True),
        jnp.sum(upstream, axis=0, keepdims=True),
    )


def run(kernel, name, steps, ins, outs, scratch, flops, after=(), scalar=None, reuse=()):
    in_arrays, in_specs = zip(*ins)
    out_shapes, out_specs = zip(*outs)
    moved = sum(a.size * a.dtype.itemsize for a in in_arrays)
    moved += sum(math.prod(s.shape) * s.dtype.itemsize for s in out_shapes)
    lead = 0 if scalar is None else 1

    spare = [*after, *reuse]
    aliases = {lead + len(ins) + len(after) + number: number for number in range(len(reuse))}

    def body(*refs):
        kernel(*refs[: lead + len(ins)], *refs[lead + len(ins) + len(spare) :])

    grid_spec = pltpu.PrefetchScalarGridSpec(
        num_scalar_prefetch=lead,
        grid=(steps,),
        in_specs=list(in_specs) + [pl.BlockSpec(memory_space=pl.ANY)] * len(spare),
        out_specs=list(out_specs),
        scratch_shapes=scratch,
    )
    return pl.pallas_call(
        body,
        grid_spec=grid_spec,
        out_shape=list(out_shapes),
        input_output_aliases=aliases,
        compiler_params=pltpu.CompilerParams(vmem_limit_bytes=VMEM_LIMIT),
        cost_estimate=pl.CostEstimate(flops=flops, bytes_accessed=moved, transcendentals=0),
        name=name,
    )(*(() if scalar is None else (scalar,)), *in_arrays, *spare)


def full(shape):
    return pl.BlockSpec(shape, lambda step, *_: (0,) * len(shape))


def scalars():
    return pl.BlockSpec(memory_space=pltpu.SMEM)


def unit_spec(chunk, block, unit_of):
    owners, _, width = chunk.shape
    return chunk, pl.BlockSpec((owners, block, width), lambda step, *_: (0, unit_of(step), 0))


def unit_of_ref(ref):
    return ref[...].reshape(-1, ref.shape[-1])


def row_spec(chunk, block, units, steps):
    owners, _, width = chunk.shape
    if owners == 1:
        return unit_spec(chunk, block, lambda step: units + step)
    spec = pl.BlockSpec((owners // steps, units * block, width), lambda step, *_: (step, 1, 0))
    return chunk, spec


def project_kernel(hidden_ref, params_ref, unit_ref, normed_ref, q_ref, kv_ref):
    step = pl.program_id(0)

    @pl.when(step == 0)
    def _():
        normal, _ = normalise(hidden_ref[...])
        normed_ref[...] = (normal * params_ref[0:1] + params_ref[1:2]).astype(LOW)

    weights = unit_of_ref(unit_ref)
    added = jnp.where(step == 0, params_ref[2:3], params_ref[3:4])
    added = jnp.where(step == 1, jnp.zeros_like(added), added)
    result = (product(normed_ref[...], weights) + added).astype(LOW)

    @pl.when(step == 0)
    def _():
        q_ref[...] = result

    @pl.when(step > 0)
    def _():
        kv_ref[...] = result


def project(hidden, params, chunk, block, first, after):
    rows, width = hidden.shape
    return run(
        project_kernel,
        "project",
        3,
        [
            (hidden, full(hidden.shape)),
            (params, full(params.shape)),
            unit_spec(chunk, block, lambda step: first + step),
        ],
        [
            (jax.ShapeDtypeStruct((rows, width), LOW), full((rows, width))),
            (jax.ShapeDtypeStruct((rows, width), LOW), full((rows, width))),
            (
                jax.ShapeDtypeStruct((rows, 2 * width), LOW),
                pl.BlockSpec((rows, width), lambda step, *_: (0, jnp.maximum(step - 1, 0))),
            ),
        ],
        [],
        6 * rows * width * width,
        after,
    )


def inner_kernel(
    hidden_ref, mixed_ref, params_ref, unit_ref, middle_ref, second_ref, active_ref, slope_ref
):
    step = pl.program_id(0)

    @pl.when(step == 0)
    def _():
        middle = hidden_ref[...] + (product(mixed_ref[...], unit_of_ref(unit_ref)) + params_ref[4:5])
        middle_ref[...] = middle
        normal, _ = normalise(middle)
        second_ref[...] = (normal * params_ref[5:6] + params_ref[6:7]).astype(LOW)

    @pl.when(step > 0)
    def _():
        inner = product(second_ref[...], unit_of_ref(unit_ref)) + params_ref[pl.ds(step + 7, 1), :]
        cumulative = 0.5 * (1.0 + lax.erf(inner * INV_ROOT_TWO))
        active_ref[...] = (inner * cumulative).astype(LOW)
        slope = cumulative + inner * jnp.exp(-0.5 * inner * inner) * INV_ROOT_TAU
        slope_ref[...] = slope.astype(LOW)


def inner(hidden, mixed_out, params, chunk, block, units, after):
    rows, width = hidden.shape
    wide = pl.BlockSpec((rows, width), lambda step, *_: (0, jnp.maximum(step - 1, 0)))
    return run(
        inner_kernel,
        "inner",
        units + 1,
        [
            (hidden, full(hidden.shape)),
            (mixed_out, full(mixed_out.shape)),
            (params, full(params.shape)),
            unit_spec(
                chunk, block, lambda step: jnp.where(step == 0, 2 * units, jnp.maximum(step - 1, 0))
            ),
        ],
        [
            (jax.ShapeDtypeStruct((rows, width), F32), full((rows, width))),
            (jax.ShapeDtypeStruct((rows, width), LOW), full((rows, width))),
            (jax.ShapeDtypeStruct((rows, units * width), LOW), wide),
            (jax.ShapeDtypeStruct((rows, units * width), LOW), wide),
        ],
        [],
        2 * (units + 1) * rows * width * width,
        after,
    )


def outer_kernel(middle_ref, active_ref, params_ref, piece_ref, out_ref):
    weights = unit_of_ref(piece_ref)
    term = product(active_ref[...], weights)

    @pl.when(pl.program_id(0) == 0)
    def _():
        out_ref[...] = middle_ref[...] + (term + params_ref[7:8])

    @pl.when(pl.program_id(0) > 0)
    def _():
        out_ref[...] += term


def outer(middle, active, params, chunk, block, units, steps, after):
    rows, width = middle.shape
    return run(
        outer_kernel,
        "outer",
        steps,
        [
            (middle, full(middle.shape)),
            (active, pl.BlockSpec((rows, units * width // steps), lambda step, *_: (0, step))),
            (params, full(params.shape)),
        ]
        + [row_spec(chunk, block, units, steps)],
        [(jax.ShapeDtypeStruct((rows, width), F32), full((rows, width)))],
        [],
        2 * units * rows * width * width,
        after,
    )[0]


def outer_back_kernel(
    upstream_ref, slope_ref, piece_ref, low_ref, inner_ref, bias_inner_ref, bias_outer_ref
):
    weights = unit_of_ref(piece_ref)

    @pl.when(pl.program_id(0) == 0)
    def _():
        low = upstream_ref[...].astype(LOW)
        low_ref[...] = low
        bias_outer_ref[...] = jnp.sum(low.astype(F32), axis=0, keepdims=True)

    grad = (back_product(low_ref[...], weights) * slope_ref[...].astype(F32)).astype(LOW)
    inner_ref[...] = grad
    bias_inner_ref[...] = jnp.sum(grad.astype(F32), axis=0, keepdims=True)


def outer_back(upstream, slope, chunk, block, units, steps, after):
    rows, width = upstream.shape
    share = units * width // steps
    return run(
        outer_back_kernel,
        "outer_back",
        steps,
        [
            (upstream, full(upstream.shape)),
            (slope, pl.BlockSpec((rows, share), lambda step, *_: (0, step))),
        ]
        + [row_spec(chunk, block, units, steps)],
        [
            (jax.ShapeDtypeStruct((rows, width), LOW), full((rows, width))),
            (
                jax.ShapeDtypeStruct((rows, units * width), LOW),
                pl.BlockSpec((rows, share), lambda step, *_: (0, step)),
            ),
            (
                jax.ShapeDtypeStruct((1, units * width), F32),
                pl.BlockSpec((1, share), lambda step, *_: (0, step)),
            ),
            (jax.ShapeDtypeStruct((1, width), F32), full((1, width))),
        ],
        [],
        2 * units * rows * width * width,
        after,
    )


def inner_back_kernel(
    units,
    inner_ref,
    upstream_ref,
    middle_ref,
    params_ref,
    unit_ref,
    middle_grad_ref,
    low_ref,
    mixed_grad_ref,
    sums_ref,
    total,
):
    step = pl.program_id(0)

    @pl.when(step == 0)
    def _():
        total[...] = jnp.zeros_like(total)

    @pl.when(step < units)
    def _():
        total[...] += back_product(inner_ref[...], unit_of_ref(unit_ref))

    @pl.when(step == units)
    def _():
        normal, scale_inv = normalise(middle_ref[...])
        lifted, gain, shift = norm_backward(total[...], params_ref[5:6], normal, scale_inv)
        middle_grad = upstream_ref[...] + lifted
        middle_grad_ref[...] = middle_grad
        low = middle_grad.astype(LOW)
        low_ref[...] = low
        sums_ref[0:1] = gain
        sums_ref[1:2] = shift
        sums_ref[2:3] = jnp.sum(low.astype(F32), axis=0, keepdims=True)
        sums_ref[3:8] = jnp.zeros((5, sums_ref.shape[1]), F32)
        mixed_grad_ref[...] = back_product(low, unit_of_ref(unit_ref)).astype(LOW)


def inner_back(inner_grad, upstream, middle, params, chunk, block, units, after):
    rows, width = upstream.shape
    return run(
        functools.partial(inner_back_kernel, units),
        "inner_back",
        units + 1,
        [
            (
                inner_grad,
                pl.BlockSpec((rows, width), lambda step, *_: (0, jnp.minimum(step, units - 1))),
            ),
            (upstream, full(upstream.shape)),
            (middle, full(middle.shape)),
            (params, full(params.shape)),
            unit_spec(chunk, block, lambda step: jnp.where(step == units, 2 * units, step)),
        ],
        [
            (jax.ShapeDtypeStruct((rows, width), F32), full((rows, width))),
            (jax.ShapeDtypeStruct((rows, width), LOW), full((rows, width))),
            (jax.ShapeDtypeStruct((rows, width), LOW), full((rows, width))),
            (jax.ShapeDtypeStruct((8, width), F32), full((8, width))),
        ],
        [pltpu.VMEM((rows, width), F32)],
        2 * (units + 1) * rows * width * width,
        after,
    )


def project_back_kernel(counts, hidden_ref, middle_grad_ref, params_ref, *refs):
    groups, parts = counts
    q_refs = refs[:groups]
    k_refs = refs[groups : groups * (parts + 1)]
    v_refs = refs[groups * (parts + 1) : groups * (2 * parts + 1)]
    unit_ref, grad_ref, out_ref, sums_ref, total = refs[groups * (2 * parts + 1) :]
    step = pl.program_id(0)
    weights = unit_of_ref(unit_ref)

    def joined(terms):
        columns = []
        for group in range(groups):
            term = terms[group][...]
            if len(terms) > groups:
                others = terms[groups + group :: groups]
                term = sum([other[...].astype(F32) for other in others], term.astype(F32))
            columns.append(term.astype(LOW))
        return jnp.concatenate(columns, axis=1)

    @pl.when(step == 0)
    def _():
        grad = joined(q_refs)
        grad_ref[...] = grad
        sums_ref[2:3] = jnp.sum(grad.astype(F32), axis=0, keepdims=True)
        total[...] = back_product(grad, weights)

    @pl.when(step == 1)
    def _():
        grad = joined(k_refs)
        grad_ref[...] = grad
        total[...] += back_product(grad, weights)

    @pl.when(step == 2)
    def _():
        grad = joined(v_refs)
        grad_ref[...] = grad
        sums_ref[3:4] = jnp.sum(grad.astype(F32), axis=0, keepdims=True)
        first_grad = total[...] + back_product(grad, weights)
        normal, scale_inv = normalise(hidden_ref[...])
        lowered, gain, shift = norm_backward(first_grad, params_ref[0:1], normal, scale_inv)
        out_ref[...] = middle_grad_ref[...] + lowered
        sums_ref[0:1] = gain
        sums_ref[1:2] = shift
        sums_ref[4:8] = jnp.zeros((4, sums_ref.shape[1]), F32)


def project_back(
    hidden, middle_grad, params, q_terms, k_terms, v_terms, chunk, block, first, after
):
    rows, width = hidden.shape
    whole = full((rows, width))
    groups, parts = len(q_terms), len(k_terms) // len(q_terms)
    return run(
        functools.partial(project_back_kernel, (groups, parts)),
        "project_back",
        3,
        [
            (hidden, whole),
            (middle_grad, whole),
            (params, full(params.shape)),
        ]
        + [(term, full(term.shape)) for term in q_terms + k_terms + v_terms]
        + [unit_spec(chunk, block, lambda step: first + step)],
        [
            (
                jax.ShapeDtypeStruct((rows, 3 * width), LOW),
                pl.BlockSpec((rows, width), lambda step, *_: (0, step)),
            ),
            (jax.ShapeDtypeStruct((rows, width), F32), whole),
            (jax.ShapeDtypeStruct((8, width), F32), full((8, width))),
        ],
        [pltpu.VMEM((rows, width), F32)],
        6 * rows * width * width,
        after,
    )


def grad_out(cut, units, width):
    if cut is None:
        shape, scratch = (units, width, width), []
        outs = [
            (
                jax.ShapeDtypeStruct(shape, LOW),
                pl.BlockSpec((1, width, width), lambda step, *_: (step, 0, 0)),
            )
        ]
    else:
        far, deep, block = cut
        shape = (far, deep, units, block, width)
        outs = [(jax.ShapeDtypeStruct(shape, LOW), full(shape))] * 2
        scratch = [pltpu.VMEM((deep, 2 * far, block, width), F32)]
    return outs, scratch


def split_unit(targets_ref, result, refs, unit):
    if len(refs) == 1:
        refs[0][0] = result.astype(LOW)
        return
    keep_ref, give_ref, held = refs
    held[...] = result.reshape(held.shape)
    far = keep_ref.shape[0]
    for near in range(far):
        keep_ref[near, :, unit] = held[:, targets_ref[near]].astype(LOW)
        give_ref[near, :, unit] = held[:, targets_ref[far + near]].astype(LOW)


def wide_grad_kernel(units, targets_ref, second_ref, inner_ref, active_ref, low_ref, *refs):
    step = pl.program_id(0)

    @pl.when(step < units)
    def _():
        split_unit(targets_ref, outer_sum(second_ref[...], inner_ref[...]), refs[:3], step)

    @pl.when(step >= units)
    def _():
        result = outer_sum(active_ref[...], low_ref[...])
        if len(refs) == 1:
            refs[0][0] = result.astype(LOW)
        else:
            keep_ref, give_ref, _, held = refs
            held[...] = result.reshape(held.shape)
            far = keep_ref.shape[0]
            for near in range(far):
                keep_ref[near, step - units] = held[targets_ref[near]].astype(LOW)
                give_ref[near, step - units] = held[targets_ref[far + near]].astype(LOW)


def wide_weight_grad(cut, targets, second_low, inner_grad, active, outer_low, units, after):
    rows, width = second_low.shape
    outs, scratch = grad_out(cut, 2 * units, width)
    steps = units
    if cut is not None:
        far, steps, block = cut
        shape = (far, steps, 2 * units, block, width)
        spec = pl.BlockSpec(
            (far, steps, units, block, width),
            lambda step, *_: (0, 0, jnp.where(step < units, 0, 1), 0, 0),
        )
        outs = [(jax.ShapeDtypeStruct(shape, LOW), spec)] * 2
        scratch = scratch + [pltpu.VMEM((2 * far, units, block, width), F32)]
    share = units * width // steps
    return run(
        functools.partial(wide_grad_kernel, units),
        "wide_weight_grad",
        units + steps,
        [
            (targets, scalars()),
            (second_low, full((rows, width))),
            (
                inner_grad,
                pl.BlockSpec((rows, width), lambda step, *_: (0, jnp.minimum(step, units - 1))),
            ),
            (
                active,
                pl.BlockSpec((rows, share), lambda step, *_: (0, jnp.maximum(step - units, 0))),
            ),
            (outer_low, full((rows, width))),
        ],
        outs,
        scratch,
        4 * units * rows * width * width,
        after,
    )


def thin_grad_kernel(targets_ref, normed_ref, grad_ref, mixed_ref, low_ref, *refs):
    step = pl.program_id(0)

    @pl.when(step < 3)
    def _():
        split_unit(targets_ref, outer_sum(normed_ref[...], grad_ref[...]), refs, step)

    @pl.when(step == 3)
    def _():
        split_unit(targets_ref, outer_sum(mixed_ref[...], low_ref[...]), refs, step)


def thin_weight_grad(cut, targets, normed_low, projected_grad, mixed_out, branch_low, after):
    rows, width = normed_low.shape
    outs, scratch = grad_out(cut, 4, width)
    whole = full((rows, width))
    return run(
        thin_grad_kernel,
        "thin_weight_grad",
        4,
        [
            (targets, scalars()),
            (normed_low, whole),
            (
                projected_grad,
                pl.BlockSpec((rows, width), lambda step, *_: (0, jnp.minimum(step, 2))),
            ),
            (mixed_out, whole),
            (branch_low, whole),
        ],
        outs,
        scratch,
        8 * rows * width * width,
        after,
    )


def sum_along_kernel(keep_ref, taken_ref, out_ref):
    out_ref[...] = (keep_ref[0].astype(F32) + taken_ref[0].astype(F32)).astype(LOW)


def sum_along(keep, taken, step_far, after):
    _, deep, units, block, width = keep.shape
    spec = pl.BlockSpec(
        (1, 1, units, block, width), lambda step, *_: (step_far, step, 0, 0, 0)
    )
    return run(
        sum_along_kernel,
        "sum_along",
        deep,
        [(keep, spec), (taken, spec)],
        [
            (
                jax.ShapeDtypeStruct((deep, units, block, width), LOW),
                pl.BlockSpec((1, units, block, width), lambda step, *_: (step, 0, 0, 0)),
            )
        ],
        [],
        2 * units * deep * block * width,
        after,
    )[0]


def sum_near_kernel(keep_ref, taken_ref, *refs):
    along, out_ref = refs[:-1], refs[-1]
    total = keep_ref[0].astype(F32) + taken_ref[0].astype(F32)
    for ref in along:
        total += ref[...].astype(F32)
    out_ref[...] = total.astype(LOW)


def sum_near(keep, taken, along, after):
    _, deep, units, block, width = keep.shape
    near = pl.BlockSpec((1, 1, units, block, width), lambda step, *_: (0, step, 0, 0, 0))
    spec = pl.BlockSpec((1, units, block, width), lambda step, *_: (step, 0, 0, 0))
    return run(
        sum_near_kernel,
        "sum_near",
        deep,
        [(keep, near), (taken, near)] + [(array, spec) for array in along],
        [(jax.ShapeDtypeStruct((deep, units, block, width), LOW), spec)],
        [],
        3 * units * deep * block * width,
        after,
    )[0]


def sum_deep_kernel(count, depth_ref, keep_ref, taken_ref, *refs):
    along, (own_ref, *send_refs) = refs[:count], refs[count:]
    total = keep_ref[0, 0].astype(F32) + taken_ref[0, 0].astype(F32)
    for ref in along:
        total += ref[0].astype(F32)
    step = pl.program_id(0)

    @pl.when(step == 0)
    def _():
        own_ref[...] = total

    for number, ref in enumerate(send_refs):

        @pl.when(step == number + 1)
        def _():
            ref[...] = total.astype(LOW)


def sum_deep(depth, keep, taken, along, after):
    _, deep, units, block, width = keep.shape
    near = pl.BlockSpec(
        (1, 1, units, block, width),
        lambda step, depth_ref: (0, lax.rem(depth_ref[0] + step, deep), 0, 0, 0),
    )
    spec = pl.BlockSpec(
        (1, units, block, width),
        lambda step, depth_ref: (lax.rem(depth_ref[0] + step, deep), 0, 0, 0),
    )
    shape = (units, block, width)
    return run(
        functools.partial(sum_deep_kernel, len(along)),
        "sum_deep",
        deep,
        [(keep, near), (taken, near)] + [(array, spec) for array in along],
        [(jax.ShapeDtypeStruct(shape, F32), full(shape))]
        + [(jax.ShapeDtypeStruct(shape, LOW), full(shape))] * (deep - 1),
        [],
        3 * units * deep * block * width,
        after,
        depth,
    )


def sum_last_kernel(own_ref, *refs):
    arrived, out_ref = refs[:-1], refs[-1]
    total = own_ref[...]
    for ref in arrived:
        total += ref[...].astype(F32)
    out_ref[...] = total.astype(LOW)


def sum_last(own, arrived, after):
    units, block, width = own.shape
    spec = pl.BlockSpec((1, block, width), lambda step, *_: (step, 0, 0))
    return run(
        sum_last_kernel,
        "sum_last",
        units,
        [(own, spec)] + [(array, spec) for array in arrived],
        [(jax.ShapeDtypeStruct(own.shape, LOW), spec)],
        [],
        4 * units * block * width,
        after,
    )[0]


def pack_kernel(wanted, units, layers, has_rows, *refs):
    count = len(layers)
    out_ref = refs[-1]
    rows_ref = refs[count] if has_rows else None
    block = refs[0].shape[1]
    width = out_ref.shape[1]
    at = 0
    for number, (layer, unit) in enumerate(wanted):
        if has_rows and number == units:
            out_ref[at : at + units * block] = rows_ref[0].astype(LOW)
            at += units * block
        source = refs[layers.index(layer)]
        out_ref[at : at + block] = source[0, :, unit * width : (unit + 1) * width].astype(LOW)
        at += block
    if at < out_ref.shape[0]:
        out_ref[at:] = refs[-2][...]


def pack(dense_in, dense_out, wanted, units, rows_of, extra, after):
    _, block, columns = dense_in.shape
    width = dense_out.shape[2]
    layers = sorted({layer for layer, _ in wanted})
    ins = [
        (dense_in, pl.BlockSpec((1, block, columns), lambda step, *_, layer=layer: (layer, 0, 0)))
        for layer in layers
    ]
    rows = len(wanted) * block
    if rows_of is not None:
        shape = (1,) + dense_out.shape[1:]
        ins.append((dense_out, pl.BlockSpec(shape, lambda step, *_: (rows_of, 0, 0))))
        rows += dense_out.shape[1]
    if extra is not None:
        ins.append((extra, full(extra.shape)))
        rows += extra.shape[0]
    return run(
        functools.partial(pack_kernel, wanted, units, layers, rows_of is not None),
        "pack",
        1,
        ins,
        [(jax.ShapeDtypeStruct((rows, width), LOW), full((rows, width)))],
        [],
        rows * width,
        after,
    )[0]


def small_cut_kernel(layers, block, targets_ref, *refs):
    keep_ref, give_ref, held = refs[-3:]
    _, deep, rows, _ = keep_ref.shape
    each = rows // layers
    keep_ref[...] = jnp.zeros_like(keep_ref)
    give_ref[...] = jnp.zeros_like(give_ref)
    for layer in range(layers):
        one, two, outer_sums, inner_sums = (ref[...] for ref in refs[4 * layer : 4 * layer + 4])
        width = one.shape[1]
        at = layer * each
        held[at : at + 4] = one[:4]
        held[at + 4 : at + 5] = two[2:3]
        held[at + 5 : at + 7] = two[:2]
        held[at + 7 : at + 8] = outer_sums
        for unit in range(each - 8):
            held[at + 8 + unit : at + 9 + unit] = inner_sums[:, unit * width : (unit + 1) * width]
    far = keep_ref.shape[0]
    for depth in range(deep):
        for near in range(far):
            for place in range(2 * far):
                start = (depth * 2 * far + place) * block

                @pl.when(targets_ref[near] == place)
                def _():
                    keep_ref[near, depth, :, :block] = held[:, start : start + block]

                @pl.when(targets_ref[far + near] == place)
                def _():
                    give_ref[near, depth, :, :block] = held[:, start : start + block]


def small_cut(cut, targets, parts, layers, after):
    far, deep, block = cut
    width = parts[0].shape[1]
    rows = layers * (8 + parts[3].shape[1] // width)
    shape = (far, deep, rows, LANES)
    return run(
        functools.partial(small_cut_kernel, layers, block),
        "small_cut",
        1,
        [(targets, scalars())] + [(part, full(part.shape)) for part in parts],
        [(jax.ShapeDtypeStruct(shape, F32), full(shape))] * 2,
        [pltpu.VMEM((rows, width), F32)],
        rows * width,
        after,
    )


def adam_kernel(usual, special, chosen, weight_ref, first_ref, second_ref, *refs):
    grads, (grad_ref, moment_ref, square_ref, updated_ref) = refs[:-4], refs[-4:]
    grad = sum([ref[0].astype(F32) for ref in grads[1:]], grads[0][0].astype(F32))
    grad = grad.reshape(weight_ref.shape)
    rate = jnp.where(pl.program_id(0) == chosen, special, usual)
    moment, square, updated = adam_step(weight_ref[...], grad, first_ref[...], second_ref[...], rate)
    grad_ref[...] = grad
    moment_ref[...] = moment
    square_ref[...] = square
    updated_ref[...] = updated


def adam(state, grads, layer, first, count, from_unit, rates, after, reuse):
    weight = state[0]
    block, width = grads[0].shape[1:]
    if weight.ndim == 3:
        spec = pl.BlockSpec((1, block, width), lambda step, *_: (layer, 0, first + step))
    else:
        spec = pl.BlockSpec((1, 1, block, width), lambda step, *_: (layer, first + step, 0, 0))
    usual, special, chosen = rates
    return run(
        functools.partial(adam_kernel, usual, special, chosen - first),
        "adam",
        count,
        [(array, spec) for array in state]
        + [
            (grad, pl.BlockSpec((1, block, width), lambda step, *_: (from_unit + step, 0, 0)))
            for grad in grads
        ],
        [(jax.ShapeDtypeStruct(weight.shape, F32), spec)] * 4,
        [],
        16 * count * block * width,
        after,
        None,
        reuse,
    )


def query_block(rows):
    return next(size for size in (384, 256, 128) if rows % size == 0)


def attend_kernel(parts, block, bias_ref, q_ref, *refs):
    k_refs, v_refs = refs[:parts], refs[parts : 2 * parts]
    o_ref, lse_ref = refs[2 * parts :]
    rows = q_ref.shape[0]
    q_side = (q_ref[...] * jnp.bfloat16(LOGIT_SCALE)).T
    v_side = [ref[...].T for ref in v_refs]
    head_of = lax.broadcasted_iota(jnp.int32, (LANES, block), 0) // HDIM
    for start in range(0, rows, block):
        q_block = q_side[:, start : start + block]
        both = []
        for head in range(2):
            q_head = jnp.where(head_of == head, q_block, jnp.zeros_like(q_block))
            scores = []
            for part in range(parts):
                score = product(k_refs[part][...], q_head)
                lower, upper = score[: rows // 2], score[rows // 2 :]
                bias = jnp.tile(bias_ref[part], (1, block // LANES))
                scores.append(jnp.concatenate([lower, upper + bias], axis=0))
            top = functools.reduce(
                jnp.maximum, [jnp.max(score, axis=0, keepdims=True) for score in scores]
            )
            weights = [jnp.exp(score - top) for score in scores]
            total = sum(jnp.sum(weight, axis=0, keepdims=True) for weight in weights)
            mixed = sum(
                product(v_side[part][head * HDIM : (head + 1) * HDIM], weights[part].astype(LOW))
                for part in range(parts)
            )
            both.append(mixed / total)
            lse_ref[0, head : head + 1, start : start + block] = top + jnp.log(total)
        o_ref[start : start + block, :] = jnp.concatenate(both, axis=0).T.astype(LOW)


def attend(queries, own, others, bias, after):
    rows, width = queries.shape
    pairs = width // LANES
    parts = len(others) + 1

    def columns(base):
        return pl.BlockSpec((rows, LANES), lambda pair, *_: (0, base * pairs + pair))

    return run(
        functools.partial(attend_kernel, parts, query_block(rows)),
        "attend",
        pairs,
        [(bias, full(bias.shape)), (queries, columns(0))]
        + [(array, columns(0)) for array in (own, *others)]
        + [(array, columns(1)) for array in (own, *others)],
        [
            (jax.ShapeDtypeStruct((rows, width), LOW), columns(0)),
            (
                jax.ShapeDtypeStruct((pairs, 2, rows), F32),
                pl.BlockSpec((1, 2, rows), lambda pair, *_: (pair, 0, 0)),
            ),
        ],
        [],
        16 * rows * rows * parts * width,
        after,
    )


def attend_back_kernel(parts, block, bias_ref, q_ref, *refs):
    k_refs, v_refs = refs[:parts], refs[parts : 2 * parts]
    o_ref, do_ref, lse_ref = refs[2 * parts : 2 * parts + 3]
    dq_ref = refs[2 * parts + 3]
    dk_refs = refs[2 * parts + 4 : 3 * parts + 4]
    dv_refs = refs[3 * parts + 4 :]
    rows = q_ref.shape[0]
    q_rows = q_ref[...] * jnp.bfloat16(LOGIT_SCALE)
    do_rows = do_ref[...]
    q_side, do_side = q_rows.T, do_rows.T
    shared = (do_rows.astype(F32) * o_ref[...].astype(F32)).T
    delta = [
        jnp.sum(shared[head * HDIM : (head + 1) * HDIM], axis=0, keepdims=True)
        for head in range(2)
    ]
    head_of = lax.broadcasted_iota(jnp.int32, (LANES, rows), 0) // HDIM
    zeros = jnp.zeros_like(q_side)
    q_heads = [jnp.where(head_of == head, q_side, zeros) for head in range(2)]
    do_heads = [jnp.where(head_of == head, do_side, zeros) for head in range(2)]
    lane = lax.broadcasted_iota(jnp.int32, (block, LANES), 1)
    dq_sides = [jnp.zeros((HDIM, rows), F32)] * 2
    for part in range(parts):
        for start in range(0, rows, block):
            here = slice(start, start + block)
            k_block, v_block = k_refs[part][here], v_refs[part][here]
            k_side = k_block.T
            dk_heads, dv_heads = [], []
            for head in range(2):
                score = product(k_block, q_heads[head])
                if start + block > rows // 2:
                    skip = max(rows // 2 - start, 0)
                    upper = bias_ref[part][start + skip - rows // 2 : start + block - rows // 2]
                    raised = score[skip:] + jnp.tile(upper, (1, rows // LANES))
                    score = jnp.concatenate([score[:skip], raised], axis=0) if skip else raised
                chances = jnp.exp(score - lse_ref[0, head : head + 1])
                chance_grad = product(v_block, do_heads[head])
                score_grad = (chances * (chance_grad - delta[head])).astype(LOW)
                dq_sides[head] = dq_sides[head] + product(
                    k_side[head * HDIM : (head + 1) * HDIM], score_grad
                )
                dk_heads.append(product(score_grad, q_rows))
                dv_heads.append(product(chances.astype(LOW), do_rows))
            dk_refs[part][here] = jnp.where(lane < HDIM, *dk_heads).astype(LOW)
            dv_refs[part][here] = jnp.where(lane < HDIM, *dv_heads).astype(LOW)
    dq_ref[...] = (jnp.concatenate(dq_sides, axis=0) * LOGIT_SCALE).T.astype(LOW)


def attend_back(queries, own, others, mixed_out, mixed_grad, log_total, bias, group, groups, after):
    rows, width = queries.shape
    pairs = width // LANES
    parts = len(others) + 1
    first = group * pairs // groups
    count = (group + 1) * pairs // groups - first

    def columns(base):
        return pl.BlockSpec((rows, LANES), lambda pair, *_: (0, base * pairs + first + pair))

    out = run(
        functools.partial(attend_back_kernel, parts, query_block(rows)),
        "attend_back",
        count,
        [(bias, full(bias.shape)), (queries, columns(0))]
        + [(array, columns(0)) for array in (own, *others)]
        + [(array, columns(1)) for array in (own, *others)]
        + [
            (mixed_out, columns(0)),
            (mixed_grad, columns(0)),
            (log_total, pl.BlockSpec((1, 2, rows), lambda pair, *_: (first + pair, 0, 0))),
        ],
        [
            (
                jax.ShapeDtypeStruct((rows, count * LANES), LOW),
                pl.BlockSpec((rows, LANES), lambda pair, *_: (0, pair)),
            )
        ]
        * (2 * parts + 1),
        [],
        40 * rows * rows * parts * count * LANES,
        after,
    )
    return out[0], out[1 : parts + 1], out[parts + 1 :]


def on_device(
    frames,
    lengths,
    cotangent,
    dense_in,
    dense_out,
    small_params,
    first_in,
    first_out,
    first_small,
    second_in,
    second_out,
    second_small,
):
    clip_count, local_frames, width = frames.shape
    layer_count, block, columns_in = dense_in.shape
    units = columns_in // width - 4
    seq, deep, reps = lax.axis_size("seq"), lax.axis_size("fsdp"), lax.axis_size("rep")
    half = seq // clip_count
    total_frames = local_frames * seq
    place, depth = lax.axis_index("seq"), lax.axis_index("fsdp")
    owners = seq * deep
    my_clip, my_member = place // half, place % half
    in_lower = my_clip == 0
    swap = [(source, (source + half) % seq) for source in range(seq)]
    far = seq // 2
    row, core = place // 2, place % 2
    cut = (far, deep, block) if block % 16 == 0 else None
    depth_at = depth.astype(jnp.int32).reshape(1)

    def turn(axis, step):
        size = lax.axis_size(axis)
        return [(source, (source + step) % size) for source in range(size)]

    over_core = [(source, source ^ 1) for source in range(seq)]

    def to_clips(arrays):
        whole = jnp.stack(arrays, axis=1)
        kept = lax.dynamic_index_in_dim(whole, my_clip, 0, keepdims=False)
        given = lax.dynamic_index_in_dim(whole, 1 - my_clip, 0, keepdims=False)
        taken = lax.ppermute(given, "seq", swap)
        lower, upper = jnp.where(in_lower, kept, taken), jnp.where(in_lower, taken, kept)
        return [
            jnp.concatenate([lower[number], upper[number]], axis=0).astype(F32)
            for number in range(len(arrays))
        ]

    def split_clips(rows):
        lower, upper = rows[:local_frames], rows[local_frames:]
        return jnp.where(in_lower, lower, upper), jnp.where(in_lower, upper, lower).astype(LOW)

    def from_clips(kept, given):
        taken = lax.ppermute(given, "seq", swap).astype(kept.dtype)
        return jnp.stack([jnp.where(in_lower, kept, taken), jnp.where(in_lower, taken, kept)])

    def around(step):
        return [
            (source, source - source % half + (source % half + step) % half)
            for source in range(seq)
        ]

    def gather(wanted, rows_of, extra, after):
        if cut is not None:
            own = pack(dense_in, dense_out, wanted, units, rows_of, extra, after)
            return lax.all_gather(own, ("fsdp", "seq"), axis=0)
        columns = jnp.stack(
            [
                dense_in[layer, :, unit * width : (unit + 1) * width].astype(LOW)
                for layer, unit in wanted
            ]
        )
        columns = lax.all_gather(columns, ("fsdp", "seq"), axis=1, tiled=True)
        columns = columns.reshape(-1, width)
        if rows_of is not None:
            rows = lax.all_gather(
                dense_out[rows_of].astype(LOW), ("fsdp", "seq"), axis=0, tiled=True
            )
            columns = jnp.concatenate(
                [columns[: units * width], rows, columns[units * width :]]
            )
        return columns[None]

    targets = jnp.stack(
        [
            (row + step) % far * 2 + (core + other) % 2
            for other in range(2)
            for step in range(far)
        ]
    )

    def start_core(parts):
        if cut is None:
            return parts, []
        return (parts[0], lax.ppermute(parts[1], "seq", over_core)), [parts[0]]

    def start_far(chunk, after):
        if cut is None:
            return chunk
        keep, taken = chunk[0]
        sums = [sum_along(keep, taken, step, after) for step in range(1, far)]
        moved = [
            lax.ppermute(part, "seq", turn("seq", 2 * step + 2)) for step, part in enumerate(sums)
        ]
        return (keep, taken, moved), sums

    def start_deep(chunk, after):
        if cut is None:
            return chunk
        own, *sends = sum_deep(depth_at, *chunk[0], after)
        arrived = [
            lax.ppermute(part, "fsdp", turn("fsdp", step + 1)) for step, part in enumerate(sends)
        ]
        return (own, arrived), [own]

    def whole_deep(chunk, after):
        if cut is None:
            return chunk
        total = sum_near(*chunk[0], after)
        return lax.psum_scatter(total, "fsdp", scatter_dimension=0, tiled=True)[0], [total]

    def start_reps(chunk, after):
        if cut is None:
            result = chunk[0][0]
            owned = lax.psum_scatter(
                result[:units], ("fsdp", "seq"), scatter_dimension=1, tiled=True
            )
            if result.shape[0] > units:
                rows = lax.psum_scatter(
                    result[units:].reshape(units * width, width),
                    ("fsdp", "seq"),
                    scatter_dimension=0,
                    tiled=True,
                )
                owned = jnp.concatenate([owned, rows.reshape(units, block, width)])
        elif isinstance(chunk[0], tuple):
            owned = sum_last(*chunk[0], after)
        else:
            owned = chunk[0]
        return owned, [lax.ppermute(owned, "rep", turn("rep", step)) for step in range(1, reps)]

    def finish(state):
        owned, arrived = state
        return sum([part.astype(F32) for part in arrived], owned.astype(F32))

    length = lax.dynamic_index_in_dim(lengths, my_clip, 0, keepdims=False)
    bias = jnp.stack(
        [
            jnp.broadcast_to(
                jnp.where(
                    (half + (my_member - step) % half) * local_frames
                    + jnp.arange(local_frames, dtype=jnp.int32)
                    < length,
                    0.0,
                    MASKED,
                )[:, None],
                (local_frames, LANES),
            )
            for step in range(half)
        ]
    ).astype(F32)

    thin_units = range(3)
    small_low = small_params.astype(LOW)
    extra = None
    if cut is not None:
        extra = jnp.pad(small_low.reshape(-1), (0, -small_low.size % (16 * width)))
        extra = extra.reshape(-1, width)
    chunks = [gather([(0, unit) for unit in thin_units], None, extra, [])]
    for layer in range(layer_count):
        wanted = [(layer, 4 + unit) for unit in range(units)] + [(layer, 3)]
        if layer + 1 < layer_count:
            wanted += [(layer + 1, unit) for unit in thin_units]
        chunks.append(gather(wanted, layer, None, []))
    if cut is None:
        params_all = lax.all_gather(small_low, ("fsdp", "seq"), axis=2, tiled=True)
        block_in = width
    else:
        params_all = chunks[0][:, 3 * block :].reshape(owners, -1)[:, : small_low.size]
        params_all = params_all.reshape((owners,) + small_low.shape).transpose(1, 2, 0, 3)
        params_all = params_all.reshape(layer_count, -1, width)
        block_in = block
    params_all = params_all.astype(F32)

    row_steps = units if cut is None else deep
    hidden, upstream = to_clips([frames, cotangent])
    stored = []
    thin_at = [(chunks[0], 0)] + [
        (chunks[layer], 2 * units + 1) for layer in range(1, layer_count)
    ]
    for layer_index in range(layer_count):
        params = params_all[layer_index]
        thin, wide = thin_at[layer_index], chunks[layer_index + 1]
        normed_low, queries, own = project(hidden, params, thin[0], block_in, thin[1], [])
        others = [lax.ppermute(own, "seq", around(step)) for step in range(1, half)]
        mixed_out, log_total = attend(queries, own, others, bias, [])
        middle, second_low, active, slope = inner(
            hidden, mixed_out, params, wide, block_in, units, []
        )
        stored.append(
            (hidden, normed_low, queries, own, others, log_total, mixed_out)
            + (middle, second_low, active, slope)
        )
        hidden = outer(middle, active, params, wide, block_in, units, row_steps, [])
    encoded = from_clips(*split_clips(hidden.astype(LOW)))
    groups = 2 if width // LANES % 2 == 0 else 1
    order = [hidden]
    waiting = None
    parts_out = {}
    small_grads = []
    for layer_index in reversed(range(layer_count)):
        thin, wide = thin_at[layer_index], chunks[layer_index + 1]
        params = params_all[layer_index]
        (
            hidden,
            normed_low,
            queries,
            own,
            others,
            log_total,
            mixed_out,
            middle,
            second_low,
            active,
            slope,
        ) = stored[layer_index]
        outer_low, inner_grad, bias_inner, bias_outer = outer_back(
            upstream, slope, wide, block_in, units, row_steps, order
        )
        order = [inner_grad]
        if waiting:
            waiting = start_far(waiting, order)
            order = order + waiting[1]
        wide_part = start_core(
            wide_weight_grad(
                cut, targets, second_low, inner_grad, active, outer_low, units, order
            )
        )
        middle_grad, branch_low, mixed_grad, sums_two = inner_back(
            inner_grad, upstream, middle, params, wide, block_in, units, wide_part[1]
        )
        order = [middle_grad]
        wide_part = start_far(wide_part, order)
        order = order + wide_part[1]
        if waiting:
            waiting = whole_deep(waiting, order)
            order = order + waiting[1]
        q_terms, k_near, v_near, k_far, v_far = [], [], [], [], []
        for group in range(groups):
            q_term, k_terms, v_terms = attend_back(
                queries,
                own,
                others,
                mixed_out,
                mixed_grad,
                log_total,
                bias,
                group,
                groups,
                order,
            )
            q_terms.append(q_term)
            k_near.append(k_terms[0])
            v_near.append(v_terms[0])
            k_far.append(k_terms[1:])
            v_far.append(v_terms[1:])
            order = [q_term]

        def joined(near, terms):
            moved = [
                lax.ppermute(terms[group][step - 1], "seq", around(half - step))
                for step in range(1, half)
                for group in range(groups)
            ]
            return list(near) + moved

        projected_grad, upstream, sums_one = project_back(
            hidden,
            middle_grad,
            params,
            q_terms,
            joined(k_near, k_far),
            joined(v_near, v_far),
            thin[0],
            block_in,
            thin[1],
            [],
        )
        order = [projected_grad]
        if waiting:
            waiting = start_reps(waiting, order)
            parts_out[layer_index + 1] += (waiting,)
        wide_part = whole_deep(wide_part, order)
        order = order + wide_part[1]
        if layer_index == 0:
            clips_back = split_clips(upstream)
            order = order + [clips_back[1]]
        waiting = start_core(
            thin_weight_grad(
                cut, targets, normed_low, projected_grad, mixed_out, branch_low, order
            )
        )
        order = waiting[1]
        parts_out[layer_index] = (start_reps(wide_part, order),)
        small_grads = [sums_one, sums_two, bias_outer, bias_inner] + small_grads
    rows_shape = (layer_count, units, block, width)
    states_in = (dense_in, first_in, second_in)
    states_out = [array.reshape(rows_shape) for array in (dense_out, first_out, second_out)]
    rates_in = (RATE_DENSE, RATE_DENSE * math.sqrt(total_frames / 3.0), 3)
    rates_out = (RATE_OUTER, RATE_OUTER, 0)

    def flat(part):
        return [part[0]] + part[1]

    waiting = start_far(waiting, [])
    order = waiting[1]
    frames_grad = from_clips(*clips_back)
    done_in, done_out = (), ()
    for layer in reversed(range(1, layer_count)):
        wide_part, thin_part = parts_out[layer]
        done_in = adam(states_in, flat(thin_part), layer, 0, 4, 0, rates_in, order, done_in)
        done_in = adam(states_in, flat(wide_part), layer, 4, units, 0, rates_in, order, done_in)
        done_out = adam(
            states_out, flat(wide_part), layer, 0, units, units, rates_out, order, done_out
        )
    wide_part = parts_out[0][0]
    if cut is None:
        small_all = jnp.stack(
            [
                jnp.concatenate([one[:4], two[2:3], two[:2], outer_sums])
                for one, two, outer_sums, _ in zip(*[iter(small_grads)] * 4)
            ]
        )
        inner_all = jnp.stack([part.reshape(units, width) for part in small_grads[3::4]])
        small_all = jnp.concatenate([small_all, inner_all], axis=1)
        small_all = small_all.reshape(layer_count, -1, owners, block).transpose(2, 0, 1, 3)
        owned_small = lax.psum_scatter(
            small_all, ("fsdp", "seq"), scatter_dimension=0, tiled=True
        )
    else:
        keep, give = small_cut(cut, targets, small_grads, layer_count, order)
        cuts = keep + lax.ppermute(give, "seq", over_core)
        total = cuts[0]
        for step in range(1, far):
            total += lax.ppermute(cuts[step], "seq", turn("seq", 2 * step))
        owned_small = lax.dynamic_index_in_dim(total, depth, 0, keepdims=False)
        for step in range(1, deep):
            owned_small += lax.ppermute(
                lax.dynamic_index_in_dim(total, (depth + step) % deep, 0, keepdims=False),
                "fsdp",
                turn("fsdp", step),
            )
        owned_small = owned_small[:, :block]
    owned_small = owned_small.reshape(small_params.shape).astype(LOW)
    waiting = start_deep(waiting, list(done_in[:1]) + [wide_part[0]])
    order = waiting[1]
    done_in = adam(states_in, flat(wide_part), 0, 4, units, 0, rates_in, order, done_in)
    done_out = adam(states_out, flat(wide_part), 0, 0, units, units, rates_out, order, done_out)
    thin_part = start_reps(waiting, [done_in[0]])
    done_in = adam(states_in, flat(thin_part), 0, 0, 4, 0, rates_in, [], done_in)
    grad_in, moment_in, square_in, updated_in = done_in
    grad_out_rows, moment_out, square_out, updated_out = (
        array.reshape(dense_out.shape) for array in done_out
    )
    grad_small = finish(
        (owned_small, [lax.ppermute(owned_small, "rep", turn("rep", s)) for s in range(1, reps)])
    )
    moment_small, square_small, updated_small = adam_step(
        small_params, grad_small, first_small, second_small, RATE_SMALL
    )
    return (
        encoded,
        frames_grad,
        grad_in,
        grad_out_rows,
        grad_small,
        moment_in,
        moment_out,
        moment_small,
        square_in,
        square_out,
        square_small,
        updated_in,
        updated_out,
        updated_small,
    )


def solution(mesh):
    clips = P(("rep", "fsdp"), "seq", None)
    rows = P(None, ("fsdp", "seq"), None)
    lanes = P(None, None, ("fsdp", "seq"))
    return jax.shard_map(
        on_device,
        mesh=mesh,
        in_specs=(clips, P(("rep", "fsdp")), clips) + (rows, rows, lanes) * 3,
        out_specs=(clips, clips) + (rows, rows, lanes) * 4,
        check_vma=False,
    )
```

```python
import functools
import math

import jax
import jax.numpy as jnp
from jax import lax
from jax.experimental import pallas as pl
from jax.experimental.pallas import tpu as pltpu
from jax.sharding import PartitionSpec as P

HDIM = 64
STEP = 10

NORM_EPSILON = 1e-05
BETA_ONE = 0.9
BETA_TWO = 0.999
ADAM_EPSILON = 1e-08
DECAY_RATE = 0.01
RATE_DENSE = 0.1
RATE_OUTER = 0.05
RATE_SMALL = 0.5
INV_ROOT_TWO = 0.7071067811865476
INV_ROOT_TAU = 0.3989422804014327
LOGIT_SCALE = 0.125
MASKED = -1e30
LANES = 128
VMEM_LIMIT = 60 * 2**20

F32 = jnp.float32
LOW = jnp.bfloat16


def adam_step(weight, gradient, first, second, rate):
    moment = BETA_ONE * first + (1.0 - BETA_ONE) * gradient
    square = BETA_TWO * second + (1.0 - BETA_TWO) * gradient * gradient
    moment_hat = moment / (1.0 - BETA_ONE**STEP)
    square_hat = square / (1.0 - BETA_TWO**STEP)
    updated = weight - rate * (
        moment_hat / (jnp.sqrt(square_hat) + ADAM_EPSILON) + DECAY_RATE * weight
    )
    return (moment, square, updated)


def product(left_side, right_side):
    return jnp.dot(left_side, right_side, preferred_element_type=F32)


def back_product(left_side, right_side):
    return lax.dot_general(
        left_side, right_side, (((1,), (1,)), ((), ())), preferred_element_type=F32
    )


def outer_sum(left_side, right_side):
    return lax.dot_general(
        left_side, right_side, (((0,), (0,)), ((), ())), preferred_element_type=F32
    )


def normalise(values_in):
    centred = values_in - jnp.mean(values_in, axis=-1, keepdims=True)
    scale_inv = lax.rsqrt(jnp.mean(centred * centred, axis=-1, keepdims=True) + NORM_EPSILON)
    return centred * scale_inv, scale_inv


def norm_backward(upstream, gain_row, normal, scale_inv):
    scaled = upstream * gain_row
    inside = (
        scaled
        - jnp.mean(scaled, axis=-1, keepdims=True)
        - normal * jnp.mean(scaled * normal, axis=-1, keepdims=True)
    )
    return (
        scale_inv * inside,
        jnp.sum(upstream * normal, axis=0, keepdims=True),
        jnp.sum(upstream, axis=0, keepdims=True),
    )


def run(kernel, name, steps, ins, outs, scratch, flops, after=(), scalar=None, reuse=()):
    in_arrays, in_specs = zip(*ins)
    out_shapes, out_specs = zip(*outs)
    moved = sum(a.size * a.dtype.itemsize for a in in_arrays)
    moved += sum(math.prod(s.shape) * s.dtype.itemsize for s in out_shapes)
    lead = 0 if scalar is None else 1

    spare = [*after, *reuse]
    aliases = {lead + len(ins) + len(after) + number: number for number in range(len(reuse))}

    def body(*refs):
        kernel(*refs[: lead + len(ins)], *refs[lead + len(ins) + len(spare) :])

    grid_spec = pltpu.PrefetchScalarGridSpec(
        num_scalar_prefetch=lead,
        grid=(steps,),
        in_specs=list(in_specs) + [pl.BlockSpec(memory_space=pl.ANY)] * len(spare),
        out_specs=list(out_specs),
        scratch_shapes=scratch,
    )
    return pl.pallas_call(
        body,
        grid_spec=grid_spec,
        out_shape=list(out_shapes),
        input_output_aliases=aliases,
        compiler_params=pltpu.CompilerParams(vmem_limit_bytes=VMEM_LIMIT),
        cost_estimate=pl.CostEstimate(flops=flops, bytes_accessed=moved, transcendentals=0),
        name=name,
    )(*(() if scalar is None else (scalar,)), *in_arrays, *spare)


def full(shape):
    return pl.BlockSpec(shape, lambda step, *_: (0,) * len(shape))


def scalars():
    return pl.BlockSpec(memory_space=pltpu.SMEM)


def unit_spec(chunk, block, unit_of):
    owners, _, width = chunk.shape
    return chunk, pl.BlockSpec((owners, block, width), lambda step, *_: (0, unit_of(step), 0))


def unit_of_ref(ref):
    return ref[...].reshape(-1, ref.shape[-1])


class Wide:
    def __init__(self, chunk, sent, info, block, units):
        self.chunk, self.sent, self.info = chunk, sent, info
        self.block, self.units = block, units
        self.held = units // 2 if sent else units
        self.mix_at = 2 * self.held
        self.thin_at = self.mix_at + 1

    def mix_spec(self):
        return unit_spec(self.chunk, self.block, lambda step: self.mix_at)

    def inner_specs(self, unit_of):
        arrays = (self.chunk, *self.sent[0]) if self.sent else (self.chunk,)
        return [
            unit_spec(array, self.block, lambda step: lax.rem(unit_of(step), self.held))
            for array in arrays
        ]

    def inner_scratch(self):
        owners, _, width = self.chunk.shape
        return [pltpu.VMEM((owners, self.block, width), LOW)] if self.sent else []

    def outer_specs(self, steps):
        owners, _, width = self.chunk.shape
        if owners == 1:
            return [unit_spec(self.chunk, self.block, lambda step: self.units + step)]
        shape = (owners // steps, self.held * self.block, width)
        specs = [(self.chunk, pl.BlockSpec(shape, lambda step, *_: (step, 1, 0)))]
        if self.sent:
            near = pl.BlockSpec(shape, lambda step, *_: (lax.rem(step, steps // 2), 0, 0))
            specs += [(array, near) for array in self.sent[1]]
        return specs

    def outer_scratch(self, steps):
        owners, _, width = self.chunk.shape
        shape = (owners // steps, self.units * self.block, width)
        return [pltpu.VMEM(shape, LOW)] if self.sent else []

    def count(self):
        return 3 if self.sent else 1


def inner_unit(info_ref, refs, held, half):
    if len(refs) == 1:
        return unit_of_ref(refs[0])
    mine_ref, near_ref, far_ref = refs
    count = near_ref.shape[0]

    @pl.when(info_ref[0] == half)
    def _():
        held[...] = mine_ref[...]

    for core in range(2):

        @pl.when((info_ref[0] != half) & (info_ref[1] == core))
        def _():
            held[core * count : (core + 1) * count] = near_ref[...]
            held[(1 - core) * count : (2 - core) * count] = far_ref[...]

    return unit_of_ref(held)


def outer_unit(info_ref, refs, held, step, steps):
    if len(refs) == 1:
        return unit_of_ref(refs[0])
    mine_ref, near_ref, far_ref = refs
    count = mine_ref.shape[1]
    is_near = step // (steps // 2) == info_ref[1]
    for rep in range(2):

        @pl.when(info_ref[0] == rep)
        def _():
            held[:, rep * count : (rep + 1) * count] = mine_ref[...]

        for ref, wanted in ((near_ref, is_near), (far_ref, jnp.logical_not(is_near))):

            @pl.when((info_ref[0] == rep) & wanted)
            def _():
                held[:, (1 - rep) * count : (2 - rep) * count] = ref[...]

    return unit_of_ref(held)


def project_kernel(hidden_ref, params_ref, unit_ref, normed_ref, q_ref, kv_ref):
    step = pl.program_id(0)

    @pl.when(step == 0)
    def _():
        normal, _ = normalise(hidden_ref[...])
        normed_ref[...] = (normal * params_ref[0:1] + params_ref[1:2]).astype(LOW)

    weights = unit_of_ref(unit_ref)
    added = jnp.where(step == 0, params_ref[2:3], params_ref[3:4])
    added = jnp.where(step == 1, jnp.zeros_like(added), added)
    result = (product(normed_ref[...], weights) + added).astype(LOW)

    @pl.when(step == 0)
    def _():
        q_ref[...] = result

    @pl.when(step > 0)
    def _():
        kv_ref[...] = result


def project(hidden, params, chunk, block, first, after):
    rows, width = hidden.shape
    return run(
        project_kernel,
        "project",
        3,
        [
            (hidden, full(hidden.shape)),
            (params, full(params.shape)),
            unit_spec(chunk, block, lambda step: first + step),
        ],
        [
            (jax.ShapeDtypeStruct((rows, width), LOW), full((rows, width))),
            (jax.ShapeDtypeStruct((rows, width), LOW), full((rows, width))),
            (
                jax.ShapeDtypeStruct((rows, 2 * width), LOW),
                pl.BlockSpec((rows, width), lambda step, *_: (0, jnp.maximum(step - 1, 0))),
            ),
        ],
        [],
        6 * rows * width * width,
        after,
    )


def inner_kernel(count, per_half, info_ref, hidden_ref, mixed_ref, params_ref, mix_ref, *refs):
    unit_refs, refs = refs[:count], refs[count:]
    middle_ref, second_ref, active_ref, slope_ref, *held = refs
    step = pl.program_id(0)

    @pl.when(step == 0)
    def _():
        middle = hidden_ref[...] + (product(mixed_ref[...], unit_of_ref(mix_ref)) + params_ref[4:5])
        middle_ref[...] = middle
        normal, _ = normalise(middle)
        second_ref[...] = (normal * params_ref[5:6] + params_ref[6:7]).astype(LOW)

    @pl.when(step > 0)
    def _():
        weights = inner_unit(info_ref, unit_refs, held[0] if held else None, (step - 1) // per_half)
        inner = product(second_ref[...], weights) + params_ref[pl.ds(step + 7, 1), :]
        cumulative = 0.5 * (1.0 + lax.erf(inner * INV_ROOT_TWO))
        active_ref[...] = (inner * cumulative).astype(LOW)
        slope = cumulative + inner * jnp.exp(-0.5 * inner * inner) * INV_ROOT_TAU
        slope_ref[...] = slope.astype(LOW)


def inner(hidden, mixed_out, params, wide, after):
    units = wide.units
    rows, width = hidden.shape
    spread = pl.BlockSpec((rows, width), lambda step, *_: (0, jnp.maximum(step - 1, 0)))
    return run(
        functools.partial(inner_kernel, wide.count(), max(units // 2, 1)),
        "inner",
        units + 1,
        [
            (wide.info, scalars()),
            (hidden, full(hidden.shape)),
            (mixed_out, full(mixed_out.shape)),
            (params, full(params.shape)),
            wide.mix_spec(),
        ]
        + wide.inner_specs(lambda step: jnp.maximum(step - 1, 0)),
        [
            (jax.ShapeDtypeStruct((rows, width), F32), full((rows, width))),
            (jax.ShapeDtypeStruct((rows, width), LOW), full((rows, width))),
            (jax.ShapeDtypeStruct((rows, units * width), LOW), spread),
            (jax.ShapeDtypeStruct((rows, units * width), LOW), spread),
        ],
        wide.inner_scratch(),
        2 * (units + 1) * rows * width * width,
        after,
    )


def outer_kernel(count, steps, info_ref, middle_ref, active_ref, params_ref, *refs):
    unit_refs, (out_ref, *held) = refs[:count], refs[count:]
    weights = outer_unit(
        info_ref, unit_refs, held[0] if held else None, pl.program_id(0), steps
    )
    term = product(active_ref[...], weights)

    @pl.when(pl.program_id(0) == 0)
    def _():
        out_ref[...] = middle_ref[...] + (term + params_ref[7:8])

    @pl.when(pl.program_id(0) > 0)
    def _():
        out_ref[...] += term


def outer(middle, active, params, wide, steps, after):
    units = wide.units
    rows, width = middle.shape
    return run(
        functools.partial(outer_kernel, wide.count(), steps),
        "outer",
        steps,
        [
            (wide.info, scalars()),
            (middle, full(middle.shape)),
            (active, pl.BlockSpec((rows, units * width // steps), lambda step, *_: (0, step))),
            (params, full(params.shape)),
        ]
        + wide.outer_specs(steps),
        [(jax.ShapeDtypeStruct((rows, width), F32), full((rows, width)))],
        wide.outer_scratch(steps),
        2 * units * rows * width * width,
        after,
    )[0]


def outer_back_kernel(count, steps, info_ref, upstream_ref, slope_ref, *refs):
    unit_refs, refs = refs[:count], refs[count:]
    low_ref, inner_ref, bias_inner_ref, bias_outer_ref, *held = refs
    weights = outer_unit(
        info_ref, unit_refs, held[0] if held else None, pl.program_id(0), steps
    )

    @pl.when(pl.program_id(0) == 0)
    def _():
        low = upstream_ref[...].astype(LOW)
        low_ref[...] = low
        bias_outer_ref[...] = jnp.sum(low.astype(F32), axis=0, keepdims=True)

    grad = (back_product(low_ref[...], weights) * slope_ref[...].astype(F32)).astype(LOW)
    inner_ref[...] = grad
    bias_inner_ref[...] = jnp.sum(grad.astype(F32), axis=0, keepdims=True)


def outer_back(upstream, slope, wide, steps, after):
    units = wide.units
    rows, width = upstream.shape
    share = units * width // steps
    return run(
        functools.partial(outer_back_kernel, wide.count(), steps),
        "outer_back",
        steps,
        [
            (wide.info, scalars()),
            (upstream, full(upstream.shape)),
            (slope, pl.BlockSpec((rows, share), lambda step, *_: (0, step))),
        ]
        + wide.outer_specs(steps),
        [
            (jax.ShapeDtypeStruct((rows, width), LOW), full((rows, width))),
            (
                jax.ShapeDtypeStruct((rows, units * width), LOW),
                pl.BlockSpec((rows, share), lambda step, *_: (0, step)),
            ),
            (
                jax.ShapeDtypeStruct((1, units * width), F32),
                pl.BlockSpec((1, share), lambda step, *_: (0, step)),
            ),
            (jax.ShapeDtypeStruct((1, width), F32), full((1, width))),
        ],
        wide.outer_scratch(steps),
        2 * units * rows * width * width,
        after,
    )


def inner_back_kernel(
    count, units, info_ref, inner_ref, upstream_ref, middle_ref, params_ref, mix_ref, *refs
):
    unit_refs, refs = refs[:count], refs[count:]
    middle_grad_ref, low_ref, mixed_grad_ref, sums_ref, total, *held = refs
    step = pl.program_id(0)

    @pl.when(step == 0)
    def _():
        total[...] = jnp.zeros_like(total)

    @pl.when(step < units)
    def _():
        weights = inner_unit(
            info_ref, unit_refs, held[0] if held else None, step // max(units // 2, 1)
        )
        total[...] += back_product(inner_ref[...], weights)

    @pl.when(step == units)
    def _():
        normal, scale_inv = normalise(middle_ref[...])
        lifted, gain, shift = norm_backward(total[...], params_ref[5:6], normal, scale_inv)
        middle_grad = upstream_ref[...] + lifted
        middle_grad_ref[...] = middle_grad
        low = middle_grad.astype(LOW)
        low_ref[...] = low
        sums_ref[0:1] = gain
        sums_ref[1:2] = shift
        sums_ref[2:3] = jnp.sum(low.astype(F32), axis=0, keepdims=True)
        sums_ref[3:8] = jnp.zeros((5, sums_ref.shape[1]), F32)
        mixed_grad_ref[...] = back_product(low, unit_of_ref(mix_ref)).astype(LOW)


def inner_back(inner_grad, upstream, middle, params, wide, after):
    units = wide.units
    rows, width = upstream.shape
    return run(
        functools.partial(inner_back_kernel, wide.count(), units),
        "inner_back",
        units + 1,
        [
            (wide.info, scalars()),
            (
                inner_grad,
                pl.BlockSpec((rows, width), lambda step, *_: (0, jnp.minimum(step, units - 1))),
            ),
            (upstream, full(upstream.shape)),
            (middle, full(middle.shape)),
            (params, full(params.shape)),
            wide.mix_spec(),
        ]
        + wide.inner_specs(lambda step: jnp.minimum(step, units - 1)),
        [
            (jax.ShapeDtypeStruct((rows, width), F32), full((rows, width))),
            (jax.ShapeDtypeStruct((rows, width), LOW), full((rows, width))),
            (jax.ShapeDtypeStruct((rows, width), LOW), full((rows, width))),
            (jax.ShapeDtypeStruct((8, width), F32), full((8, width))),
        ],
        [pltpu.VMEM((rows, width), F32)] + wide.inner_scratch(),
        2 * (units + 1) * rows * width * width,
        after,
    )


def joined(terms, groups):
    columns = []
    for group in range(groups):
        term = terms[group][...]
        if len(terms) > groups:
            others = terms[groups + group :: groups]
            term = sum([other[...].astype(F32) for other in others], term.astype(F32))
        columns.append(term.astype(LOW))
    return jnp.concatenate(columns, axis=1)


def split_terms(refs, counts):
    groups, parts = counts
    ends = (groups, groups * (parts + 1), groups * (2 * parts + 1))
    return [refs[: ends[0]], refs[ends[0] : ends[1]], refs[ends[1] : ends[2]]], refs[ends[2] :]


def project_back_kernel(counts, hidden_ref, middle_grad_ref, params_ref, *refs):
    terms, (unit_ref, out_ref, sums_ref, total) = split_terms(refs, counts)
    step = pl.program_id(0)
    weights = unit_of_ref(unit_ref)

    @pl.when(step == 0)
    def _():
        grad = joined(terms[0], counts[0])
        sums_ref[2:3] = jnp.sum(grad.astype(F32), axis=0, keepdims=True)
        total[...] = back_product(grad, weights)

    @pl.when(step == 1)
    def _():
        total[...] += back_product(joined(terms[1], counts[0]), weights)

    @pl.when(step == 2)
    def _():
        grad = joined(terms[2], counts[0])
        sums_ref[3:4] = jnp.sum(grad.astype(F32), axis=0, keepdims=True)
        first_grad = total[...] + back_product(grad, weights)
        normal, scale_inv = normalise(hidden_ref[...])
        lowered, gain, shift = norm_backward(first_grad, params_ref[0:1], normal, scale_inv)
        out_ref[...] = middle_grad_ref[...] + lowered
        sums_ref[0:1] = gain
        sums_ref[1:2] = shift
        sums_ref[4:8] = jnp.zeros((4, sums_ref.shape[1]), F32)


def project_back(hidden, middle_grad, params, terms, chunk, block, first, after):
    rows, width = hidden.shape
    whole = full((rows, width))
    counts = (len(terms[0]), len(terms[1]) // len(terms[0]))
    return run(
        functools.partial(project_back_kernel, counts),
        "project_back",
        3,
        [
            (hidden, whole),
            (middle_grad, whole),
            (params, full(params.shape)),
        ]
        + [(term, full(term.shape)) for some in terms for term in some]
        + [unit_spec(chunk, block, lambda step: first + step)],
        [
            (jax.ShapeDtypeStruct((rows, width), F32), whole),
            (jax.ShapeDtypeStruct((8, width), F32), full((8, width))),
        ],
        [pltpu.VMEM((rows, width), F32)],
        6 * rows * width * width,
        after,
    )


def grad_out(cut, units, width):
    if cut is None:
        shape, scratch = (units, width, width), []
        outs = [
            (
                jax.ShapeDtypeStruct(shape, LOW),
                pl.BlockSpec((1, width, width), lambda step, *_: (step, 0, 0)),
            )
        ]
    else:
        far, deep, block = cut
        shape = (far, deep, units, block, width)
        outs = [(jax.ShapeDtypeStruct(shape, LOW), full(shape))] * 2
        scratch = [pltpu.VMEM((deep, 2 * far, block, width), F32)]
    return outs, scratch


def split_unit(targets_ref, result, refs, unit):
    if len(refs) == 1:
        refs[0][0] = result.astype(LOW)
        return
    keep_ref, give_ref, held = refs
    held[...] = result.reshape(held.shape)
    far = keep_ref.shape[0]
    for near in range(far):
        keep_ref[near, :, unit] = held[:, targets_ref[near]].astype(LOW)
        give_ref[near, :, unit] = held[:, targets_ref[far + near]].astype(LOW)


def wide_grad_kernel(units, targets_ref, second_ref, inner_ref, active_ref, low_ref, *refs):
    step = pl.program_id(0)

    @pl.when(step < units)
    def _():
        split_unit(targets_ref, outer_sum(second_ref[...], inner_ref[...]), refs[:3], step)

    @pl.when(step >= units)
    def _():
        result = outer_sum(active_ref[...], low_ref[...])
        if len(refs) == 1:
            refs[0][0] = result.astype(LOW)
        else:
            keep_ref, give_ref, _, held = refs
            held[...] = result.reshape(held.shape)
            far = keep_ref.shape[0]
            for near in range(far):
                keep_ref[near, step - units] = held[targets_ref[near]].astype(LOW)
                give_ref[near, step - units] = held[targets_ref[far + near]].astype(LOW)


def wide_weight_grad(cut, targets, second_low, inner_grad, active, outer_low, units, after):
    rows, width = second_low.shape
    outs, scratch = grad_out(cut, 2 * units, width)
    steps = units
    if cut is not None:
        far, steps, block = cut
        shape = (far, steps, 2 * units, block, width)
        spec = pl.BlockSpec(
            (far, steps, units, block, width),
            lambda step, *_: (0, 0, jnp.where(step < units, 0, 1), 0, 0),
        )
        outs = [(jax.ShapeDtypeStruct(shape, LOW), spec)] * 2
        scratch = scratch + [pltpu.VMEM((2 * far, units, block, width), F32)]
    share = units * width // steps
    return run(
        functools.partial(wide_grad_kernel, units),
        "wide_weight_grad",
        units + steps,
        [
            (targets, scalars()),
            (second_low, full((rows, width))),
            (
                inner_grad,
                pl.BlockSpec((rows, width), lambda step, *_: (0, jnp.minimum(step, units - 1))),
            ),
            (
                active,
                pl.BlockSpec((rows, share), lambda step, *_: (0, jnp.maximum(step - units, 0))),
            ),
            (outer_low, full((rows, width))),
        ],
        outs,
        scratch,
        4 * units * rows * width * width,
        after,
    )


def thin_grad_kernel(counts, targets_ref, normed_ref, mixed_ref, low_ref, *refs):
    terms, refs = split_terms(refs, counts)
    step = pl.program_id(0)
    for number in range(3):

        @pl.when(step == number)
        def _():
            grad = joined(terms[number], counts[0])
            split_unit(targets_ref, outer_sum(normed_ref[...], grad), refs, step)

    @pl.when(step == 3)
    def _():
        split_unit(targets_ref, outer_sum(mixed_ref[...], low_ref[...]), refs, step)


def thin_weight_grad(cut, targets, normed_low, terms, mixed_out, branch_low, after):
    rows, width = normed_low.shape
    outs, scratch = grad_out(cut, 4, width)
    whole = full((rows, width))
    counts = (len(terms[0]), len(terms[1]) // len(terms[0]))
    return run(
        functools.partial(thin_grad_kernel, counts),
        "thin_weight_grad",
        4,
        [
            (targets, scalars()),
            (normed_low, whole),
            (mixed_out, whole),
            (branch_low, whole),
        ]
        + [(term, full(term.shape)) for some in terms for term in some],
        outs,
        scratch,
        8 * rows * width * width,
        after,
    )


def sum_along_kernel(keep_ref, taken_ref, out_ref):
    out_ref[...] = (keep_ref[0].astype(F32) + taken_ref[0].astype(F32)).astype(LOW)


def sum_along(keep, taken, step_far, after):
    _, deep, units, block, width = keep.shape
    spec = pl.BlockSpec(
        (1, 1, units, block, width), lambda step, *_: (step_far, step, 0, 0, 0)
    )
    return run(
        sum_along_kernel,
        "sum_along",
        deep,
        [(keep, spec), (taken, spec)],
        [
            (
                jax.ShapeDtypeStruct((deep, units, block, width), LOW),
                pl.BlockSpec((1, units, block, width), lambda step, *_: (step, 0, 0, 0)),
            )
        ],
        [],
        2 * units * deep * block * width,
        after,
    )[0]


def sum_near_kernel(keep_ref, taken_ref, *refs):
    along, out_ref = refs[:-1], refs[-1]
    total = keep_ref[0].astype(F32) + taken_ref[0].astype(F32)
    for ref in along:
        total += ref[...].astype(F32)
    out_ref[...] = total.astype(LOW)


def sum_near(keep, taken, along, after):
    _, deep, units, block, width = keep.shape
    near = pl.BlockSpec((1, 1, units, block, width), lambda step, *_: (0, step, 0, 0, 0))
    spec = pl.BlockSpec((1, units, block, width), lambda step, *_: (step, 0, 0, 0))
    return run(
        sum_near_kernel,
        "sum_near",
        deep,
        [(keep, near), (taken, near)] + [(array, spec) for array in along],
        [(jax.ShapeDtypeStruct((deep, units, block, width), LOW), spec)],
        [],
        3 * units * deep * block * width,
        after,
    )[0]


def pack_kernel(units, halves, rep_ref, in_ref, rows_ref, *refs):
    out_ref = refs[-1]
    block, width = in_ref.shape[1], out_ref.shape[1]
    count = units // halves

    def column(unit):
        return in_ref[0, :, unit * width : (unit + 1) * width].astype(LOW)

    for half in range(halves):

        @pl.when((rep_ref[0] == half) | (halves == 1))
        def _():
            for unit in range(count):
                out_ref[unit * block : (unit + 1) * block] = column(4 + half * count + unit)
            rows = rows_ref[0, half * count * block : (half + 1) * count * block]
            out_ref[count * block : 2 * count * block] = rows.astype(LOW)

    for number, unit in enumerate((3, 0, 1, 2)):
        at = (2 * count + number) * block
        out_ref[at : at + block] = column(unit)
    if len(refs) > 1:
        out_ref[(2 * count + 4) * block :] = refs[0][...]


def pack(dense_in, dense_out, layer, units, halves, rep, extra, after):
    _, block, columns = dense_in.shape
    width = dense_out.shape[2]
    rows = (2 * units // halves + 4) * block
    ins = [
        (rep, scalars()),
        (dense_in, pl.BlockSpec((1, block, columns), lambda step, *_: (layer, 0, 0))),
        (
            dense_out,
            pl.BlockSpec((1,) + dense_out.shape[1:], lambda step, *_: (layer, 0, 0)),
        ),
    ]
    if extra is not None:
        ins.append((extra, full(extra.shape)))
        rows += extra.shape[0]
    return run(
        functools.partial(pack_kernel, units, halves),
        "pack",
        1,
        ins,
        [(jax.ShapeDtypeStruct((rows, width), LOW), full((rows, width)))],
        [],
        rows * width,
        after,
    )[0]


def small_cut_kernel(layers, block, targets_ref, *refs):
    keep_ref, give_ref, held = refs[-3:]
    _, deep, rows, _ = keep_ref.shape
    each = rows // layers
    keep_ref[...] = jnp.zeros_like(keep_ref)
    give_ref[...] = jnp.zeros_like(give_ref)
    for layer in range(layers):
        one, two, outer_sums, inner_sums = (ref[...] for ref in refs[4 * layer : 4 * layer + 4])
        width = one.shape[1]
        at = layer * each
        held[at : at + 4] = one[:4]
        held[at + 4 : at + 5] = two[2:3]
        held[at + 5 : at + 7] = two[:2]
        held[at + 7 : at + 8] = outer_sums
        for unit in range(each - 8):
            held[at + 8 + unit : at + 9 + unit] = inner_sums[:, unit * width : (unit + 1) * width]
    far = keep_ref.shape[0]
    for depth in range(deep):
        for near in range(far):
            for place in range(2 * far):
                start = (depth * 2 * far + place) * block

                @pl.when(targets_ref[near] == place)
                def _():
                    keep_ref[near, depth, :, :block] = held[:, start : start + block]

                @pl.when(targets_ref[far + near] == place)
                def _():
                    give_ref[near, depth, :, :block] = held[:, start : start + block]


def small_cut(cut, targets, parts, layers, after):
    far, deep, block = cut
    width = parts[0].shape[1]
    rows = layers * (8 + parts[3].shape[1] // width)
    shape = (far, deep, rows, LANES)
    return run(
        functools.partial(small_cut_kernel, layers, block),
        "small_cut",
        1,
        [(targets, scalars())] + [(part, full(part.shape)) for part in parts],
        [(jax.ShapeDtypeStruct(shape, F32), full(shape))] * 2,
        [pltpu.VMEM((rows, width), F32)],
        rows * width,
        after,
    )


def adam_kernel(usual, special, chosen, weight_ref, first_ref, second_ref, *refs):
    grads, (grad_ref, moment_ref, square_ref, updated_ref) = refs[:-4], refs[-4:]
    grad = sum([ref[0].astype(F32) for ref in grads[1:]], grads[0][0].astype(F32))
    grad = grad.reshape(weight_ref.shape)
    rate = jnp.where(pl.program_id(0) == chosen, special, usual)
    moment, square, updated = adam_step(weight_ref[...], grad, first_ref[...], second_ref[...], rate)
    grad_ref[...] = grad
    moment_ref[...] = moment
    square_ref[...] = square
    updated_ref[...] = updated


def adam(state, grads, layer, first, count, from_unit, rates, after, reuse):
    weight = state[0]
    block, width = grads[0].shape[1:]
    if weight.ndim == 3:
        spec = pl.BlockSpec((1, block, width), lambda step, *_: (layer, 0, first + step))
    else:
        spec = pl.BlockSpec((1, 1, block, width), lambda step, *_: (layer, first + step, 0, 0))
    usual, special, chosen = rates
    return run(
        functools.partial(adam_kernel, usual, special, chosen - first),
        "adam",
        count,
        [(array, spec) for array in state]
        + [
            (grad, pl.BlockSpec((1, block, width), lambda step, *_: (from_unit + step, 0, 0)))
            for grad in grads
        ],
        [(jax.ShapeDtypeStruct(weight.shape, F32), spec)] * 4,
        [],
        16 * count * block * width,
        after,
        None,
        reuse,
    )


def part_kernel(lower_ref, rows_ref, keep_ref, give_ref):
    count = keep_ref.shape[0]
    lower, upper = rows_ref[:count], rows_ref[count:]
    in_lower = lower_ref[0] != 0
    keep_ref[...] = jnp.where(in_lower, lower, upper)
    give_ref[...] = jnp.where(in_lower, upper, lower).astype(LOW)


def part_clips(in_lower, rows, after):
    count, width = rows.shape[0] // 2, rows.shape[1]
    return run(
        part_kernel,
        "part_clips",
        1,
        [(in_lower, scalars()), (rows, full(rows.shape))],
        [
            (jax.ShapeDtypeStruct((count, width), F32), full((count, width))),
            (jax.ShapeDtypeStruct((count, width), LOW), full((count, width))),
        ],
        [],
        rows.size,
        after,
    )


def query_block(rows):
    return next(size for size in (768, 384, 256, 128) if rows % size == 0)


def attend_kernel(parts, block, bias_ref, q_ref, *refs):
    k_refs, v_refs = refs[:parts], refs[parts : 2 * parts]
    o_ref, lse_ref = refs[2 * parts :]
    rows = q_ref.shape[0]
    q_side = (q_ref[...] * jnp.bfloat16(LOGIT_SCALE)).T
    ones = jnp.ones((16, rows), LOW)
    v_heads = []
    for ref in v_refs:
        side = ref[...].T
        v_heads.append(
            [jnp.concatenate([side[h * HDIM : (h + 1) * HDIM], ones]) for h in range(2)]
        )
    head_of = lax.broadcasted_iota(jnp.int32, (LANES, block), 0) // HDIM
    for start in range(0, rows, block):
        q_block = q_side[:, start : start + block]
        both = []
        for head in range(2):
            q_head = jnp.where(head_of == head, q_block, jnp.zeros_like(q_block))
            scores = []
            for part in range(parts):
                score = product(k_refs[part][...], q_head)
                lower, upper = score[: rows // 2], score[rows // 2 :]
                bias = jnp.tile(bias_ref[part], (1, block // LANES))
                scores.append(jnp.concatenate([lower, upper + bias], axis=0))
            top = functools.reduce(
                jnp.maximum, [jnp.max(score, axis=0, keepdims=True) for score in scores]
            )
            weights = [jnp.exp(score - top).astype(LOW) for score in scores]
            summed = sum(product(v_heads[part][head], weights[part]) for part in range(parts))
            total = summed[HDIM : HDIM + 1]
            both.append(summed[:HDIM] / total)
            lse_ref[0, head : head + 1, start : start + block] = top + jnp.log(total)
        o_ref[start : start + block, :] = jnp.concatenate(both, axis=0).T.astype(LOW)


def attend(queries, own, others, bias, after):
    rows, width = queries.shape
    pairs = width // LANES
    parts = len(others) + 1

    def columns(base):
        return pl.BlockSpec((rows, LANES), lambda pair, *_: (0, base * pairs + pair))

    return run(
        functools.partial(attend_kernel, parts, query_block(rows)),
        "attend",
        pairs,
        [(bias, full(bias.shape)), (queries, columns(0))]
        + [(array, columns(0)) for array in (own, *others)]
        + [(array, columns(1)) for array in (own, *others)],
        [
            (jax.ShapeDtypeStruct((rows, width), LOW), columns(0)),
            (
                jax.ShapeDtypeStruct((pairs, 2, rows), F32),
                pl.BlockSpec((1, 2, rows), lambda pair, *_: (pair, 0, 0)),
            ),
        ],
        [],
        16 * rows * rows * parts * width,
        after,
    )


def attend_back_kernel(parts, block, bias_ref, q_ref, *refs):
    k_refs, v_refs = refs[:parts], refs[parts : 2 * parts]
    o_ref, do_ref, lse_ref = refs[2 * parts : 2 * parts + 3]
    dq_ref = refs[2 * parts + 3]
    dk_refs = refs[2 * parts + 4 : 3 * parts + 4]
    dv_refs = refs[3 * parts + 4 :]
    rows = q_ref.shape[0]
    q_rows = q_ref[...] * jnp.bfloat16(LOGIT_SCALE)
    do_rows = do_ref[...]
    q_side, do_side = q_rows.T, do_rows.T
    shared = (do_rows.astype(F32) * o_ref[...].astype(F32)).T
    delta = [
        jnp.sum(shared[head * HDIM : (head + 1) * HDIM], axis=0, keepdims=True)
        for head in range(2)
    ]
    head_of = lax.broadcasted_iota(jnp.int32, (LANES, rows), 0) // HDIM
    zeros = jnp.zeros_like(q_side)
    q_heads = [jnp.where(head_of == head, q_side, zeros) for head in range(2)]
    do_heads = [jnp.where(head_of == head, do_side, zeros) for head in range(2)]
    lane = lax.broadcasted_iota(jnp.int32, (block, LANES), 1)
    dq_sides = [jnp.zeros((HDIM, rows), F32)] * 2
    for part in range(parts):
        for start in range(0, rows, block):
            here = slice(start, start + block)
            k_block, v_block = k_refs[part][here], v_refs[part][here]
            k_side = k_block.T
            dk_heads, dv_heads = [], []
            for head in range(2):
                score = product(k_block, q_heads[head])
                if start + block > rows // 2:
                    skip = max(rows // 2 - start, 0)
                    upper = bias_ref[part][start + skip - rows // 2 : start + block - rows // 2]
                    raised = score[skip:] + jnp.tile(upper, (1, rows // LANES))
                    score = jnp.concatenate([score[:skip], raised], axis=0) if skip else raised
                chances = jnp.exp(score - lse_ref[0, head : head + 1])
                chance_grad = product(v_block, do_heads[head])
                score_grad = (chances * (chance_grad - delta[head])).astype(LOW)
                dq_sides[head] = dq_sides[head] + product(
                    k_side[head * HDIM : (head + 1) * HDIM], score_grad
                )
                dk_heads.append(product(score_grad, q_rows))
                dv_heads.append(product(chances.astype(LOW), do_rows))
            dk_refs[part][here] = jnp.where(lane < HDIM, *dk_heads).astype(LOW)
            dv_refs[part][here] = jnp.where(lane < HDIM, *dv_heads).astype(LOW)
    dq_ref[...] = (jnp.concatenate(dq_sides, axis=0) * LOGIT_SCALE).T.astype(LOW)


def attend_back(queries, own, others, mixed_out, mixed_grad, log_total, bias, group, groups, after):
    rows, width = queries.shape
    pairs = width // LANES
    parts = len(others) + 1
    first = group * pairs // groups
    count = (group + 1) * pairs // groups - first

    def columns(base):
        return pl.BlockSpec((rows, LANES), lambda pair, *_: (0, base * pairs + first + pair))

    out = run(
        functools.partial(attend_back_kernel, parts, query_block(rows)),
        "attend_back",
        count,
        [(bias, full(bias.shape)), (queries, columns(0))]
        + [(array, columns(0)) for array in (own, *others)]
        + [(array, columns(1)) for array in (own, *others)]
        + [
            (mixed_out, columns(0)),
            (mixed_grad, columns(0)),
            (log_total, pl.BlockSpec((1, 2, rows), lambda pair, *_: (first + pair, 0, 0))),
        ],
        [
            (
                jax.ShapeDtypeStruct((rows, count * LANES), LOW),
                pl.BlockSpec((rows, LANES), lambda pair, *_: (0, pair)),
            )
        ]
        * (2 * parts + 1),
        [],
        40 * rows * rows * parts * count * LANES,
        after,
    )
    return out[0], out[1 : parts + 1], out[parts + 1 :]


def on_device(
    frames,
    lengths,
    cotangent,
    dense_in,
    dense_out,
    small_params,
    first_in,
    first_out,
    first_small,
    second_in,
    second_out,
    second_small,
):
    clip_count, local_frames, width = frames.shape
    layer_count, block, columns_in = dense_in.shape
    units = columns_in // width - 4
    seq, deep, reps = lax.axis_size("seq"), lax.axis_size("fsdp"), lax.axis_size("rep")
    half = seq // clip_count
    total_frames = local_frames * seq
    place, depth = lax.axis_index("seq"), lax.axis_index("fsdp")
    owners = seq * deep
    my_clip, my_member = place // half, place % half
    in_lower = my_clip == 0
    swap = [(source, (source + half) % seq) for source in range(seq)]
    far = seq // 2
    row, core = place // 2, place % 2
    cut = (far, deep, block) if block % 16 == 0 else None

    def turn(axis, step):
        size = lax.axis_size(axis)
        return [(source, (source + step) % size) for source in range(size)]

    over_core = [(source, source ^ 1) for source in range(seq)]

    def to_clips(arrays):
        whole = jnp.stack(arrays, axis=1)
        kept = lax.dynamic_index_in_dim(whole, my_clip, 0, keepdims=False)
        given = lax.dynamic_index_in_dim(whole, 1 - my_clip, 0, keepdims=False)
        taken = lax.ppermute(given, "seq", swap)
        lower, upper = jnp.where(in_lower, kept, taken), jnp.where(in_lower, taken, kept)
        return [
            jnp.concatenate([lower[number], upper[number]], axis=0).astype(F32)
            for number in range(len(arrays))
        ]

    def split_clips(rows):
        lower, upper = rows[:local_frames], rows[local_frames:]
        return jnp.where(in_lower, lower, upper), jnp.where(in_lower, upper, lower).astype(LOW)

    def from_clips(kept, given):
        taken = lax.ppermute(given, "seq", swap).astype(kept.dtype)
        return jnp.stack([jnp.where(in_lower, kept, taken), jnp.where(in_lower, taken, kept)])

    def around(step):
        return [
            (source, source - source % half + (source % half + step) % half)
            for source in range(seq)
        ]

    halves = 2 if reps == 2 and units % 2 == 0 and deep % 2 == 0 and cut is not None else 1
    info = jnp.stack([lax.axis_index("rep"), core])

    def gather(layer, extra, after):
        if cut is None:
            columns = dense_in[layer].astype(LOW).reshape(block, 4 + units, width)
            columns = columns.transpose(1, 0, 2)
            columns = lax.all_gather(columns, ("fsdp", "seq"), axis=1, tiled=True)
            rows = lax.all_gather(
                dense_out[layer].astype(LOW), ("fsdp", "seq"), axis=0, tiled=True
            )
            parts = [columns[4:].reshape(-1, width), rows, columns[3], *columns[:3]]
            return Wide(jnp.concatenate(parts)[None], None, info, width, units)
        own = pack(dense_in, dense_out, layer, units, halves, info, extra, after)
        chunk = lax.all_gather(own, ("fsdp", "seq"), axis=0)
        if halves == 1:
            return Wide(chunk, None, info, block, units)
        return Wide(chunk, [None, None], info, block, units)

    def share(wide, marker):
        wide.given = []
        if wide.sent:
            wide.chunk, marker = lax.optimization_barrier((wide.chunk, marker))
            rows = units // 2 * block
            shape = (owners // 2, rows, width)
            wide.given = [
                lax.dynamic_slice(wide.chunk, (core * (owners // 2), number * rows, 0), shape)
                for number in range(2)
            ]
            wide.near = [lax.ppermute(part, "rep", turn("rep", 1)) for part in wide.given]
        return marker

    def exchange(wide, number, marker):
        if wide.sent:
            near, marker = lax.optimization_barrier((wide.near[number], marker))
            wide.sent[number] = (near, lax.ppermute(near, "seq", over_core))
        return marker

    targets = jnp.stack(
        [
            (row + step) % far * 2 + (core + other) % 2
            for other in range(2)
            for step in range(far)
        ]
    )

    def start_core(parts):
        if cut is None:
            return parts, []
        return (parts[0], lax.ppermute(parts[1], "seq", over_core)), [parts[0]]

    def start_far(chunk, after):
        if cut is None:
            return chunk
        keep, taken = chunk[0]
        sums = [sum_along(keep, taken, step, after) for step in range(1, far)]
        moved = [
            lax.ppermute(part, "seq", turn("seq", 2 * step + 2)) for step, part in enumerate(sums)
        ]
        return (keep, taken, moved), sums

    def whole_deep(chunk, after):
        if cut is None:
            return chunk
        total = sum_near(*chunk[0], after)
        return lax.psum_scatter(total, "fsdp", scatter_dimension=0, tiled=True)[0], [total]

    def start_reps(chunk):
        if cut is None:
            result = chunk[0][0]
            owned = lax.psum_scatter(
                result[:units], ("fsdp", "seq"), scatter_dimension=1, tiled=True
            )
            if result.shape[0] > units:
                rows = lax.psum_scatter(
                    result[units:].reshape(units * width, width),
                    ("fsdp", "seq"),
                    scatter_dimension=0,
                    tiled=True,
                )
                owned = jnp.concatenate([owned, rows.reshape(units, block, width)])
        else:
            owned = chunk[0]
        return owned, [lax.ppermute(owned, "rep", turn("rep", step)) for step in range(1, reps)]

    def finish(state):
        owned, arrived = state
        return sum([part.astype(F32) for part in arrived], owned.astype(F32))

    length = lax.dynamic_index_in_dim(lengths, my_clip, 0, keepdims=False)
    bias = jnp.stack(
        [
            jnp.broadcast_to(
                jnp.where(
                    (half + (my_member - step) % half) * local_frames
                    + jnp.arange(local_frames, dtype=jnp.int32)
                    < length,
                    0.0,
                    MASKED,
                )[:, None],
                (local_frames, LANES),
            )
            for step in range(half)
        ]
    ).astype(F32)

    small_low = small_params.astype(LOW)
    extra = None
    if cut is not None:
        extra = jnp.pad(small_low.reshape(-1), (0, -small_low.size % (16 * width)))
        extra = extra.reshape(-1, width)
    wides = []
    for layer in range(layer_count):
        wides.append(gather(layer, extra if layer == 0 else None, []))
    if cut is None:
        params_all = lax.all_gather(small_low, ("fsdp", "seq"), axis=2, tiled=True)
    else:
        first_row = (wides[0].thin_at + 3) * block
        params_all = wides[0].chunk[:, first_row:].reshape(owners, -1)[:, : small_low.size]
        params_all = params_all.reshape((owners,) + small_low.shape).transpose(1, 2, 0, 3)
        params_all = params_all.reshape(layer_count, -1, width)
    params_all = params_all.astype(F32)

    row_steps = units if cut is None else deep
    hidden, upstream = to_clips([frames, cotangent])
    stored = []
    for layer_index in range(layer_count):
        params = params_all[layer_index]
        wide = wides[layer_index]
        hidden = share(wide, hidden)
        normed_low, queries, own = project(
            hidden, params, wide.chunk, wide.block, wide.thin_at, wide.given
        )
        others = [lax.ppermute(own, "seq", around(step)) for step in range(1, half)]
        mixed_out, log_total = attend(queries, own, others, bias, [])
        mixed_out = exchange(wide, 0, mixed_out)
        middle, second_low, active, slope = inner(hidden, mixed_out, params, wide, [])
        middle = exchange(wide, 1, middle)
        stored.append(
            (hidden, normed_low, queries, own, others, log_total, mixed_out)
            + (middle, second_low, active, slope)
        )
        hidden = outer(middle, active, params, wide, row_steps, [])
    encoded = from_clips(*split_clips(hidden.astype(LOW)))
    groups = 2 if width // LANES % 2 == 0 else 1
    order = [hidden]
    waiting = None
    parts_out = {}
    small_grads = []
    for layer_index in reversed(range(layer_count)):
        wide = wides[layer_index]
        params = params_all[layer_index]
        (
            hidden,
            normed_low,
            queries,
            own,
            others,
            log_total,
            mixed_out,
            middle,
            second_low,
            active,
            slope,
        ) = stored[layer_index]
        outer_low, inner_grad, bias_inner, bias_outer = outer_back(
            upstream, slope, wide, row_steps, order
        )
        order = [inner_grad]
        if waiting:
            waiting = start_far(waiting, order)
            order = order + waiting[1]
        wide_part = start_core(
            wide_weight_grad(
                cut, targets, second_low, inner_grad, active, outer_low, units, order
            )
        )
        middle_grad, branch_low, mixed_grad, sums_two = inner_back(
            inner_grad, upstream, middle, params, wide, wide_part[1]
        )
        order = [middle_grad]
        wide_part = start_far(wide_part, order)
        order = order + wide_part[1]
        q_terms, k_near, v_near, k_far, v_far = [], [], [], [], []
        for group in range(groups):
            q_term, k_terms, v_terms = attend_back(
                queries,
                own,
                others,
                mixed_out,
                mixed_grad,
                log_total,
                bias,
                group,
                groups,
                order,
            )
            q_terms.append(q_term)
            k_near.append(k_terms[0])
            v_near.append(v_terms[0])
            k_far.append(k_terms[1:])
            v_far.append(v_terms[1:])
            order = [q_term]
            if waiting and group == 0:
                waiting = whole_deep(waiting, order)
                order = order + waiting[1]

        def all_terms(near, terms):
            moved = [
                lax.ppermute(terms[group][step - 1], "seq", around(half - step))
                for step in range(1, half)
                for group in range(groups)
            ]
            return list(near) + moved

        terms = [q_terms, all_terms(k_near, k_far), all_terms(v_near, v_far)]
        order = [q_terms[-1]]

        if layer_index == 0:
            thin_part = thin_weight_grad(
                cut, targets, normed_low, terms, mixed_out, branch_low, order
            )
            order = [thin_part[0]]
            wide_part = whole_deep(wide_part, order)
            order = order + wide_part[1]
        upstream, sums_one = project_back(
            hidden, middle_grad, params, terms, wide.chunk, wide.block, wide.thin_at, order
        )
        if waiting:
            waiting = start_reps(waiting)
            parts_out[layer_index + 1] += (waiting,)
        if layer_index > 0:
            wide_part = whole_deep(wide_part, [upstream])
            thin_part = thin_weight_grad(
                cut, targets, normed_low, terms, mixed_out, branch_low, [upstream] + wide_part[1]
            )
        waiting = start_core(thin_part)
        order = waiting[1]
        parts_out[layer_index] = (start_reps(wide_part),)
        small_grads = [sums_one, sums_two, bias_outer, bias_inner] + small_grads
    rows_shape = (layer_count, units, block, width)
    states_in = (dense_in, first_in, second_in)
    states_out = [array.reshape(rows_shape) for array in (dense_out, first_out, second_out)]
    rates_in = (RATE_DENSE, RATE_DENSE * math.sqrt(total_frames / 3.0), 3)
    rates_out = (RATE_OUTER, RATE_OUTER, 0)

    def flat(part):
        return [part[0]] + part[1]

    arrived = [part for layer in range(1, layer_count) for _, some in parts_out[layer] for part in some]
    waiting = start_far(waiting, [upstream] + arrived)
    order = waiting[1]
    done_in, done_out = (), ()
    for layer in reversed(range(1, layer_count)):
        wide_part, thin_part = parts_out[layer]
        done_in = adam(states_in, flat(thin_part), layer, 0, 4, 0, rates_in, order, done_in)
        done_in = adam(states_in, flat(wide_part), layer, 4, units, 0, rates_in, order, done_in)
        done_out = adam(
            states_out, flat(wide_part), layer, 0, units, units, rates_out, order, done_out
        )
    wide_part = parts_out[0][0]
    waiting = whole_deep(waiting, list(done_in[:1]) + list(done_out[:1]))
    order = waiting[1]
    if cut is None:
        small_all = jnp.stack(
            [
                jnp.concatenate([one[:4], two[2:3], two[:2], outer_sums])
                for one, two, outer_sums, _ in zip(*[iter(small_grads)] * 4)
            ]
        )
        inner_all = jnp.stack([part.reshape(units, width) for part in small_grads[3::4]])
        small_all = jnp.concatenate([small_all, inner_all], axis=1)
        small_all = small_all.reshape(layer_count, -1, owners, block).transpose(2, 0, 1, 3)
        owned_small = lax.psum_scatter(
            small_all, ("fsdp", "seq"), scatter_dimension=0, tiled=True
        )
    else:
        keep, give = small_cut(cut, targets, small_grads, layer_count, order + wide_part[1])
        cuts = keep + lax.ppermute(give, "seq", over_core)
        total = cuts[0]
        for step in range(1, far):
            total += lax.ppermute(cuts[step], "seq", turn("seq", 2 * step))
        owned_small = lax.dynamic_index_in_dim(total, depth, 0, keepdims=False)
        for step in range(1, deep):
            owned_small += lax.ppermute(
                lax.dynamic_index_in_dim(total, (depth + step) % deep, 0, keepdims=False),
                "fsdp",
                turn("fsdp", step),
            )
        owned_small = owned_small[:, :block]
    owned_small = owned_small.reshape(small_params.shape).astype(LOW)
    frames_grad = from_clips(
        *part_clips(in_lower.astype(jnp.int32).reshape(1), upstream, order)
    )
    done_in = adam(states_in, flat(wide_part), 0, 4, units, 0, rates_in, order, done_in)
    done_out = adam(states_out, flat(wide_part), 0, 0, units, units, rates_out, order, done_out)
    thin_part = start_reps(waiting)
    done_in = adam(states_in, flat(thin_part), 0, 0, 4, 0, rates_in, [], done_in)
    grad_in, moment_in, square_in, updated_in = done_in
    grad_out_rows, moment_out, square_out, updated_out = (
        array.reshape(dense_out.shape) for array in done_out
    )
    grad_small = finish(
        (owned_small, [lax.ppermute(owned_small, "rep", turn("rep", s)) for s in range(1, reps)])
    )
    moment_small, square_small, updated_small = adam_step(
        small_params, grad_small, first_small, second_small, RATE_SMALL
    )
    return (
        encoded,
        frames_grad,
        grad_in,
        grad_out_rows,
        grad_small,
        moment_in,
        moment_out,
        moment_small,
        square_in,
        square_out,
        square_small,
        updated_in,
        updated_out,
        updated_small,
    )


def solution(mesh):
    clips = P(("rep", "fsdp"), "seq", None)
    rows = P(None, ("fsdp", "seq"), None)
    lanes = P(None, None, ("fsdp", "seq"))
    return jax.shard_map(
        on_device,
        mesh=mesh,
        in_specs=(clips, P(("rep", "fsdp")), clips) + (rows, rows, lanes) * 3,
        out_specs=(clips, clips) + (rows, rows, lanes) * 4,
        check_vma=False,
    )
```

```python
import functools
import math

import jax
import jax.numpy as jnp
from jax import lax
from jax.experimental import pallas as pl
from jax.experimental.pallas import tpu as pltpu
from jax.sharding import PartitionSpec as P

HDIM = 64
STEP = 10

NORM_EPSILON = 1e-05
BETA_ONE = 0.9
BETA_TWO = 0.999
ADAM_EPSILON = 1e-08
DECAY_RATE = 0.01
RATE_DENSE = 0.1
RATE_OUTER = 0.05
RATE_SMALL = 0.5
INV_ROOT_TWO = 0.7071067811865476
INV_ROOT_TAU = 0.3989422804014327
LOGIT_SCALE = 0.125
MASKED = -1e30
LANES = 128
VMEM_LIMIT = 60 * 2**20

F32 = jnp.float32
LOW = jnp.bfloat16


def adam_step(weight, gradient, first, second, rate):
    moment = BETA_ONE * first + (1.0 - BETA_ONE) * gradient
    square = BETA_TWO * second + (1.0 - BETA_TWO) * gradient * gradient
    moment_hat = moment / (1.0 - BETA_ONE**STEP)
    square_hat = square / (1.0 - BETA_TWO**STEP)
    updated = weight - rate * (
        moment_hat / (jnp.sqrt(square_hat) + ADAM_EPSILON) + DECAY_RATE * weight
    )
    return (moment, square, updated)


def product(left_side, right_side):
    return jnp.dot(left_side, right_side, preferred_element_type=F32)


def back_product(left_side, right_side):
    return lax.dot_general(
        left_side, right_side, (((1,), (1,)), ((), ())), preferred_element_type=F32
    )


def outer_sum(left_side, right_side):
    return lax.dot_general(
        left_side, right_side, (((0,), (0,)), ((), ())), preferred_element_type=F32
    )


def normalise(values_in):
    centred = values_in - jnp.mean(values_in, axis=-1, keepdims=True)
    scale_inv = lax.rsqrt(jnp.mean(centred * centred, axis=-1, keepdims=True) + NORM_EPSILON)
    return centred * scale_inv, scale_inv


def norm_backward(upstream, gain_row, normal, scale_inv):
    scaled = upstream * gain_row
    inside = (
        scaled
        - jnp.mean(scaled, axis=-1, keepdims=True)
        - normal * jnp.mean(scaled * normal, axis=-1, keepdims=True)
    )
    return (
        scale_inv * inside,
        jnp.sum(upstream * normal, axis=0, keepdims=True),
        jnp.sum(upstream, axis=0, keepdims=True),
    )


def run(kernel, name, steps, ins, outs, scratch, flops, after=(), scalar=None, reuse=()):
    in_arrays, in_specs = zip(*ins)
    out_shapes, out_specs = zip(*outs)
    moved = sum(a.size * a.dtype.itemsize for a in in_arrays)
    moved += sum(math.prod(s.shape) * s.dtype.itemsize for s in out_shapes)
    lead = 0 if scalar is None else 1

    spare = [*after, *reuse]
    aliases = {lead + len(ins) + len(after) + number: number for number in range(len(reuse))}

    def body(*refs):
        kernel(*refs[: lead + len(ins)], *refs[lead + len(ins) + len(spare) :])

    grid_spec = pltpu.PrefetchScalarGridSpec(
        num_scalar_prefetch=lead,
        grid=(steps,),
        in_specs=list(in_specs) + [pl.BlockSpec(memory_space=pl.ANY)] * len(spare),
        out_specs=list(out_specs),
        scratch_shapes=scratch,
    )
    return pl.pallas_call(
        body,
        grid_spec=grid_spec,
        out_shape=list(out_shapes),
        input_output_aliases=aliases,
        compiler_params=pltpu.CompilerParams(vmem_limit_bytes=VMEM_LIMIT),
        cost_estimate=pl.CostEstimate(flops=flops, bytes_accessed=moved, transcendentals=0),
        name=name,
    )(*(() if scalar is None else (scalar,)), *in_arrays, *spare)


def full(shape):
    return pl.BlockSpec(shape, lambda step, *_: (0,) * len(shape))


def scalars():
    return pl.BlockSpec(memory_space=pltpu.SMEM)


def unit_spec(chunk, block, unit_of):
    owners, _, width = chunk.shape
    return chunk, pl.BlockSpec((owners, block, width), lambda step, *_: (0, unit_of(step), 0))


def unit_of_ref(ref):
    return ref[...].reshape(-1, ref.shape[-1])


class Wide:
    def __init__(self, chunk, sent, info, block, units):
        self.chunk, self.sent, self.info = chunk, sent, info
        self.block, self.units = block, units
        self.held = units // 2 if sent else units
        self.mix_at = 2 * self.held
        self.thin_at = self.mix_at + 1

    def mix_spec(self):
        return unit_spec(self.chunk, self.block, lambda step: self.mix_at)

    def inner_specs(self, unit_of):
        arrays = (self.chunk, *self.sent[0]) if self.sent else (self.chunk,)
        return [
            unit_spec(array, self.block, lambda step: lax.rem(unit_of(step), self.held))
            for array in arrays
        ]

    def inner_scratch(self):
        owners, _, width = self.chunk.shape
        return [pltpu.VMEM((owners, self.block, width), LOW)] if self.sent else []

    def outer_specs(self, steps):
        owners, _, width = self.chunk.shape
        if owners == 1:
            return [unit_spec(self.chunk, self.block, lambda step: self.units + step)]
        shape = (owners // steps, self.held * self.block, width)
        specs = [(self.chunk, pl.BlockSpec(shape, lambda step, *_: (step, 1, 0)))]
        if self.sent:
            near = pl.BlockSpec(shape, lambda step, *_: (lax.rem(step, steps // 2), 0, 0))
            specs += [(array, near) for array in self.sent[1]]
        return specs

    def outer_scratch(self, steps):
        owners, _, width = self.chunk.shape
        shape = (owners // steps, self.units * self.block, width)
        return [pltpu.VMEM(shape, LOW)] if self.sent else []

    def count(self):
        return 3 if self.sent else 1


def inner_unit(info_ref, refs, held, half):
    if len(refs) == 1:
        return unit_of_ref(refs[0])
    mine_ref, near_ref, far_ref = refs
    count = near_ref.shape[0]

    @pl.when(info_ref[0] == half)
    def _():
        held[...] = mine_ref[...]

    for core in range(2):

        @pl.when((info_ref[0] != half) & (info_ref[1] == core))
        def _():
            held[core * count : (core + 1) * count] = near_ref[...]
            held[(1 - core) * count : (2 - core) * count] = far_ref[...]

    return unit_of_ref(held)


def outer_unit(info_ref, refs, held, step, steps):
    if len(refs) == 1:
        return unit_of_ref(refs[0])
    mine_ref, near_ref, far_ref = refs
    count = mine_ref.shape[1]
    is_near = step // (steps // 2) == info_ref[1]
    for rep in range(2):

        @pl.when(info_ref[0] == rep)
        def _():
            held[:, rep * count : (rep + 1) * count] = mine_ref[...]

        for ref, wanted in ((near_ref, is_near), (far_ref, jnp.logical_not(is_near))):

            @pl.when((info_ref[0] == rep) & wanted)
            def _():
                held[:, (1 - rep) * count : (2 - rep) * count] = ref[...]

    return unit_of_ref(held)


def project_kernel(hidden_ref, params_ref, unit_ref, normed_ref, q_ref, kv_ref):
    step = pl.program_id(0)

    @pl.when(step == 0)
    def _():
        normal, _ = normalise(hidden_ref[...])
        normed_ref[...] = (normal * params_ref[0:1] + params_ref[1:2]).astype(LOW)

    weights = unit_of_ref(unit_ref)
    added = jnp.where(step == 0, params_ref[2:3], params_ref[3:4])
    added = jnp.where(step == 1, jnp.zeros_like(added), added)
    result = (product(normed_ref[...], weights) + added).astype(LOW)

    @pl.when(step == 0)
    def _():
        q_ref[...] = result

    @pl.when(step > 0)
    def _():
        kv_ref[...] = result


def project(hidden, params, chunk, block, first, after):
    rows, width = hidden.shape
    return run(
        project_kernel,
        "project",
        3,
        [
            (hidden, full(hidden.shape)),
            (params, full(params.shape)),
            unit_spec(chunk, block, lambda step: first + step),
        ],
        [
            (jax.ShapeDtypeStruct((rows, width), LOW), full((rows, width))),
            (jax.ShapeDtypeStruct((rows, width), LOW), full((rows, width))),
            (
                jax.ShapeDtypeStruct((rows, 2 * width), LOW),
                pl.BlockSpec((rows, width), lambda step, *_: (0, jnp.maximum(step - 1, 0))),
            ),
        ],
        [],
        6 * rows * width * width,
        after,
    )


def inner_kernel(count, per_half, info_ref, hidden_ref, mixed_ref, params_ref, mix_ref, *refs):
    unit_refs, refs = refs[:count], refs[count:]
    middle_ref, second_ref, active_ref, slope_ref, *held = refs
    step = pl.program_id(0)

    @pl.when(step == 0)
    def _():
        middle = hidden_ref[...] + (product(mixed_ref[...], unit_of_ref(mix_ref)) + params_ref[4:5])
        middle_ref[...] = middle
        normal, _ = normalise(middle)
        second_ref[...] = (normal * params_ref[5:6] + params_ref[6:7]).astype(LOW)

    @pl.when(step > 0)
    def _():
        weights = inner_unit(info_ref, unit_refs, held[0] if held else None, (step - 1) // per_half)
        inner = product(second_ref[...], weights) + params_ref[pl.ds(step + 7, 1), :]
        cumulative = 0.5 * (1.0 + lax.erf(inner * INV_ROOT_TWO))
        active_ref[...] = (inner * cumulative).astype(LOW)
        slope = cumulative + inner * jnp.exp(-0.5 * inner * inner) * INV_ROOT_TAU
        slope_ref[...] = slope.astype(LOW)


def inner(hidden, mixed_out, params, wide, after):
    units = wide.units
    rows, width = hidden.shape
    spread = pl.BlockSpec((rows, width), lambda step, *_: (0, jnp.maximum(step - 1, 0)))
    return run(
        functools.partial(inner_kernel, wide.count(), max(units // 2, 1)),
        "inner",
        units + 1,
        [
            (wide.info, scalars()),
            (hidden, full(hidden.shape)),
            (mixed_out, full(mixed_out.shape)),
            (params, full(params.shape)),
            wide.mix_spec(),
        ]
        + wide.inner_specs(lambda step: jnp.maximum(step - 1, 0)),
        [
            (jax.ShapeDtypeStruct((rows, width), F32), full((rows, width))),
            (jax.ShapeDtypeStruct((rows, width), LOW), full((rows, width))),
            (jax.ShapeDtypeStruct((rows, units * width), LOW), spread),
            (jax.ShapeDtypeStruct((rows, units * width), LOW), spread),
        ],
        wide.inner_scratch(),
        2 * (units + 1) * rows * width * width,
        after,
    )


def outer_kernel(count, steps, info_ref, middle_ref, active_ref, params_ref, *refs):
    unit_refs, (out_ref, *held) = refs[:count], refs[count:]
    weights = outer_unit(
        info_ref, unit_refs, held[0] if held else None, pl.program_id(0), steps
    )
    term = product(active_ref[...], weights)

    @pl.when(pl.program_id(0) == 0)
    def _():
        out_ref[...] = middle_ref[...] + (term + params_ref[7:8])

    @pl.when(pl.program_id(0) > 0)
    def _():
        out_ref[...] += term


def outer(middle, active, params, wide, steps, after):
    units = wide.units
    rows, width = middle.shape
    return run(
        functools.partial(outer_kernel, wide.count(), steps),
        "outer",
        steps,
        [
            (wide.info, scalars()),
            (middle, full(middle.shape)),
            (active, pl.BlockSpec((rows, units * width // steps), lambda step, *_: (0, step))),
            (params, full(params.shape)),
        ]
        + wide.outer_specs(steps),
        [(jax.ShapeDtypeStruct((rows, width), F32), full((rows, width)))],
        wide.outer_scratch(steps),
        2 * units * rows * width * width,
        after,
    )[0]


def outer_back_kernel(count, steps, info_ref, upstream_ref, slope_ref, *refs):
    unit_refs, refs = refs[:count], refs[count:]
    low_ref, inner_ref, bias_inner_ref, bias_outer_ref, *held = refs
    weights = outer_unit(
        info_ref, unit_refs, held[0] if held else None, pl.program_id(0), steps
    )

    @pl.when(pl.program_id(0) == 0)
    def _():
        low = upstream_ref[...].astype(LOW)
        low_ref[...] = low
        bias_outer_ref[...] = jnp.sum(low.astype(F32), axis=0, keepdims=True)

    grad = (back_product(low_ref[...], weights) * slope_ref[...].astype(F32)).astype(LOW)
    inner_ref[...] = grad
    bias_inner_ref[...] = jnp.sum(grad.astype(F32), axis=0, keepdims=True)


def outer_back(upstream, slope, wide, steps, after):
    units = wide.units
    rows, width = upstream.shape
    share = units * width // steps
    return run(
        functools.partial(outer_back_kernel, wide.count(), steps),
        "outer_back",
        steps,
        [
            (wide.info, scalars()),
            (upstream, full(upstream.shape)),
            (slope, pl.BlockSpec((rows, share), lambda step, *_: (0, step))),
        ]
        + wide.outer_specs(steps),
        [
            (jax.ShapeDtypeStruct((rows, width), LOW), full((rows, width))),
            (
                jax.ShapeDtypeStruct((rows, units * width), LOW),
                pl.BlockSpec((rows, share), lambda step, *_: (0, step)),
            ),
            (
                jax.ShapeDtypeStruct((1, units * width), F32),
                pl.BlockSpec((1, share), lambda step, *_: (0, step)),
            ),
            (jax.ShapeDtypeStruct((1, width), F32), full((1, width))),
        ],
        wide.outer_scratch(steps),
        2 * units * rows * width * width,
        after,
    )


def inner_back_kernel(
    count, units, info_ref, inner_ref, upstream_ref, middle_ref, params_ref, mix_ref, *refs
):
    unit_refs, refs = refs[:count], refs[count:]
    middle_grad_ref, low_ref, mixed_grad_ref, sums_ref, total, *held = refs
    step = pl.program_id(0)

    @pl.when(step == 0)
    def _():
        total[...] = jnp.zeros_like(total)

    @pl.when(step < units)
    def _():
        weights = inner_unit(
            info_ref, unit_refs, held[0] if held else None, step // max(units // 2, 1)
        )
        total[...] += back_product(inner_ref[...], weights)

    @pl.when(step == units)
    def _():
        normal, scale_inv = normalise(middle_ref[...])
        lifted, gain, shift = norm_backward(total[...], params_ref[5:6], normal, scale_inv)
        middle_grad = upstream_ref[...] + lifted
        middle_grad_ref[...] = middle_grad
        low = middle_grad.astype(LOW)
        low_ref[...] = low
        sums_ref[0:1] = gain
        sums_ref[1:2] = shift
        sums_ref[2:3] = jnp.sum(low.astype(F32), axis=0, keepdims=True)
        sums_ref[3:8] = jnp.zeros((5, sums_ref.shape[1]), F32)
        mixed_grad_ref[...] = back_product(low, unit_of_ref(mix_ref)).astype(LOW)


def inner_back(inner_grad, upstream, middle, params, wide, after):
    units = wide.units
    rows, width = upstream.shape
    return run(
        functools.partial(inner_back_kernel, wide.count(), units),
        "inner_back",
        units + 1,
        [
            (wide.info, scalars()),
            (
                inner_grad,
                pl.BlockSpec((rows, width), lambda step, *_: (0, jnp.minimum(step, units - 1))),
            ),
            (upstream, full(upstream.shape)),
            (middle, full(middle.shape)),
            (params, full(params.shape)),
            wide.mix_spec(),
        ]
        + wide.inner_specs(lambda step: jnp.minimum(step, units - 1)),
        [
            (jax.ShapeDtypeStruct((rows, width), F32), full((rows, width))),
            (jax.ShapeDtypeStruct((rows, width), LOW), full((rows, width))),
            (jax.ShapeDtypeStruct((rows, width), LOW), full((rows, width))),
            (jax.ShapeDtypeStruct((8, width), F32), full((8, width))),
        ],
        [pltpu.VMEM((rows, width), F32)] + wide.inner_scratch(),
        2 * (units + 1) * rows * width * width,
        after,
    )


def joined(terms, groups):
    columns = []
    for group in range(groups):
        term = terms[group][...]
        if len(terms) > groups:
            others = terms[groups + group :: groups]
            term = sum([other[...].astype(F32) for other in others], term.astype(F32))
        columns.append(term.astype(LOW))
    return jnp.concatenate(columns, axis=1)


def split_terms(refs, counts):
    groups, parts = counts
    ends = (groups, groups * (parts + 1), groups * (2 * parts + 1))
    return [refs[: ends[0]], refs[ends[0] : ends[1]], refs[ends[1] : ends[2]]], refs[ends[2] :]


def project_back_kernel(counts, hidden_ref, middle_grad_ref, params_ref, *refs):
    terms, (unit_ref, out_ref, sums_ref, total) = split_terms(refs, counts)
    step = pl.program_id(0)
    weights = unit_of_ref(unit_ref)

    @pl.when(step == 0)
    def _():
        grad = joined(terms[0], counts[0])
        sums_ref[2:3] = jnp.sum(grad.astype(F32), axis=0, keepdims=True)
        total[...] = back_product(grad, weights)

    @pl.when(step == 1)
    def _():
        total[...] += back_product(joined(terms[1], counts[0]), weights)

    @pl.when(step == 2)
    def _():
        grad = joined(terms[2], counts[0])
        sums_ref[3:4] = jnp.sum(grad.astype(F32), axis=0, keepdims=True)
        first_grad = total[...] + back_product(grad, weights)
        normal, scale_inv = normalise(hidden_ref[...])
        lowered, gain, shift = norm_backward(first_grad, params_ref[0:1], normal, scale_inv)
        out_ref[...] = middle_grad_ref[...] + lowered
        sums_ref[0:1] = gain
        sums_ref[1:2] = shift
        sums_ref[4:8] = jnp.zeros((4, sums_ref.shape[1]), F32)


def project_back(hidden, middle_grad, params, terms, chunk, block, first, after):
    rows, width = hidden.shape
    whole = full((rows, width))
    counts = (len(terms[0]), len(terms[1]) // len(terms[0]))
    return run(
        functools.partial(project_back_kernel, counts),
        "project_back",
        3,
        [
            (hidden, whole),
            (middle_grad, whole),
            (params, full(params.shape)),
        ]
        + [(term, full(term.shape)) for some in terms for term in some]
        + [unit_spec(chunk, block, lambda step: first + step)],
        [
            (jax.ShapeDtypeStruct((rows, width), F32), whole),
            (jax.ShapeDtypeStruct((8, width), F32), full((8, width))),
        ],
        [pltpu.VMEM((rows, width), F32)],
        6 * rows * width * width,
        after,
    )


def grad_out(cut, units, width):
    if cut is None:
        shape, scratch = (units, width, width), []
        outs = [
            (
                jax.ShapeDtypeStruct(shape, LOW),
                pl.BlockSpec((1, width, width), lambda step, *_: (step, 0, 0)),
            )
        ]
    else:
        far, deep, block = cut
        shape = (far, deep, units, block, width)
        outs = [(jax.ShapeDtypeStruct(shape, LOW), full(shape))] * 2
        scratch = [pltpu.VMEM((deep, 2 * far, block, width), LOW)]
    return outs, scratch


def split_unit(targets_ref, result, refs, unit):
    if len(refs) == 1:
        refs[0][0] = result.astype(LOW)
        return
    keep_ref, give_ref, held = refs
    held[...] = result.astype(LOW).reshape(held.shape)
    far = keep_ref.shape[0]
    for near in range(far):
        keep_ref[near, :, unit] = held[:, targets_ref[near]]
        give_ref[near, :, unit] = held[:, targets_ref[far + near]]


def wide_grad_kernel(units, targets_ref, second_ref, inner_ref, active_ref, low_ref, *refs):
    step = pl.program_id(0)

    @pl.when(step < units)
    def _():
        split_unit(targets_ref, outer_sum(second_ref[...], inner_ref[...]), refs[:3], step)

    @pl.when(step >= units)
    def _():
        result = outer_sum(active_ref[...], low_ref[...])
        if len(refs) == 1:
            refs[0][0] = result.astype(LOW)
        else:
            keep_ref, give_ref, _, held = refs
            held[...] = result.astype(LOW).reshape(held.shape)
            far = keep_ref.shape[0]
            for near in range(far):
                keep_ref[near, step - units] = held[targets_ref[near]]
                give_ref[near, step - units] = held[targets_ref[far + near]]


def wide_weight_grad(cut, targets, second_low, inner_grad, active, outer_low, units, after):
    rows, width = second_low.shape
    outs, scratch = grad_out(cut, 2 * units, width)
    steps = units
    if cut is not None:
        far, steps, block = cut
        shape = (far, steps, 2 * units, block, width)
        spec = pl.BlockSpec(
            (far, steps, units, block, width),
            lambda step, *_: (0, 0, jnp.where(step < units, 0, 1), 0, 0),
        )
        outs = [(jax.ShapeDtypeStruct(shape, LOW), spec)] * 2
        scratch = scratch + [pltpu.VMEM((2 * far, units, block, width), LOW)]
    share = units * width // steps
    return run(
        functools.partial(wide_grad_kernel, units),
        "wide_weight_grad",
        units + steps,
        [
            (targets, scalars()),
            (second_low, full((rows, width))),
            (
                inner_grad,
                pl.BlockSpec((rows, width), lambda step, *_: (0, jnp.minimum(step, units - 1))),
            ),
            (
                active,
                pl.BlockSpec((rows, share), lambda step, *_: (0, jnp.maximum(step - units, 0))),
            ),
            (outer_low, full((rows, width))),
        ],
        outs,
        scratch,
        4 * units * rows * width * width,
        after,
    )


def thin_grad_kernel(counts, targets_ref, normed_ref, mixed_ref, low_ref, *refs):
    terms, refs = split_terms(refs, counts)
    step = pl.program_id(0)
    for number in range(3):

        @pl.when(step == number)
        def _():
            grad = joined(terms[number], counts[0])
            split_unit(targets_ref, outer_sum(normed_ref[...], grad), refs, step)

    @pl.when(step == 3)
    def _():
        split_unit(targets_ref, outer_sum(mixed_ref[...], low_ref[...]), refs, step)


def thin_weight_grad(cut, targets, normed_low, terms, mixed_out, branch_low, after):
    rows, width = normed_low.shape
    outs, scratch = grad_out(cut, 4, width)
    whole = full((rows, width))
    counts = (len(terms[0]), len(terms[1]) // len(terms[0]))
    return run(
        functools.partial(thin_grad_kernel, counts),
        "thin_weight_grad",
        4,
        [
            (targets, scalars()),
            (normed_low, whole),
            (mixed_out, whole),
            (branch_low, whole),
        ]
        + [(term, full(term.shape)) for some in terms for term in some],
        outs,
        scratch,
        8 * rows * width * width,
        after,
    )


def sum_along_kernel(keep_ref, taken_ref, out_ref):
    out_ref[...] = keep_ref[0] + taken_ref[0]


def sum_along(keep, taken, step_far, after):
    _, deep, units, block, width = keep.shape
    spec = pl.BlockSpec(
        (1, 1, units, block, width), lambda step, *_: (step_far, step, 0, 0, 0)
    )
    return run(
        sum_along_kernel,
        "sum_along",
        deep,
        [(keep, spec), (taken, spec)],
        [
            (
                jax.ShapeDtypeStruct((deep, units, block, width), LOW),
                pl.BlockSpec((1, units, block, width), lambda step, *_: (step, 0, 0, 0)),
            )
        ],
        [],
        2 * units * deep * block * width,
        after,
    )[0]


def sum_near_kernel(keep_ref, taken_ref, *refs):
    along, out_ref = refs[:-1], refs[-1]
    total = keep_ref[0].astype(F32) + taken_ref[0].astype(F32)
    for ref in along:
        total += ref[...].astype(F32)
    out_ref[...] = total.astype(LOW)


def sum_near(keep, taken, along, after):
    _, deep, units, block, width = keep.shape
    near = pl.BlockSpec((1, 1, units, block, width), lambda step, *_: (0, step, 0, 0, 0))
    spec = pl.BlockSpec((1, units, block, width), lambda step, *_: (step, 0, 0, 0))
    return run(
        sum_near_kernel,
        "sum_near",
        deep,
        [(keep, near), (taken, near)] + [(array, spec) for array in along],
        [(jax.ShapeDtypeStruct((deep, units, block, width), LOW), spec)],
        [],
        3 * units * deep * block * width,
        after,
    )[0]


def pack_kernel(units, halves, rep_ref, in_ref, rows_ref, *refs):
    out_ref = refs[-1]
    block, width = in_ref.shape[1], out_ref.shape[1]
    count = units // halves

    def column(unit):
        return in_ref[0, :, unit * width : (unit + 1) * width].astype(LOW)

    for half in range(halves):

        @pl.when((rep_ref[0] == half) | (halves == 1))
        def _():
            for unit in range(count):
                out_ref[unit * block : (unit + 1) * block] = column(4 + half * count + unit)
            rows = rows_ref[0, half * count * block : (half + 1) * count * block]
            out_ref[count * block : 2 * count * block] = rows.astype(LOW)

    for number, unit in enumerate((3, 0, 1, 2)):
        at = (2 * count + number) * block
        out_ref[at : at + block] = column(unit)
    if len(refs) > 1:
        out_ref[(2 * count + 4) * block :] = refs[0][...]


def pack(dense_in, dense_out, layer, units, halves, rep, extra, after):
    _, block, columns = dense_in.shape
    width = dense_out.shape[2]
    rows = (2 * units // halves + 4) * block
    ins = [
        (rep, scalars()),
        (dense_in, pl.BlockSpec((1, block, columns), lambda step, *_: (layer, 0, 0))),
        (
            dense_out,
            pl.BlockSpec((1,) + dense_out.shape[1:], lambda step, *_: (layer, 0, 0)),
        ),
    ]
    if extra is not None:
        ins.append((extra, full(extra.shape)))
        rows += extra.shape[0]
    return run(
        functools.partial(pack_kernel, units, halves),
        "pack",
        1,
        ins,
        [(jax.ShapeDtypeStruct((rows, width), LOW), full((rows, width)))],
        [],
        rows * width,
        after,
    )[0]


def small_cut_kernel(layers, block, targets_ref, *refs):
    keep_ref, give_ref, held = refs[-3:]
    _, deep, rows, _ = keep_ref.shape
    each = rows // layers
    keep_ref[...] = jnp.zeros_like(keep_ref)
    give_ref[...] = jnp.zeros_like(give_ref)
    for layer in range(layers):
        one, two, outer_sums, inner_sums = (ref[...] for ref in refs[4 * layer : 4 * layer + 4])
        width = one.shape[1]
        at = layer * each
        held[at : at + 4] = one[:4]
        held[at + 4 : at + 5] = two[2:3]
        held[at + 5 : at + 7] = two[:2]
        held[at + 7 : at + 8] = outer_sums
        for unit in range(each - 8):
            held[at + 8 + unit : at + 9 + unit] = inner_sums[:, unit * width : (unit + 1) * width]
    far = keep_ref.shape[0]
    for depth in range(deep):
        for near in range(far):
            for place in range(2 * far):
                start = (depth * 2 * far + place) * block

                @pl.when(targets_ref[near] == place)
                def _():
                    keep_ref[near, depth, :, :block] = held[:, start : start + block]

                @pl.when(targets_ref[far + near] == place)
                def _():
                    give_ref[near, depth, :, :block] = held[:, start : start + block]


def small_cut(cut, targets, parts, layers, after):
    far, deep, block = cut
    width = parts[0].shape[1]
    rows = layers * (8 + parts[3].shape[1] // width)
    shape = (far, deep, rows, LANES)
    return run(
        functools.partial(small_cut_kernel, layers, block),
        "small_cut",
        1,
        [(targets, scalars())] + [(part, full(part.shape)) for part in parts],
        [(jax.ShapeDtypeStruct(shape, F32), full(shape))] * 2,
        [pltpu.VMEM((rows, width), F32)],
        rows * width,
        after,
    )


def adam_kernel(usual, special, chosen, weight_ref, first_ref, second_ref, *refs):
    grads, (grad_ref, moment_ref, square_ref, updated_ref) = refs[:-4], refs[-4:]
    grad = sum([ref[0].astype(F32) for ref in grads[1:]], grads[0][0].astype(F32))
    grad = grad.reshape(weight_ref.shape)
    rate = jnp.where(pl.program_id(0) == chosen, special, usual)
    moment, square, updated = adam_step(weight_ref[...], grad, first_ref[...], second_ref[...], rate)
    grad_ref[...] = grad
    moment_ref[...] = moment
    square_ref[...] = square
    updated_ref[...] = updated


def adam(state, grads, layer, first, count, from_unit, rates, after, reuse):
    weight = state[0]
    block, width = grads[0].shape[1:]
    if weight.ndim == 3 and weight.shape[2] == width:
        spec = pl.BlockSpec((1, block, width), lambda step, *_: (layer, first + step, 0))
    elif weight.ndim == 3:
        spec = pl.BlockSpec((1, block, width), lambda step, *_: (layer, 0, first + step))
    else:
        spec = pl.BlockSpec((1, 1, block, width), lambda step, *_: (layer, first + step, 0, 0))
    usual, special, chosen = rates
    return run(
        functools.partial(adam_kernel, usual, special, chosen - first),
        "adam",
        count,
        [(array, spec) for array in state]
        + [
            (grad, pl.BlockSpec((1, block, width), lambda step, *_: (from_unit + step, 0, 0)))
            for grad in grads
        ],
        [(jax.ShapeDtypeStruct(weight.shape, F32), spec)] * 4,
        [],
        16 * count * block * width,
        after,
        None,
        reuse,
    )


def part_kernel(lower_ref, rows_ref, keep_ref, give_ref):
    count = keep_ref.shape[0]
    lower, upper = rows_ref[:count], rows_ref[count:]
    in_lower = lower_ref[0] != 0
    keep_ref[...] = jnp.where(in_lower, lower, upper).astype(keep_ref.dtype)
    give_ref[...] = jnp.where(in_lower, upper, lower).astype(LOW)


def part_clips(in_lower, rows, kind, after):
    count, width = rows.shape[0] // 2, rows.shape[1]
    return run(
        part_kernel,
        "part_clips",
        1,
        [(in_lower, scalars()), (rows, full(rows.shape))],
        [
            (jax.ShapeDtypeStruct((count, width), kind), full((count, width))),
            (jax.ShapeDtypeStruct((count, width), LOW), full((count, width))),
        ],
        [],
        rows.size,
        after,
    )


def query_block(rows):
    return next(size for size in (768, 384, 256, 128) if rows % size == 0)


def attend_kernel(parts, block, bias_ref, q_ref, *refs):
    k_refs, v_refs = refs[:parts], refs[parts : 2 * parts]
    o_ref, lse_ref = refs[2 * parts :]
    rows = q_ref.shape[0]
    q_side = (q_ref[...] * jnp.bfloat16(LOGIT_SCALE)).T
    ones = jnp.ones((16, rows), LOW)
    v_heads = []
    for ref in v_refs:
        side = ref[...].T
        v_heads.append(
            [jnp.concatenate([side[h * HDIM : (h + 1) * HDIM], ones]) for h in range(2)]
        )
    head_of = lax.broadcasted_iota(jnp.int32, (LANES, block), 0) // HDIM
    for start in range(0, rows, block):
        q_block = q_side[:, start : start + block]
        both = []
        for head in range(2):
            q_head = jnp.where(head_of == head, q_block, jnp.zeros_like(q_block))
            scores = []
            for part in range(parts):
                score = product(k_refs[part][...], q_head)
                lower, upper = score[: rows // 2], score[rows // 2 :]
                bias = jnp.tile(bias_ref[part], (1, block // LANES))
                scores.append(jnp.concatenate([lower, upper + bias], axis=0))
            top = functools.reduce(
                jnp.maximum, [jnp.max(score, axis=0, keepdims=True) for score in scores]
            )
            weights = [jnp.exp(score - top).astype(LOW) for score in scores]
            summed = sum(product(v_heads[part][head], weights[part]) for part in range(parts))
            total = summed[HDIM : HDIM + 1]
            both.append(summed[:HDIM] / total)
            lse_ref[0, head : head + 1, start : start + block] = top + jnp.log(total)
        o_ref[start : start + block, :] = jnp.concatenate(both, axis=0).T.astype(LOW)


def attend(queries, own, others, bias, after):
    rows, width = queries.shape
    pairs = width // LANES
    parts = len(others) + 1

    def columns(base):
        return pl.BlockSpec((rows, LANES), lambda pair, *_: (0, base * pairs + pair))

    return run(
        functools.partial(attend_kernel, parts, query_block(rows)),
        "attend",
        pairs,
        [(bias, full(bias.shape)), (queries, columns(0))]
        + [(array, columns(0)) for array in (own, *others)]
        + [(array, columns(1)) for array in (own, *others)],
        [
            (jax.ShapeDtypeStruct((rows, width), LOW), columns(0)),
            (
                jax.ShapeDtypeStruct((pairs, 2, rows), F32),
                pl.BlockSpec((1, 2, rows), lambda pair, *_: (pair, 0, 0)),
            ),
        ],
        [],
        16 * rows * rows * parts * width,
        after,
    )


def attend_back_kernel(parts, block, bias_ref, q_ref, *refs):
    k_refs, v_refs = refs[:parts], refs[parts : 2 * parts]
    o_ref, do_ref, lse_ref = refs[2 * parts : 2 * parts + 3]
    dq_ref = refs[2 * parts + 3]
    dk_refs = refs[2 * parts + 4 : 3 * parts + 4]
    dv_refs = refs[3 * parts + 4 :]
    rows = q_ref.shape[0]
    q_rows = q_ref[...] * jnp.bfloat16(LOGIT_SCALE)
    do_rows = do_ref[...]
    q_side, do_side = q_rows.T, do_rows.T
    shared = (do_rows.astype(F32) * o_ref[...].astype(F32)).T
    delta = [
        jnp.sum(shared[head * HDIM : (head + 1) * HDIM], axis=0, keepdims=True)
        for head in range(2)
    ]
    head_of = lax.broadcasted_iota(jnp.int32, (LANES, rows), 0) // HDIM
    zeros = jnp.zeros_like(q_side)
    q_heads = [jnp.where(head_of == head, q_side, zeros) for head in range(2)]
    do_heads = [jnp.where(head_of == head, do_side, zeros) for head in range(2)]
    lane = lax.broadcasted_iota(jnp.int32, (block, LANES), 1)
    dq_sides = [jnp.zeros((HDIM, rows), F32)] * 2
    for part in range(parts):
        for start in range(0, rows, block):
            here = slice(start, start + block)
            k_block, v_block = k_refs[part][here], v_refs[part][here]
            k_side = k_block.T
            dk_heads, dv_heads = [], []
            for head in range(2):
                score = product(k_block, q_heads[head])
                if start + block > rows // 2:
                    skip = max(rows // 2 - start, 0)
                    upper = bias_ref[part][start + skip - rows // 2 : start + block - rows // 2]
                    raised = score[skip:] + jnp.tile(upper, (1, rows // LANES))
                    score = jnp.concatenate([score[:skip], raised], axis=0) if skip else raised
                chances = jnp.exp(score - lse_ref[0, head : head + 1])
                chance_grad = product(v_block, do_heads[head])
                score_grad = (chances * (chance_grad - delta[head])).astype(LOW)
                dq_sides[head] = dq_sides[head] + product(
                    k_side[head * HDIM : (head + 1) * HDIM], score_grad
                )
                dk_heads.append(product(score_grad, q_rows))
                dv_heads.append(product(chances.astype(LOW), do_rows))
            dk_refs[part][here] = jnp.where(lane < HDIM, *dk_heads).astype(LOW)
            dv_refs[part][here] = jnp.where(lane < HDIM, *dv_heads).astype(LOW)
    dq_ref[...] = (jnp.concatenate(dq_sides, axis=0) * LOGIT_SCALE).T.astype(LOW)


def attend_back(queries, own, others, mixed_out, mixed_grad, log_total, bias, group, groups, after):
    rows, width = queries.shape
    pairs = width // LANES
    parts = len(others) + 1
    first = group * pairs // groups
    count = (group + 1) * pairs // groups - first

    def columns(base):
        return pl.BlockSpec((rows, LANES), lambda pair, *_: (0, base * pairs + first + pair))

    out = run(
        functools.partial(attend_back_kernel, parts, query_block(rows)),
        "attend_back",
        count,
        [(bias, full(bias.shape)), (queries, columns(0))]
        + [(array, columns(0)) for array in (own, *others)]
        + [(array, columns(1)) for array in (own, *others)]
        + [
            (mixed_out, columns(0)),
            (mixed_grad, columns(0)),
            (log_total, pl.BlockSpec((1, 2, rows), lambda pair, *_: (first + pair, 0, 0))),
        ],
        [
            (
                jax.ShapeDtypeStruct((rows, count * LANES), LOW),
                pl.BlockSpec((rows, LANES), lambda pair, *_: (0, pair)),
            )
        ]
        * (2 * parts + 1),
        [],
        40 * rows * rows * parts * count * LANES,
        after,
    )
    return out[0], out[1 : parts + 1], out[parts + 1 :]


def on_device(
    frames,
    lengths,
    cotangent,
    dense_in,
    dense_out,
    small_params,
    first_in,
    first_out,
    first_small,
    second_in,
    second_out,
    second_small,
):
    clip_count, local_frames, width = frames.shape
    layer_count, block, columns_in = dense_in.shape
    units = columns_in // width - 4
    seq, deep, reps = lax.axis_size("seq"), lax.axis_size("fsdp"), lax.axis_size("rep")
    half = seq // clip_count
    total_frames = local_frames * seq
    place, depth = lax.axis_index("seq"), lax.axis_index("fsdp")
    owners = seq * deep
    my_clip, my_member = place // half, place % half
    in_lower = my_clip == 0
    swap = [(source, (source + half) % seq) for source in range(seq)]
    far = seq // 2
    row, core = place // 2, place % 2
    cut = (far, deep, block) if block % 16 == 0 else None

    def turn(axis, step):
        size = lax.axis_size(axis)
        return [(source, (source + step) % size) for source in range(size)]

    over_core = [(source, source ^ 1) for source in range(seq)]

    def to_clips(arrays):
        whole = jnp.stack(arrays, axis=1)
        kept = lax.dynamic_index_in_dim(whole, my_clip, 0, keepdims=False)
        given = lax.dynamic_index_in_dim(whole, 1 - my_clip, 0, keepdims=False)
        taken = lax.ppermute(given, "seq", swap)
        lower, upper = jnp.where(in_lower, kept, taken), jnp.where(in_lower, taken, kept)
        return [
            jnp.concatenate([lower[number], upper[number]], axis=0).astype(F32)
            for number in range(len(arrays))
        ]

    def split_clips(rows):
        lower, upper = rows[:local_frames], rows[local_frames:]
        return jnp.where(in_lower, lower, upper), jnp.where(in_lower, upper, lower).astype(LOW)

    def from_clips(kept, given):
        taken = lax.ppermute(given, "seq", swap).astype(kept.dtype)
        return jnp.stack([jnp.where(in_lower, kept, taken), jnp.where(in_lower, taken, kept)])

    def around(step):
        return [
            (source, source - source % half + (source % half + step) % half)
            for source in range(seq)
        ]

    halves = 2 if reps == 2 and units % 2 == 0 and deep % 2 == 0 and cut is not None else 1
    info = jnp.stack([lax.axis_index("rep"), core])

    def gather(layer, extra, after):
        if cut is None:
            columns = dense_in[layer].astype(LOW).reshape(block, 4 + units, width)
            columns = columns.transpose(1, 0, 2)
            columns = lax.all_gather(columns, ("fsdp", "seq"), axis=1, tiled=True)
            rows = lax.all_gather(
                dense_out[layer].astype(LOW), ("fsdp", "seq"), axis=0, tiled=True
            )
            parts = [columns[4:].reshape(-1, width), rows, columns[3], *columns[:3]]
            return Wide(jnp.concatenate(parts)[None], None, info, width, units)
        own = pack(dense_in, dense_out, layer, units, halves, info, extra, after)
        chunk = lax.all_gather(own, ("fsdp", "seq"), axis=0)
        if halves == 1:
            return Wide(chunk, None, info, block, units)
        return Wide(chunk, [None, None], info, block, units)

    def share(wide, marker):
        wide.given = []
        if wide.sent:
            wide.chunk, marker = lax.optimization_barrier((wide.chunk, marker))
            rows = units // 2 * block
            shape = (owners // 2, rows, width)
            wide.given = [
                lax.dynamic_slice(wide.chunk, (core * (owners // 2), number * rows, 0), shape)
                for number in range(2)
            ]
            wide.near = [lax.ppermute(part, "rep", turn("rep", 1)) for part in wide.given]
        return marker

    def exchange(wide, number, marker):
        if wide.sent:
            near, marker = lax.optimization_barrier((wide.near[number], marker))
            wide.sent[number] = (near, lax.ppermute(near, "seq", over_core))
        return marker

    targets = jnp.stack(
        [
            (row + step) % far * 2 + (core + other) % 2
            for other in range(2)
            for step in range(far)
        ]
    )

    def start_core(parts):
        if cut is None:
            return parts, []
        return (parts[0], lax.ppermute(parts[1], "seq", over_core)), [parts[0]]

    def start_far(chunk, after):
        if cut is None:
            return chunk
        keep, taken = chunk[0]
        sums = [sum_along(keep, taken, step, after) for step in range(1, far)]
        moved = [
            lax.ppermute(part, "seq", turn("seq", 2 * step + 2)) for step, part in enumerate(sums)
        ]
        return (keep, taken, moved), sums

    def whole_deep(chunk, after):
        if cut is None:
            return chunk
        total = sum_near(*chunk[0], after)
        return lax.psum_scatter(total, "fsdp", scatter_dimension=0, tiled=True)[0], [total]

    def start_reps(chunk):
        if cut is None:
            result = chunk[0][0]
            owned = lax.psum_scatter(
                result[:units], ("fsdp", "seq"), scatter_dimension=1, tiled=True
            )
            if result.shape[0] > units:
                rows = lax.psum_scatter(
                    result[units:].reshape(units * width, width),
                    ("fsdp", "seq"),
                    scatter_dimension=0,
                    tiled=True,
                )
                owned = jnp.concatenate([owned, rows.reshape(units, block, width)])
        else:
            owned = chunk[0]
        return owned, [lax.ppermute(owned, "rep", turn("rep", step)) for step in range(1, reps)]

    def finish(state):
        owned, arrived = state
        return sum([part.astype(F32) for part in arrived], owned.astype(F32))

    length = lax.dynamic_index_in_dim(lengths, my_clip, 0, keepdims=False)
    bias = jnp.stack(
        [
            jnp.broadcast_to(
                jnp.where(
                    (half + (my_member - step) % half) * local_frames
                    + jnp.arange(local_frames, dtype=jnp.int32)
                    < length,
                    0.0,
                    MASKED,
                )[:, None],
                (local_frames, LANES),
            )
            for step in range(half)
        ]
    ).astype(F32)

    small_low = small_params.astype(LOW)
    extra = None
    if cut is not None:
        extra = jnp.pad(small_low.reshape(-1), (0, -small_low.size % (16 * width)))
        extra = extra.reshape(-1, width)
    wides = []
    for layer in range(layer_count):
        wides.append(gather(layer, extra if layer == 0 else None, []))
    if cut is None:
        params_all = lax.all_gather(small_low, ("fsdp", "seq"), axis=2, tiled=True)
    else:
        first_row = (wides[0].thin_at + 3) * block
        params_all = wides[0].chunk[:, first_row:].reshape(owners, -1)[:, : small_low.size]
        params_all = params_all.reshape((owners,) + small_low.shape).transpose(1, 2, 0, 3)
        params_all = params_all.reshape(layer_count, -1, width)
    params_all = params_all.astype(F32)

    row_steps = units if cut is None else deep
    hidden, upstream = to_clips([frames, cotangent])
    stored = []
    for layer_index in range(layer_count):
        params = params_all[layer_index]
        wide = wides[layer_index]
        hidden = share(wide, hidden)
        normed_low, queries, own = project(
            hidden, params, wide.chunk, wide.block, wide.thin_at, wide.given
        )
        others = [lax.ppermute(own, "seq", around(step)) for step in range(1, half)]
        mixed_out, log_total = attend(queries, own, others, bias, [])
        mixed_out = exchange(wide, 0, mixed_out)
        middle, second_low, active, slope = inner(hidden, mixed_out, params, wide, [])
        middle = exchange(wide, 1, middle)
        stored.append(
            (hidden, normed_low, queries, own, others, log_total, mixed_out)
            + (middle, second_low, active, slope)
        )
        if layer_index + 1 < layer_count:
            hidden = outer(middle, active, params, wide, row_steps, [])
    groups = 2 if width // LANES % 2 == 0 else 1
    def arrivals(number):
        return [
            part
            for layer in range(1, layer_count)
            for some in parts_out[layer][number : number + 1]
            for part in some[1]
        ]

    order = []
    waiting = None
    parts_out = {}
    done_in, done_out = (), ()
    rows_shape = (layer_count, units, block, width)
    states_in = (dense_in, first_in, second_in)
    states_out = (dense_out, first_out, second_out)
    if cut is None:
        states_out = [array.reshape(rows_shape) for array in states_out]
    rates_in = (RATE_DENSE, RATE_DENSE * math.sqrt(total_frames / 3.0), 3)
    rates_out = (RATE_OUTER, RATE_OUTER, 0)

    def flat(part):
        return [part[0]] + part[1]

    small_grads = []
    for layer_index in reversed(range(layer_count)):
        wide = wides[layer_index]
        params = params_all[layer_index]
        (
            hidden,
            normed_low,
            queries,
            own,
            others,
            log_total,
            mixed_out,
            middle,
            second_low,
            active,
            slope,
        ) = stored[layer_index]
        outer_low, inner_grad, bias_inner, bias_outer = outer_back(
            upstream, slope, wide, row_steps, order
        )
        order = [inner_grad]
        if waiting:
            waiting = start_far(waiting, order)
            order = order + waiting[1]
        wide_part = start_core(
            wide_weight_grad(
                cut, targets, second_low, inner_grad, active, outer_low, units, order
            )
        )
        middle_grad, branch_low, mixed_grad, sums_two = inner_back(
            inner_grad, upstream, middle, params, wide, wide_part[1]
        )
        order = [middle_grad]
        wide_part = start_far(wide_part, order)
        order = order + wide_part[1]
        q_terms, k_near, v_near, k_far, v_far = [], [], [], [], []
        for group in range(groups):
            q_term, k_terms, v_terms = attend_back(
                queries,
                own,
                others,
                mixed_out,
                mixed_grad,
                log_total,
                bias,
                group,
                groups,
                order,
            )
            q_terms.append(q_term)
            k_near.append(k_terms[0])
            v_near.append(v_terms[0])
            k_far.append(k_terms[1:])
            v_far.append(v_terms[1:])
            order = [q_term]
            if waiting and group == 0:
                waiting = whole_deep(waiting, order)
                order = order + waiting[1]

        def all_terms(near, terms):
            moved = [
                lax.ppermute(terms[group][step - 1], "seq", around(half - step))
                for step in range(1, half)
                for group in range(groups)
            ]
            return list(near) + moved

        terms = [q_terms, all_terms(k_near, k_far), all_terms(v_near, v_far)]
        order = [q_terms[-1]]

        if layer_index == 0:
            if waiting:
                waiting = start_reps(waiting)
                parts_out[1] += (waiting,)
            thin_part = start_core(
                thin_weight_grad(
                    cut, targets, normed_low, terms, mixed_out, branch_low, order
                )
            )
            wide_part = whole_deep(wide_part, thin_part[1] + arrivals(0))
            for layer in reversed(range(1, layer_count)):
                last = flat(parts_out[layer][0])
                done_out = adam(
                    states_out, last, layer, 0, units, units, rates_out, wide_part[1], done_out
                )
            thin_part = start_far(thin_part, list(done_out[:1]) + arrivals(1))
            order = thin_part[1]
        upstream, sums_one = project_back(
            hidden, middle_grad, params, terms, wide.chunk, wide.block, wide.thin_at, order
        )
        if layer_index > 0:
            if waiting:
                waiting = start_reps(waiting)
                parts_out[layer_index + 1] += (waiting,)
            wide_part = whole_deep(wide_part, [upstream])
            thin_part = start_core(
                thin_weight_grad(
                    cut,
                    targets,
                    normed_low,
                    terms,
                    mixed_out,
                    branch_low,
                    [upstream] + wide_part[1],
                )
            )
        waiting = thin_part
        order = waiting[1]
        parts_out[layer_index] = (start_reps(wide_part) if layer_index > 0 else wide_part,)
        small_grads = [sums_one, sums_two, bias_outer, bias_inner] + small_grads
    if cut is not None:
        keep, give = small_cut(cut, targets, small_grads, layer_count, [upstream])
        cuts = keep + lax.ppermute(give, "seq", over_core)
        along = [lax.ppermute(cuts[step], "seq", turn("seq", 2 * step)) for step in range(1, far)]

    middle, active = stored[-1][7], stored[-1][9]
    result = outer(middle, active, params_all[-1], wides[-1], row_steps, [upstream])
    waiting = whole_deep(waiting, list(done_out[:1]) + [result])
    order = waiting[1] or [upstream]
    encoded = from_clips(*part_clips(in_lower.astype(jnp.int32).reshape(1), result, LOW, order))
    for layer in reversed(range(1, layer_count)):
        wide_part, thin_part = parts_out[layer]
        for part, first, count in ((wide_part, 4, units), (thin_part, 0, 4)):
            done_in = adam(
                states_in, flat(part), layer, first, count, 0, rates_in, order, done_in
            )
    wide_part = parts_out[0][0]
    if cut is not None and done_in:
        mine, *done_in = lax.optimization_barrier((wide_part[0], *done_in))
        wide_part = (mine, wide_part[1])
    wide_part = start_reps(wide_part)
    ready = order + list(done_in[:1]) + (along if cut else [])
    frames_grad = from_clips(
        *part_clips(in_lower.astype(jnp.int32).reshape(1), upstream, F32, ready)
    )
    if cut is not None:
        total = sum(along, cuts[0])
        deeper = [
            lax.ppermute(
                lax.dynamic_index_in_dim(total, (depth + step) % deep, 0, keepdims=False),
                "fsdp",
                turn("fsdp", step),
            )
            for step in range(1, deep)
        ]
    done_in = adam(states_in, flat(wide_part), 0, 4, units, 0, rates_in, order, done_in)
    thin_part = start_reps(waiting)
    order = order + [done_in[0], thin_part[0]]
    done_out = adam(states_out, flat(wide_part), 0, 0, units, units, rates_out, order, done_out)
    if cut is None:
        small_all = jnp.stack(
            [
                jnp.concatenate([one[:4], two[2:3], two[:2], outer_sums])
                for one, two, outer_sums, _ in zip(*[iter(small_grads)] * 4)
            ]
        )
        inner_all = jnp.stack([part.reshape(units, width) for part in small_grads[3::4]])
        small_all = jnp.concatenate([small_all, inner_all], axis=1)
        small_all = small_all.reshape(layer_count, -1, owners, block).transpose(2, 0, 1, 3)
        owned_small = lax.psum_scatter(
            small_all, ("fsdp", "seq"), scatter_dimension=0, tiled=True
        )
    else:
        (total, *deeper, _) = lax.optimization_barrier((total, *deeper, done_in[0]))
        owned_small = lax.dynamic_index_in_dim(total, depth, 0, keepdims=False)
        owned_small = sum(deeper, owned_small)[:, :block]
    owned_small = owned_small.reshape(small_params.shape).astype(LOW)
    done_in = adam(states_in, flat(thin_part), 0, 0, 4, 0, rates_in, [done_out[0]], done_in)
    grad_in, moment_in, square_in, updated_in = done_in
    grad_out_rows, moment_out, square_out, updated_out = (
        array.reshape(dense_out.shape) for array in done_out
    )
    grad_small = finish(
        (owned_small, [lax.ppermute(owned_small, "rep", turn("rep", s)) for s in range(1, reps)])
    )
    moment_small, square_small, updated_small = adam_step(
        small_params, grad_small, first_small, second_small, RATE_SMALL
    )
    return (
        encoded,
        frames_grad,
        grad_in,
        grad_out_rows,
        grad_small,
        moment_in,
        moment_out,
        moment_small,
        square_in,
        square_out,
        square_small,
        updated_in,
        updated_out,
        updated_small,
    )


def solution(mesh):
    clips = P(("rep", "fsdp"), "seq", None)
    rows = P(None, ("fsdp", "seq"), None)
    lanes = P(None, None, ("fsdp", "seq"))
    return jax.shard_map(
        on_device,
        mesh=mesh,
        in_specs=(clips, P(("rep", "fsdp")), clips) + (rows, rows, lanes) * 3,
        out_specs=(clips, clips) + (rows, rows, lanes) * 4,
        check_vma=False,
    )
```

```python
import functools
import math

import jax
import jax.numpy as jnp
from jax import lax
from jax.experimental import pallas as pl
from jax.experimental.pallas import tpu as pltpu
from jax.sharding import PartitionSpec as P

HDIM = 64
STEP = 10

NORM_EPSILON = 1e-05
BETA_ONE = 0.9
BETA_TWO = 0.999
ADAM_EPSILON = 1e-08
DECAY_RATE = 0.01
RATE_DENSE = 0.1
RATE_OUTER = 0.05
RATE_SMALL = 0.5
INV_ROOT_TWO = 0.7071067811865476
INV_ROOT_TAU = 0.3989422804014327
LOGIT_SCALE = 0.125
MASKED = -1e30
LANES = 128
VMEM_LIMIT = 60 * 2**20

F32 = jnp.float32
LOW = jnp.bfloat16


def adam_step(weight, gradient, first, second, rate):
    moment = BETA_ONE * first + (1.0 - BETA_ONE) * gradient
    square = BETA_TWO * second + (1.0 - BETA_TWO) * gradient * gradient
    moment_hat = moment / (1.0 - BETA_ONE**STEP)
    square_hat = square / (1.0 - BETA_TWO**STEP)
    updated = weight - rate * (
        moment_hat / (jnp.sqrt(square_hat) + ADAM_EPSILON) + DECAY_RATE * weight
    )
    return (moment, square, updated)


def product(left_side, right_side):
    return jnp.dot(left_side, right_side, preferred_element_type=F32)


def back_product(left_side, right_side):
    return lax.dot_general(
        left_side, right_side, (((1,), (1,)), ((), ())), preferred_element_type=F32
    )


def outer_sum(left_side, right_side):
    return lax.dot_general(
        left_side, right_side, (((0,), (0,)), ((), ())), preferred_element_type=F32
    )


def normalise(values_in):
    centred = values_in - jnp.mean(values_in, axis=-1, keepdims=True)
    scale_inv = lax.rsqrt(jnp.mean(centred * centred, axis=-1, keepdims=True) + NORM_EPSILON)
    return centred * scale_inv, scale_inv


def norm_backward(upstream, gain_row, normal, scale_inv):
    scaled = upstream * gain_row
    inside = (
        scaled
        - jnp.mean(scaled, axis=-1, keepdims=True)
        - normal * jnp.mean(scaled * normal, axis=-1, keepdims=True)
    )
    return (
        scale_inv * inside,
        jnp.sum(upstream * normal, axis=0, keepdims=True),
        jnp.sum(upstream, axis=0, keepdims=True),
    )


def run(kernel, name, steps, ins, outs, scratch, flops, after=(), scalar=None, reuse=()):
    in_arrays, in_specs = zip(*ins)
    out_shapes, out_specs = zip(*outs)
    moved = sum(a.size * a.dtype.itemsize for a in in_arrays)
    moved += sum(math.prod(s.shape) * s.dtype.itemsize for s in out_shapes)
    lead = 0 if scalar is None else 1

    spare = [*after, *reuse]
    aliases = {lead + len(ins) + len(after) + number: number for number in range(len(reuse))}

    def body(*refs):
        kernel(*refs[: lead + len(ins)], *refs[lead + len(ins) + len(spare) :])

    grid_spec = pltpu.PrefetchScalarGridSpec(
        num_scalar_prefetch=lead,
        grid=(steps,),
        in_specs=list(in_specs) + [pl.BlockSpec(memory_space=pl.ANY)] * len(spare),
        out_specs=list(out_specs),
        scratch_shapes=scratch,
    )
    return pl.pallas_call(
        body,
        grid_spec=grid_spec,
        out_shape=list(out_shapes),
        input_output_aliases=aliases,
        compiler_params=pltpu.CompilerParams(vmem_limit_bytes=VMEM_LIMIT),
        cost_estimate=pl.CostEstimate(flops=flops, bytes_accessed=moved, transcendentals=0),
        name=name,
    )(*(() if scalar is None else (scalar,)), *in_arrays, *spare)


def full(shape):
    return pl.BlockSpec(shape, lambda step, *_: (0,) * len(shape))


def scalars():
    return pl.BlockSpec(memory_space=pltpu.SMEM)


def unit_spec(chunk, block, unit_of):
    owners, _, width = chunk.shape
    return chunk, pl.BlockSpec((owners, block, width), lambda step, *_: (0, unit_of(step), 0))


def unit_of_ref(ref):
    return ref[...].reshape(-1, ref.shape[-1])


class Wide:
    def __init__(self, chunk, sent, info, block, units):
        self.chunk, self.sent, self.info = chunk, sent, info
        self.block, self.units = block, units
        self.held = units // 2 if sent else units
        self.mix_at = 2 * self.held
        self.thin_at = self.mix_at + 1

    def mix_spec(self):
        return unit_spec(self.chunk, self.block, lambda step: self.mix_at)

    def inner_specs(self, unit_of):
        arrays = (self.chunk, *self.sent[0]) if self.sent else (self.chunk,)
        return [
            unit_spec(array, self.block, lambda step: lax.rem(unit_of(step), self.held))
            for array in arrays
        ]

    def inner_scratch(self):
        owners, _, width = self.chunk.shape
        return [pltpu.VMEM((owners, self.block, width), LOW)] if self.sent else []

    def outer_specs(self, steps):
        owners, _, width = self.chunk.shape
        if owners == 1:
            return [unit_spec(self.chunk, self.block, lambda step: self.units + step)]
        shape = (owners // steps, self.held * self.block, width)
        specs = [(self.chunk, pl.BlockSpec(shape, lambda step, *_: (step, 1, 0)))]
        if self.sent:
            near = pl.BlockSpec(shape, lambda step, *_: (lax.rem(step, steps // 2), 0, 0))
            specs += [(array, near) for array in self.sent[1]]
        return specs

    def outer_scratch(self, steps):
        owners, _, width = self.chunk.shape
        shape = (owners // steps, self.units * self.block, width)
        return [pltpu.VMEM(shape, LOW)] if self.sent else []

    def count(self):
        return 3 if self.sent else 1


def inner_unit(info_ref, refs, held, half):
    if len(refs) == 1:
        return unit_of_ref(refs[0])
    mine_ref, near_ref, far_ref = refs
    count = near_ref.shape[0]

    @pl.when(info_ref[0] == half)
    def _():
        held[...] = mine_ref[...]

    for core in range(2):

        @pl.when((info_ref[0] != half) & (info_ref[1] == core))
        def _():
            held[core * count : (core + 1) * count] = near_ref[...]
            held[(1 - core) * count : (2 - core) * count] = far_ref[...]

    return unit_of_ref(held)


def outer_unit(info_ref, refs, held, step, steps):
    if len(refs) == 1:
        return unit_of_ref(refs[0])
    mine_ref, near_ref, far_ref = refs
    count = mine_ref.shape[1]
    is_near = step // (steps // 2) == info_ref[1]
    for rep in range(2):

        @pl.when(info_ref[0] == rep)
        def _():
            held[:, rep * count : (rep + 1) * count] = mine_ref[...]

        for ref, wanted in ((near_ref, is_near), (far_ref, jnp.logical_not(is_near))):

            @pl.when((info_ref[0] == rep) & wanted)
            def _():
                held[:, (1 - rep) * count : (2 - rep) * count] = ref[...]

    return unit_of_ref(held)


def project_kernel(hidden_ref, params_ref, unit_ref, normed_ref, q_ref, kv_ref):
    step = pl.program_id(0)

    @pl.when(step == 0)
    def _():
        normal, _ = normalise(hidden_ref[...])
        normed_ref[...] = (normal * params_ref[0:1] + params_ref[1:2]).astype(LOW)

    weights = unit_of_ref(unit_ref)
    added = jnp.where(step == 0, params_ref[2:3], params_ref[3:4])
    added = jnp.where(step == 1, jnp.zeros_like(added), added)
    result = (product(normed_ref[...], weights) + added).astype(LOW)

    @pl.when(step == 0)
    def _():
        q_ref[...] = result

    @pl.when(step > 0)
    def _():
        kv_ref[...] = result


def project(hidden, params, chunk, block, first, after):
    rows, width = hidden.shape
    return run(
        project_kernel,
        "project",
        3,
        [
            (hidden, full(hidden.shape)),
            (params, full(params.shape)),
            unit_spec(chunk, block, lambda step: first + step),
        ],
        [
            (jax.ShapeDtypeStruct((rows, width), LOW), full((rows, width))),
            (jax.ShapeDtypeStruct((rows, width), LOW), full((rows, width))),
            (
                jax.ShapeDtypeStruct((rows, 2 * width), LOW),
                pl.BlockSpec((rows, width), lambda step, *_: (0, jnp.maximum(step - 1, 0))),
            ),
        ],
        [],
        6 * rows * width * width,
        after,
    )


def inner_kernel(count, per_half, info_ref, hidden_ref, mixed_ref, params_ref, mix_ref, *refs):
    unit_refs, refs = refs[:count], refs[count:]
    middle_ref, second_ref, active_ref, slope_ref, *held = refs
    step = pl.program_id(0)

    @pl.when(step == 0)
    def _():
        middle = hidden_ref[...] + (product(mixed_ref[...], unit_of_ref(mix_ref)) + params_ref[4:5])
        middle_ref[...] = middle
        normal, _ = normalise(middle)
        second_ref[...] = (normal * params_ref[5:6] + params_ref[6:7]).astype(LOW)

    @pl.when(step > 0)
    def _():
        weights = inner_unit(info_ref, unit_refs, held[0] if held else None, (step - 1) // per_half)
        inner = product(second_ref[...], weights) + params_ref[pl.ds(step + 7, 1), :]
        cumulative = 0.5 * (1.0 + lax.erf(inner * INV_ROOT_TWO))
        active_ref[...] = (inner * cumulative).astype(LOW)
        slope = cumulative + inner * jnp.exp(-0.5 * inner * inner) * INV_ROOT_TAU
        slope_ref[...] = slope.astype(LOW)


def inner(hidden, mixed_out, params, wide, after):
    units = wide.units
    rows, width = hidden.shape
    spread = pl.BlockSpec((rows, width), lambda step, *_: (0, jnp.maximum(step - 1, 0)))
    return run(
        functools.partial(inner_kernel, wide.count(), max(units // 2, 1)),
        "inner",
        units + 1,
        [
            (wide.info, scalars()),
            (hidden, full(hidden.shape)),
            (mixed_out, full(mixed_out.shape)),
            (params, full(params.shape)),
            wide.mix_spec(),
        ]
        + wide.inner_specs(lambda step: jnp.maximum(step - 1, 0)),
        [
            (jax.ShapeDtypeStruct((rows, width), F32), full((rows, width))),
            (jax.ShapeDtypeStruct((rows, width), LOW), full((rows, width))),
            (jax.ShapeDtypeStruct((rows, units * width), LOW), spread),
            (jax.ShapeDtypeStruct((rows, units * width), LOW), spread),
        ],
        wide.inner_scratch(),
        2 * (units + 1) * rows * width * width,
        after,
    )


def outer_kernel(count, steps, info_ref, middle_ref, active_ref, params_ref, *refs):
    unit_refs, (out_ref, *held) = refs[:count], refs[count:]
    weights = outer_unit(
        info_ref, unit_refs, held[0] if held else None, pl.program_id(0), steps
    )
    term = product(active_ref[...], weights)

    @pl.when(pl.program_id(0) == 0)
    def _():
        out_ref[...] = middle_ref[...] + (term + params_ref[7:8])

    @pl.when(pl.program_id(0) > 0)
    def _():
        out_ref[...] += term


def outer(middle, active, params, wide, steps, after):
    units = wide.units
    rows, width = middle.shape
    return run(
        functools.partial(outer_kernel, wide.count(), steps),
        "outer",
        steps,
        [
            (wide.info, scalars()),
            (middle, full(middle.shape)),
            (active, pl.BlockSpec((rows, units * width // steps), lambda step, *_: (0, step))),
            (params, full(params.shape)),
        ]
        + wide.outer_specs(steps),
        [(jax.ShapeDtypeStruct((rows, width), F32), full((rows, width)))],
        wide.outer_scratch(steps),
        2 * units * rows * width * width,
        after,
    )[0]


def outer_back_kernel(count, steps, info_ref, upstream_ref, slope_ref, *refs):
    unit_refs, refs = refs[:count], refs[count:]
    low_ref, inner_ref, bias_inner_ref, bias_outer_ref, *held = refs
    weights = outer_unit(
        info_ref, unit_refs, held[0] if held else None, pl.program_id(0), steps
    )

    @pl.when(pl.program_id(0) == 0)
    def _():
        low = upstream_ref[...].astype(LOW)
        low_ref[...] = low
        bias_outer_ref[...] = jnp.sum(low.astype(F32), axis=0, keepdims=True)

    grad = (back_product(low_ref[...], weights) * slope_ref[...].astype(F32)).astype(LOW)
    inner_ref[...] = grad
    bias_inner_ref[...] = jnp.sum(grad.astype(F32), axis=0, keepdims=True)


def outer_back(upstream, slope, wide, steps, after):
    units = wide.units
    rows, width = upstream.shape
    share = units * width // steps
    return run(
        functools.partial(outer_back_kernel, wide.count(), steps),
        "outer_back",
        steps,
        [
            (wide.info, scalars()),
            (upstream, full(upstream.shape)),
            (slope, pl.BlockSpec((rows, share), lambda step, *_: (0, step))),
        ]
        + wide.outer_specs(steps),
        [
            (jax.ShapeDtypeStruct((rows, width), LOW), full((rows, width))),
            (
                jax.ShapeDtypeStruct((rows, units * width), LOW),
                pl.BlockSpec((rows, share), lambda step, *_: (0, step)),
            ),
            (
                jax.ShapeDtypeStruct((1, units * width), F32),
                pl.BlockSpec((1, share), lambda step, *_: (0, step)),
            ),
            (jax.ShapeDtypeStruct((1, width), F32), full((1, width))),
        ],
        wide.outer_scratch(steps),
        2 * units * rows * width * width,
        after,
    )


def inner_back_kernel(
    count, units, info_ref, inner_ref, upstream_ref, middle_ref, params_ref, mix_ref, *refs
):
    unit_refs, refs = refs[:count], refs[count:]
    middle_grad_ref, low_ref, mixed_grad_ref, sums_ref, total, *held = refs
    step = pl.program_id(0)

    @pl.when(step == 0)
    def _():
        total[...] = jnp.zeros_like(total)

    @pl.when(step < units)
    def _():
        weights = inner_unit(
            info_ref, unit_refs, held[0] if held else None, step // max(units // 2, 1)
        )
        total[...] += back_product(inner_ref[...], weights)

    @pl.when(step == units)
    def _():
        normal, scale_inv = normalise(middle_ref[...])
        lifted, gain, shift = norm_backward(total[...], params_ref[5:6], normal, scale_inv)
        middle_grad = upstream_ref[...] + lifted
        middle_grad_ref[...] = middle_grad
        low = middle_grad.astype(LOW)
        low_ref[...] = low
        sums_ref[0:1] = gain
        sums_ref[1:2] = shift
        sums_ref[2:3] = jnp.sum(low.astype(F32), axis=0, keepdims=True)
        sums_ref[3:8] = jnp.zeros((5, sums_ref.shape[1]), F32)
        mixed_grad_ref[...] = back_product(low, unit_of_ref(mix_ref)).astype(LOW)


def inner_back(inner_grad, upstream, middle, params, wide, after):
    units = wide.units
    rows, width = upstream.shape
    return run(
        functools.partial(inner_back_kernel, wide.count(), units),
        "inner_back",
        units + 1,
        [
            (wide.info, scalars()),
            (
                inner_grad,
                pl.BlockSpec((rows, width), lambda step, *_: (0, jnp.minimum(step, units - 1))),
            ),
            (upstream, full(upstream.shape)),
            (middle, full(middle.shape)),
            (params, full(params.shape)),
            wide.mix_spec(),
        ]
        + wide.inner_specs(lambda step: jnp.minimum(step, units - 1)),
        [
            (jax.ShapeDtypeStruct((rows, width), F32), full((rows, width))),
            (jax.ShapeDtypeStruct((rows, width), LOW), full((rows, width))),
            (jax.ShapeDtypeStruct((rows, width), LOW), full((rows, width))),
            (jax.ShapeDtypeStruct((8, width), F32), full((8, width))),
        ],
        [pltpu.VMEM((rows, width), F32)] + wide.inner_scratch(),
        2 * (units + 1) * rows * width * width,
        after,
    )


def joined(terms, groups):
    columns = []
    for group in range(groups):
        term = terms[group][...]
        if len(terms) > groups:
            others = terms[groups + group :: groups]
            term = sum([other[...].astype(F32) for other in others], term.astype(F32))
        columns.append(term.astype(LOW))
    return jnp.concatenate(columns, axis=1)


def split_terms(refs, counts):
    groups, parts = counts
    ends = (groups, groups * (parts + 1), groups * (2 * parts + 1))
    return [refs[: ends[0]], refs[ends[0] : ends[1]], refs[ends[1] : ends[2]]], refs[ends[2] :]


def project_back_kernel(counts, hidden_ref, middle_grad_ref, params_ref, *refs):
    terms, (unit_ref, out_ref, sums_ref, total) = split_terms(refs, counts)
    step = pl.program_id(0)
    weights = unit_of_ref(unit_ref)

    @pl.when(step == 0)
    def _():
        grad = joined(terms[0], counts[0])
        sums_ref[2:3] = jnp.sum(grad.astype(F32), axis=0, keepdims=True)
        total[...] = back_product(grad, weights)

    @pl.when(step == 1)
    def _():
        total[...] += back_product(joined(terms[1], counts[0]), weights)

    @pl.when(step == 2)
    def _():
        grad = joined(terms[2], counts[0])
        sums_ref[3:4] = jnp.sum(grad.astype(F32), axis=0, keepdims=True)
        first_grad = total[...] + back_product(grad, weights)
        normal, scale_inv = normalise(hidden_ref[...])
        lowered, gain, shift = norm_backward(first_grad, params_ref[0:1], normal, scale_inv)
        out_ref[...] = middle_grad_ref[...] + lowered
        sums_ref[0:1] = gain
        sums_ref[1:2] = shift
        sums_ref[4:8] = jnp.zeros((4, sums_ref.shape[1]), F32)


def project_back(hidden, middle_grad, params, terms, chunk, block, first, after):
    rows, width = hidden.shape
    whole = full((rows, width))
    counts = (len(terms[0]), len(terms[1]) // len(terms[0]))
    return run(
        functools.partial(project_back_kernel, counts),
        "project_back",
        3,
        [
            (hidden, whole),
            (middle_grad, whole),
            (params, full(params.shape)),
        ]
        + [(term, full(term.shape)) for some in terms for term in some]
        + [unit_spec(chunk, block, lambda step: first + step)],
        [
            (jax.ShapeDtypeStruct((rows, width), F32), whole),
            (jax.ShapeDtypeStruct((8, width), F32), full((8, width))),
        ],
        [pltpu.VMEM((rows, width), F32)],
        6 * rows * width * width,
        after,
    )


def grad_out(cut, units, width):
    if cut is None:
        shape, scratch = (units, width, width), []
        outs = [
            (
                jax.ShapeDtypeStruct(shape, LOW),
                pl.BlockSpec((1, width, width), lambda step, *_: (step, 0, 0)),
            )
        ]
    else:
        far, deep, block = cut
        shape = (far, deep, units, block, width)
        outs = [(jax.ShapeDtypeStruct(shape, LOW), full(shape))] * 2
        scratch = [pltpu.VMEM((deep, 2 * far, block, width), LOW)]
    return outs, scratch


def split_unit(targets_ref, result, refs, unit):
    if len(refs) == 1:
        refs[0][0] = result.astype(LOW)
        return
    keep_ref, give_ref, held = refs
    held[...] = result.astype(LOW).reshape(held.shape)
    far = keep_ref.shape[0]
    for near in range(far):
        keep_ref[near, :, unit] = held[:, targets_ref[near]]
        give_ref[near, :, unit] = held[:, targets_ref[far + near]]


def wide_grad_kernel(units, targets_ref, second_ref, inner_ref, active_ref, low_ref, *refs):
    step = pl.program_id(0)

    @pl.when(step < units)
    def _():
        split_unit(targets_ref, outer_sum(second_ref[...], inner_ref[...]), refs[:3], step)

    @pl.when(step >= units)
    def _():
        result = outer_sum(active_ref[...], low_ref[...])
        if len(refs) == 1:
            refs[0][0] = result.astype(LOW)
        else:
            keep_ref, give_ref, _, held = refs
            held[...] = result.astype(LOW).reshape(held.shape)
            far = keep_ref.shape[0]
            for near in range(far):
                keep_ref[near, step - units] = held[targets_ref[near]]
                give_ref[near, step - units] = held[targets_ref[far + near]]


def wide_weight_grad(cut, targets, second_low, inner_grad, active, outer_low, units, after):
    rows, width = second_low.shape
    outs, scratch = grad_out(cut, 2 * units, width)
    steps = units
    if cut is not None:
        far, steps, block = cut
        shape = (far, steps, 2 * units, block, width)
        spec = pl.BlockSpec(
            (far, steps, units, block, width),
            lambda step, *_: (0, 0, jnp.where(step < units, 0, 1), 0, 0),
        )
        outs = [(jax.ShapeDtypeStruct(shape, LOW), spec)] * 2
        scratch = scratch + [pltpu.VMEM((2 * far, units, block, width), LOW)]
    share = units * width // steps
    return run(
        functools.partial(wide_grad_kernel, units),
        "wide_weight_grad",
        units + steps,
        [
            (targets, scalars()),
            (second_low, full((rows, width))),
            (
                inner_grad,
                pl.BlockSpec((rows, width), lambda step, *_: (0, jnp.minimum(step, units - 1))),
            ),
            (
                active,
                pl.BlockSpec((rows, share), lambda step, *_: (0, jnp.maximum(step - units, 0))),
            ),
            (outer_low, full((rows, width))),
        ],
        outs,
        scratch,
        4 * units * rows * width * width,
        after,
    )


def thin_grad_kernel(counts, targets_ref, normed_ref, mixed_ref, low_ref, *refs):
    terms, refs = split_terms(refs, counts)
    step = pl.program_id(0)
    for number in range(3):

        @pl.when(step == number)
        def _():
            grad = joined(terms[number], counts[0])
            split_unit(targets_ref, outer_sum(normed_ref[...], grad), refs, step)

    @pl.when(step == 3)
    def _():
        split_unit(targets_ref, outer_sum(mixed_ref[...], low_ref[...]), refs, step)


def thin_weight_grad(cut, targets, normed_low, terms, mixed_out, branch_low, after):
    rows, width = normed_low.shape
    outs, scratch = grad_out(cut, 4, width)
    whole = full((rows, width))
    counts = (len(terms[0]), len(terms[1]) // len(terms[0]))
    return run(
        functools.partial(thin_grad_kernel, counts),
        "thin_weight_grad",
        4,
        [
            (targets, scalars()),
            (normed_low, whole),
            (mixed_out, whole),
            (branch_low, whole),
        ]
        + [(term, full(term.shape)) for some in terms for term in some],
        outs,
        scratch,
        8 * rows * width * width,
        after,
    )


def sum_along_kernel(keep_ref, taken_ref, out_ref):
    out_ref[...] = keep_ref[0] + taken_ref[0]


def sum_along(keep, taken, step_far, after):
    _, deep, units, block, width = keep.shape
    spec = pl.BlockSpec(
        (1, 1, units, block, width), lambda step, *_: (step_far, step, 0, 0, 0)
    )
    return run(
        sum_along_kernel,
        "sum_along",
        deep,
        [(keep, spec), (taken, spec)],
        [
            (
                jax.ShapeDtypeStruct((deep, units, block, width), LOW),
                pl.BlockSpec((1, units, block, width), lambda step, *_: (step, 0, 0, 0)),
            )
        ],
        [],
        2 * units * deep * block * width,
        after,
    )[0]


def sum_near_kernel(keep_ref, taken_ref, *refs):
    along, out_ref = refs[:-1], refs[-1]
    total = keep_ref[0].astype(F32) + taken_ref[0].astype(F32)
    for ref in along:
        total += ref[...].astype(F32)
    out_ref[...] = total.astype(LOW)


def sum_near(keep, taken, along, after):
    _, deep, units, block, width = keep.shape
    near = pl.BlockSpec((1, 1, units, block, width), lambda step, *_: (0, step, 0, 0, 0))
    spec = pl.BlockSpec((1, units, block, width), lambda step, *_: (step, 0, 0, 0))
    return run(
        sum_near_kernel,
        "sum_near",
        deep,
        [(keep, near), (taken, near)] + [(array, spec) for array in along],
        [(jax.ShapeDtypeStruct((deep, units, block, width), LOW), spec)],
        [],
        3 * units * deep * block * width,
        after,
    )[0]


def pack_kernel(units, halves, rep_ref, in_ref, rows_ref, *refs):
    out_ref = refs[-1]
    block, width = in_ref.shape[1], out_ref.shape[1]
    count = units // halves

    def column(unit):
        return in_ref[0, :, unit * width : (unit + 1) * width].astype(LOW)

    for half in range(halves):

        @pl.when((rep_ref[0] == half) | (halves == 1))
        def _():
            for unit in range(count):
                out_ref[unit * block : (unit + 1) * block] = column(4 + half * count + unit)
            rows = rows_ref[0, half * count * block : (half + 1) * count * block]
            out_ref[count * block : 2 * count * block] = rows.astype(LOW)

    for number, unit in enumerate((3, 0, 1, 2)):
        at = (2 * count + number) * block
        out_ref[at : at + block] = column(unit)
    if len(refs) > 1:
        out_ref[(2 * count + 4) * block :] = refs[0][...]


def pack(dense_in, dense_out, layer, units, halves, rep, extra, after):
    _, block, columns = dense_in.shape
    width = dense_out.shape[2]
    rows = (2 * units // halves + 4) * block
    ins = [
        (rep, scalars()),
        (dense_in, pl.BlockSpec((1, block, columns), lambda step, *_: (layer, 0, 0))),
        (
            dense_out,
            pl.BlockSpec((1,) + dense_out.shape[1:], lambda step, *_: (layer, 0, 0)),
        ),
    ]
    if extra is not None:
        ins.append((extra, full(extra.shape)))
        rows += extra.shape[0]
    return run(
        functools.partial(pack_kernel, units, halves),
        "pack",
        1,
        ins,
        [(jax.ShapeDtypeStruct((rows, width), LOW), full((rows, width)))],
        [],
        rows * width,
        after,
    )[0]


def small_cut_kernel(layers, block, targets_ref, *refs):
    keep_ref, give_ref, held = refs[-3:]
    _, deep, rows, _ = keep_ref.shape
    each = rows // layers
    keep_ref[...] = jnp.zeros_like(keep_ref)
    give_ref[...] = jnp.zeros_like(give_ref)
    for layer in range(layers):
        one, two, outer_sums, inner_sums = (ref[...] for ref in refs[4 * layer : 4 * layer + 4])
        width = one.shape[1]
        at = layer * each
        held[at : at + 4] = one[:4]
        held[at + 4 : at + 5] = two[2:3]
        held[at + 5 : at + 7] = two[:2]
        held[at + 7 : at + 8] = outer_sums
        for unit in range(each - 8):
            held[at + 8 + unit : at + 9 + unit] = inner_sums[:, unit * width : (unit + 1) * width]
    far = keep_ref.shape[0]
    for depth in range(deep):
        for near in range(far):
            for place in range(2 * far):
                start = (depth * 2 * far + place) * block

                @pl.when(targets_ref[near] == place)
                def _():
                    keep_ref[near, depth, :, :block] = held[:, start : start + block]

                @pl.when(targets_ref[far + near] == place)
                def _():
                    give_ref[near, depth, :, :block] = held[:, start : start + block]


def small_cut(cut, targets, parts, layers, after):
    far, deep, block = cut
    width = parts[0].shape[1]
    rows = layers * (8 + parts[3].shape[1] // width)
    shape = (far, deep, rows, LANES)
    return run(
        functools.partial(small_cut_kernel, layers, block),
        "small_cut",
        1,
        [(targets, scalars())] + [(part, full(part.shape)) for part in parts],
        [(jax.ShapeDtypeStruct(shape, F32), full(shape))] * 2,
        [pltpu.VMEM((rows, width), F32)],
        rows * width,
        after,
    )


def adam_kernel(usual, special, chosen, weight_ref, first_ref, second_ref, *refs):
    grads, (grad_ref, moment_ref, square_ref, updated_ref) = refs[:-4], refs[-4:]
    grad = sum([ref[0].astype(F32) for ref in grads[1:]], grads[0][0].astype(F32))
    grad = grad.reshape(weight_ref.shape)
    rate = jnp.where(pl.program_id(0) == chosen, special, usual)
    moment, square, updated = adam_step(weight_ref[...], grad, first_ref[...], second_ref[...], rate)
    grad_ref[...] = grad
    moment_ref[...] = moment
    square_ref[...] = square
    updated_ref[...] = updated


def adam(state, grads, layer, first, count, from_unit, rates, after, reuse):
    weight = state[0]
    block, width = grads[0].shape[1:]
    if weight.ndim == 3 and weight.shape[2] == width:
        spec = pl.BlockSpec((1, block, width), lambda step, *_: (layer, first + step, 0))
    elif weight.ndim == 3:
        spec = pl.BlockSpec((1, block, width), lambda step, *_: (layer, 0, first + step))
    else:
        spec = pl.BlockSpec((1, 1, block, width), lambda step, *_: (layer, first + step, 0, 0))
    usual, special, chosen = rates
    return run(
        functools.partial(adam_kernel, usual, special, chosen - first),
        "adam",
        count,
        [(array, spec) for array in state]
        + [
            (grad, pl.BlockSpec((1, block, width), lambda step, *_: (from_unit + step, 0, 0)))
            for grad in grads
        ],
        [(jax.ShapeDtypeStruct(weight.shape, F32), spec)] * 4,
        [],
        16 * count * block * width,
        after,
        None,
        reuse,
    )


def part_kernel(lower_ref, rows_ref, keep_ref, give_ref):
    count = keep_ref.shape[0]
    lower, upper = rows_ref[:count], rows_ref[count:]
    in_lower = lower_ref[0] != 0
    keep_ref[...] = jnp.where(in_lower, lower, upper).astype(keep_ref.dtype)
    give_ref[...] = jnp.where(in_lower, upper, lower).astype(LOW)


def part_clips(in_lower, rows, kind, after):
    count, width = rows.shape[0] // 2, rows.shape[1]
    return run(
        part_kernel,
        "part_clips",
        1,
        [(in_lower, scalars()), (rows, full(rows.shape))],
        [
            (jax.ShapeDtypeStruct((count, width), kind), full((count, width))),
            (jax.ShapeDtypeStruct((count, width), LOW), full((count, width))),
        ],
        [],
        rows.size,
        after,
    )


def query_block(rows):
    return next(size for size in (768, 384, 256, 128) if rows % size == 0)


def attend_kernel(parts, block, bias_ref, q_ref, *refs):
    k_refs, v_refs = refs[:parts], refs[parts : 2 * parts]
    o_ref, lse_ref = refs[2 * parts :]
    rows = q_ref.shape[0]
    q_side = (q_ref[...] * jnp.bfloat16(LOGIT_SCALE)).T
    ones = jnp.ones((16, rows), LOW)
    v_heads = []
    for ref in v_refs:
        side = ref[...].T
        v_heads.append(
            [jnp.concatenate([side[h * HDIM : (h + 1) * HDIM], ones]) for h in range(2)]
        )
    head_of = lax.broadcasted_iota(jnp.int32, (LANES, block), 0) // HDIM
    for start in range(0, rows, block):
        q_block = q_side[:, start : start + block]
        both = []
        for head in range(2):
            q_head = jnp.where(head_of == head, q_block, jnp.zeros_like(q_block))
            scores = []
            for part in range(parts):
                score = product(k_refs[part][...], q_head)
                lower, upper = score[: rows // 2], score[rows // 2 :]
                bias = jnp.tile(bias_ref[part], (1, block // LANES))
                scores.append(jnp.concatenate([lower, upper + bias], axis=0))
            top = functools.reduce(
                jnp.maximum, [jnp.max(score, axis=0, keepdims=True) for score in scores]
            )
            weights = [jnp.exp(score - top).astype(LOW) for score in scores]
            summed = sum(product(v_heads[part][head], weights[part]) for part in range(parts))
            total = summed[HDIM : HDIM + 1]
            both.append(summed[:HDIM] / total)
            lse_ref[0, head : head + 1, start : start + block] = top + jnp.log(total)
        o_ref[start : start + block, :] = jnp.concatenate(both, axis=0).T.astype(LOW)


def attend(queries, own, others, bias, after):
    rows, width = queries.shape
    pairs = width // LANES
    parts = len(others) + 1

    def columns(base):
        return pl.BlockSpec((rows, LANES), lambda pair, *_: (0, base * pairs + pair))

    return run(
        functools.partial(attend_kernel, parts, query_block(rows)),
        "attend",
        pairs,
        [(bias, full(bias.shape)), (queries, columns(0))]
        + [(array, columns(0)) for array in (own, *others)]
        + [(array, columns(1)) for array in (own, *others)],
        [
            (jax.ShapeDtypeStruct((rows, width), LOW), columns(0)),
            (
                jax.ShapeDtypeStruct((pairs, 2, rows), F32),
                pl.BlockSpec((1, 2, rows), lambda pair, *_: (pair, 0, 0)),
            ),
        ],
        [],
        16 * rows * rows * parts * width,
        after,
    )


def attend_back_kernel(parts, block, bias_ref, q_ref, *refs):
    k_refs, v_refs = refs[:parts], refs[parts : 2 * parts]
    o_ref, do_ref, lse_ref = refs[2 * parts : 2 * parts + 3]
    dq_ref = refs[2 * parts + 3]
    dk_refs = refs[2 * parts + 4 : 3 * parts + 4]
    dv_refs = refs[3 * parts + 4 :]
    rows = q_ref.shape[0]
    q_rows = q_ref[...] * jnp.bfloat16(LOGIT_SCALE)
    do_rows = do_ref[...]
    q_side, do_side = q_rows.T, do_rows.T
    shared = (do_rows.astype(F32) * o_ref[...].astype(F32)).T
    delta = [
        jnp.sum(shared[head * HDIM : (head + 1) * HDIM], axis=0, keepdims=True)
        for head in range(2)
    ]
    head_of = lax.broadcasted_iota(jnp.int32, (LANES, rows), 0) // HDIM
    zeros = jnp.zeros_like(q_side)
    q_heads = [jnp.where(head_of == head, q_side, zeros) for head in range(2)]
    do_heads = [jnp.where(head_of == head, do_side, zeros) for head in range(2)]
    lane = lax.broadcasted_iota(jnp.int32, (block, LANES), 1)
    dq_sides = [jnp.zeros((HDIM, rows), F32)] * 2
    for part in range(parts):
        for start in range(0, rows, block):
            here = slice(start, start + block)
            k_block, v_block = k_refs[part][here], v_refs[part][here]
            k_side = k_block.T
            dk_heads, dv_heads = [], []
            for head in range(2):
                score = product(k_block, q_heads[head])
                if start + block > rows // 2:
                    skip = max(rows // 2 - start, 0)
                    upper = bias_ref[part][start + skip - rows // 2 : start + block - rows // 2]
                    raised = score[skip:] + jnp.tile(upper, (1, rows // LANES))
                    score = jnp.concatenate([score[:skip], raised], axis=0) if skip else raised
                chances = jnp.exp(score - lse_ref[0, head : head + 1])
                chance_grad = product(v_block, do_heads[head])
                score_grad = (chances * (chance_grad - delta[head])).astype(LOW)
                dq_sides[head] = dq_sides[head] + product(
                    k_side[head * HDIM : (head + 1) * HDIM], score_grad
                )
                dk_heads.append(product(score_grad, q_rows))
                dv_heads.append(product(chances.astype(LOW), do_rows))
            dk_refs[part][here] = jnp.where(lane < HDIM, *dk_heads).astype(LOW)
            dv_refs[part][here] = jnp.where(lane < HDIM, *dv_heads).astype(LOW)
    dq_ref[...] = (jnp.concatenate(dq_sides, axis=0) * LOGIT_SCALE).T.astype(LOW)


def attend_back(queries, own, others, mixed_out, mixed_grad, log_total, bias, group, groups, after):
    rows, width = queries.shape
    pairs = width // LANES
    parts = len(others) + 1
    first = group * pairs // groups
    count = (group + 1) * pairs // groups - first

    def columns(base):
        return pl.BlockSpec((rows, LANES), lambda pair, *_: (0, base * pairs + first + pair))

    out = run(
        functools.partial(attend_back_kernel, parts, query_block(rows)),
        "attend_back",
        count,
        [(bias, full(bias.shape)), (queries, columns(0))]
        + [(array, columns(0)) for array in (own, *others)]
        + [(array, columns(1)) for array in (own, *others)]
        + [
            (mixed_out, columns(0)),
            (mixed_grad, columns(0)),
            (log_total, pl.BlockSpec((1, 2, rows), lambda pair, *_: (first + pair, 0, 0))),
        ],
        [
            (
                jax.ShapeDtypeStruct((rows, count * LANES), LOW),
                pl.BlockSpec((rows, LANES), lambda pair, *_: (0, pair)),
            )
        ]
        * (2 * parts + 1),
        [],
        40 * rows * rows * parts * count * LANES,
        after,
    )
    return out[0], out[1 : parts + 1], out[parts + 1 :]


def on_device(
    frames,
    lengths,
    cotangent,
    dense_in,
    dense_out,
    small_params,
    first_in,
    first_out,
    first_small,
    second_in,
    second_out,
    second_small,
):
    clip_count, local_frames, width = frames.shape
    layer_count, block, columns_in = dense_in.shape
    units = columns_in // width - 4
    seq, deep, reps = lax.axis_size("seq"), lax.axis_size("fsdp"), lax.axis_size("rep")
    half = seq // clip_count
    total_frames = local_frames * seq
    place, depth = lax.axis_index("seq"), lax.axis_index("fsdp")
    owners = seq * deep
    my_clip, my_member = place // half, place % half
    in_lower = my_clip == 0
    swap = [(source, (source + half) % seq) for source in range(seq)]
    far = seq // 2
    row, core = place // 2, place % 2
    cut = (far, deep, block) if block % 16 == 0 else None

    def turn(axis, step):
        size = lax.axis_size(axis)
        return [(source, (source + step) % size) for source in range(size)]

    over_core = [(source, source ^ 1) for source in range(seq)]

    def to_clips(arrays):
        whole = jnp.stack(arrays, axis=1)
        kept = lax.dynamic_index_in_dim(whole, my_clip, 0, keepdims=False)
        given = lax.dynamic_index_in_dim(whole, 1 - my_clip, 0, keepdims=False)
        taken = lax.ppermute(given, "seq", swap)
        lower, upper = jnp.where(in_lower, kept, taken), jnp.where(in_lower, taken, kept)
        return [
            jnp.concatenate([lower[number], upper[number]], axis=0).astype(F32)
            for number in range(len(arrays))
        ]

    def split_clips(rows):
        lower, upper = rows[:local_frames], rows[local_frames:]
        return jnp.where(in_lower, lower, upper), jnp.where(in_lower, upper, lower).astype(LOW)

    def from_clips(kept, given):
        taken = lax.ppermute(given, "seq", swap).astype(kept.dtype)
        return jnp.stack([jnp.where(in_lower, kept, taken), jnp.where(in_lower, taken, kept)])

    def around(step):
        return [
            (source, source - source % half + (source % half + step) % half)
            for source in range(seq)
        ]

    halves = 2 if reps == 2 and units % 2 == 0 and deep % 2 == 0 and cut is not None else 1
    info = jnp.stack([lax.axis_index("rep"), core])

    def gather(layer, extra, after):
        if cut is None:
            columns = dense_in[layer].astype(LOW).reshape(block, 4 + units, width)
            columns = columns.transpose(1, 0, 2)
            columns = lax.all_gather(columns, ("fsdp", "seq"), axis=1, tiled=True)
            rows = lax.all_gather(
                dense_out[layer].astype(LOW), ("fsdp", "seq"), axis=0, tiled=True
            )
            parts = [columns[4:].reshape(-1, width), rows, columns[3], *columns[:3]]
            return Wide(jnp.concatenate(parts)[None], None, info, width, units)
        own = pack(dense_in, dense_out, layer, units, halves, info, extra, after)
        chunk = lax.all_gather(own, ("fsdp", "seq"), axis=0)
        if halves == 1:
            return Wide(chunk, None, info, block, units)
        return Wide(chunk, [None, None], info, block, units)

    def share(wide, marker):
        wide.given = []
        if wide.sent:
            wide.chunk, marker = lax.optimization_barrier((wide.chunk, marker))
            rows = units // 2 * block
            shape = (owners // 2, rows, width)
            wide.given = [
                lax.dynamic_slice(wide.chunk, (core * (owners // 2), number * rows, 0), shape)
                for number in range(2)
            ]
            wide.near = [lax.ppermute(part, "rep", turn("rep", 1)) for part in wide.given]
        return marker

    def exchange(wide, number, marker):
        if wide.sent:
            near, marker = lax.optimization_barrier((wide.near[number], marker))
            wide.sent[number] = (near, lax.ppermute(near, "seq", over_core))
        return marker

    targets = jnp.stack(
        [
            (row + step) % far * 2 + (core + other) % 2
            for other in range(2)
            for step in range(far)
        ]
    )

    def start_core(parts):
        if cut is None:
            return parts, []
        return (parts[0], lax.ppermute(parts[1], "seq", over_core)), [parts[0]]

    def start_far(chunk, after):
        if cut is None:
            return chunk
        keep, taken = chunk[0]
        sums = [sum_along(keep, taken, step, after) for step in range(1, far)]
        moved = [
            lax.ppermute(part, "seq", turn("seq", 2 * step + 2)) for step, part in enumerate(sums)
        ]
        return (keep, taken, moved), sums

    def whole_deep(chunk, after):
        if cut is None:
            return chunk
        total = sum_near(*chunk[0], after)
        return lax.psum_scatter(total, "fsdp", scatter_dimension=0, tiled=True)[0], [total]

    def start_reps(chunk):
        if cut is None:
            result = chunk[0][0]
            owned = lax.psum_scatter(
                result[:units], ("fsdp", "seq"), scatter_dimension=1, tiled=True
            )
            if result.shape[0] > units:
                rows = lax.psum_scatter(
                    result[units:].reshape(units * width, width),
                    ("fsdp", "seq"),
                    scatter_dimension=0,
                    tiled=True,
                )
                owned = jnp.concatenate([owned, rows.reshape(units, block, width)])
        else:
            owned = chunk[0]
        return owned, [lax.ppermute(owned, "rep", turn("rep", step)) for step in range(1, reps)]

    def finish(state):
        owned, arrived = state
        return sum([part.astype(F32) for part in arrived], owned.astype(F32))

    length = lax.dynamic_index_in_dim(lengths, my_clip, 0, keepdims=False)
    bias = jnp.stack(
        [
            jnp.broadcast_to(
                jnp.where(
                    (half + (my_member - step) % half) * local_frames
                    + jnp.arange(local_frames, dtype=jnp.int32)
                    < length,
                    0.0,
                    MASKED,
                )[:, None],
                (local_frames, LANES),
            )
            for step in range(half)
        ]
    ).astype(F32)

    small_low = small_params.astype(LOW)
    extra = None
    if cut is not None:
        extra = jnp.pad(small_low.reshape(-1), (0, -small_low.size % (16 * width)))
        extra = extra.reshape(-1, width)
    wides = []
    for layer in range(layer_count):
        wides.append(gather(layer, extra if layer == 0 else None, []))
    if cut is None:
        params_all = lax.all_gather(small_low, ("fsdp", "seq"), axis=2, tiled=True)
    else:
        first_row = (wides[0].thin_at + 3) * block
        params_all = wides[0].chunk[:, first_row:].reshape(owners, -1)[:, : small_low.size]
        params_all = params_all.reshape((owners,) + small_low.shape).transpose(1, 2, 0, 3)
        params_all = params_all.reshape(layer_count, -1, width)
    params_all = params_all.astype(F32)

    row_steps = units if cut is None else deep
    hidden, upstream = to_clips([frames, cotangent])
    stored = []
    for layer_index in range(layer_count):
        params = params_all[layer_index]
        wide = wides[layer_index]
        hidden = share(wide, hidden)
        normed_low, queries, own = project(
            hidden, params, wide.chunk, wide.block, wide.thin_at, wide.given
        )
        others = [lax.ppermute(own, "seq", around(step)) for step in range(1, half)]
        mixed_out, log_total = attend(queries, own, others, bias, [])
        mixed_out = exchange(wide, 0, mixed_out)
        middle, second_low, active, slope = inner(hidden, mixed_out, params, wide, [])
        middle = exchange(wide, 1, middle)
        stored.append(
            (hidden, normed_low, queries, own, others, log_total, mixed_out)
            + (middle, second_low, active, slope)
        )
        if layer_index + 1 < layer_count:
            hidden = outer(middle, active, params, wide, row_steps, [])
    groups = 2 if width // LANES % 2 == 0 else 1
    def arrivals(number):
        return [
            part
            for layer in range(1, layer_count)
            for some in parts_out[layer][number : number + 1]
            for part in some[1]
        ]

    order = []
    waiting = None
    parts_out = {}
    done_in, done_out = (), ()
    rows_shape = (layer_count, units, block, width)
    states_in = (dense_in, first_in, second_in)
    states_out = (dense_out, first_out, second_out)
    if cut is None:
        states_out = [array.reshape(rows_shape) for array in states_out]
    rates_in = (RATE_DENSE, RATE_DENSE * math.sqrt(total_frames / 3.0), 3)
    rates_out = (RATE_OUTER, RATE_OUTER, 0)

    def flat(part):
        return [part[0]] + part[1]

    small_grads = []
    for layer_index in reversed(range(layer_count)):
        wide = wides[layer_index]
        params = params_all[layer_index]
        (
            hidden,
            normed_low,
            queries,
            own,
            others,
            log_total,
            mixed_out,
            middle,
            second_low,
            active,
            slope,
        ) = stored[layer_index]
        outer_low, inner_grad, bias_inner, bias_outer = outer_back(
            upstream, slope, wide, row_steps, order
        )
        order = [inner_grad]
        if waiting:
            waiting = start_far(waiting, order)
            order = order + waiting[1]
        wide_part = start_core(
            wide_weight_grad(
                cut, targets, second_low, inner_grad, active, outer_low, units, order
            )
        )
        middle_grad, branch_low, mixed_grad, sums_two = inner_back(
            inner_grad, upstream, middle, params, wide, wide_part[1]
        )
        order = [middle_grad]
        wide_part = start_far(wide_part, order)
        order = order + wide_part[1]
        q_terms, k_near, v_near, k_far, v_far = [], [], [], [], []
        for group in range(groups):
            q_term, k_terms, v_terms = attend_back(
                queries,
                own,
                others,
                mixed_out,
                mixed_grad,
                log_total,
                bias,
                group,
                groups,
                order,
            )
            q_terms.append(q_term)
            k_near.append(k_terms[0])
            v_near.append(v_terms[0])
            k_far.append(k_terms[1:])
            v_far.append(v_terms[1:])
            order = [q_term]
            if waiting and group == 0:
                waiting = whole_deep(waiting, order)
                order = order + waiting[1]

        def all_terms(near, terms):
            moved = [
                lax.ppermute(terms[group][step - 1], "seq", around(half - step))
                for step in range(1, half)
                for group in range(groups)
            ]
            return list(near) + moved

        terms = [q_terms, all_terms(k_near, k_far), all_terms(v_near, v_far)]
        order = [q_terms[-1]]

        if layer_index == 0:
            if waiting:
                waiting = start_reps(waiting)
                parts_out[1] += (waiting,)
            thin_part = start_core(
                thin_weight_grad(
                    cut, targets, normed_low, terms, mixed_out, branch_low, order
                )
            )
            wide_part = whole_deep(wide_part, thin_part[1] + arrivals(0))
            for layer in reversed(range(1, layer_count)):
                last = flat(parts_out[layer][0])
                done_out = adam(
                    states_out, last, layer, 0, units, units, rates_out, wide_part[1], done_out
                )
            thin_part = start_far(thin_part, list(done_out[:1]) + arrivals(1))
            order = thin_part[1]
        upstream, sums_one = project_back(
            hidden, middle_grad, params, terms, wide.chunk, wide.block, wide.thin_at, order
        )
        if layer_index > 0:
            if waiting:
                waiting = start_reps(waiting)
                parts_out[layer_index + 1] += (waiting,)
            wide_part = whole_deep(wide_part, [upstream])
            thin_part = start_core(
                thin_weight_grad(
                    cut,
                    targets,
                    normed_low,
                    terms,
                    mixed_out,
                    branch_low,
                    [upstream] + wide_part[1],
                )
            )
        waiting = thin_part
        order = waiting[1]
        parts_out[layer_index] = (start_reps(wide_part) if layer_index > 0 else wide_part,)
        small_grads = [sums_one, sums_two, bias_outer, bias_inner] + small_grads
    if cut is not None:
        keep, give = small_cut(cut, targets, small_grads, layer_count, [upstream])
        cuts = keep + lax.ppermute(give, "seq", over_core)
        along = [lax.ppermute(cuts[step], "seq", turn("seq", 2 * step)) for step in range(1, far)]

    middle, active = stored[-1][7], stored[-1][9]
    result = outer(middle, active, params_all[-1], wides[-1], row_steps, [upstream])
    for layer in reversed(range(1, layer_count)):
        last = flat(parts_out[layer][0])
        done_in = adam(states_in, last, layer, 4, units, 0, rates_in, [result], done_in)
    waiting = whole_deep(waiting, list(done_out[:1]) + list(done_in[:1]) + [result])
    order = waiting[1] or [upstream]
    ready = order + (along if cut else [])
    encoded = from_clips(*part_clips(in_lower.astype(jnp.int32).reshape(1), result, LOW, ready))
    for layer in reversed(range(1, layer_count)):
        last = flat(parts_out[layer][1])
        done_in = adam(states_in, last, layer, 0, 4, 0, rates_in, order, done_in)
    wide_part = parts_out[0][0]
    if cut is not None and done_in:
        mine, *done_in = lax.optimization_barrier((wide_part[0], *done_in))
        wide_part = (mine, wide_part[1])
    wide_part = start_reps(wide_part)
    ready = order + list(done_in[:1])
    frames_grad = from_clips(
        *part_clips(in_lower.astype(jnp.int32).reshape(1), upstream, F32, ready)
    )
    if cut is not None:
        total = sum(along, cuts[0])
        deeper = [
            lax.ppermute(
                lax.dynamic_index_in_dim(total, (depth + step) % deep, 0, keepdims=False),
                "fsdp",
                turn("fsdp", step),
            )
            for step in range(1, deep)
        ]
    done_in = adam(states_in, flat(wide_part), 0, 4, units, 0, rates_in, order, done_in)
    thin_part = start_reps(waiting)
    order = order + [done_in[0], thin_part[0]]
    done_out = adam(states_out, flat(wide_part), 0, 0, units, units, rates_out, order, done_out)
    if cut is None:
        small_all = jnp.stack(
            [
                jnp.concatenate([one[:4], two[2:3], two[:2], outer_sums])
                for one, two, outer_sums, _ in zip(*[iter(small_grads)] * 4)
            ]
        )
        inner_all = jnp.stack([part.reshape(units, width) for part in small_grads[3::4]])
        small_all = jnp.concatenate([small_all, inner_all], axis=1)
        small_all = small_all.reshape(layer_count, -1, owners, block).transpose(2, 0, 1, 3)
        owned_small = lax.psum_scatter(
            small_all, ("fsdp", "seq"), scatter_dimension=0, tiled=True
        )
    else:
        (total, *deeper, _) = lax.optimization_barrier((total, *deeper, done_in[0]))
        owned_small = lax.dynamic_index_in_dim(total, depth, 0, keepdims=False)
        owned_small = sum(deeper, owned_small)[:, :block]
    owned_small = owned_small.reshape(small_params.shape).astype(LOW)
    done_in = adam(states_in, flat(thin_part), 0, 0, 4, 0, rates_in, [done_out[0]], done_in)
    grad_in, moment_in, square_in, updated_in = done_in
    grad_out_rows, moment_out, square_out, updated_out = (
        array.reshape(dense_out.shape) for array in done_out
    )
    grad_small = finish(
        (owned_small, [lax.ppermute(owned_small, "rep", turn("rep", s)) for s in range(1, reps)])
    )
    moment_small, square_small, updated_small = adam_step(
        small_params, grad_small, first_small, second_small, RATE_SMALL
    )
    return (
        encoded,
        frames_grad,
        grad_in,
        grad_out_rows,
        grad_small,
        moment_in,
        moment_out,
        moment_small,
        square_in,
        square_out,
        square_small,
        updated_in,
        updated_out,
        updated_small,
    )


def solution(mesh):
    clips = P(("rep", "fsdp"), "seq", None)
    rows = P(None, ("fsdp", "seq"), None)
    lanes = P(None, None, ("fsdp", "seq"))
    return jax.shard_map(
        on_device,
        mesh=mesh,
        in_specs=(clips, P(("rep", "fsdp")), clips) + (rows, rows, lanes) * 3,
        out_specs=(clips, clips) + (rows, rows, lanes) * 4,
        check_vma=False,
    )
```

```python
import functools
import math

import jax
import jax.numpy as jnp
from jax import lax
from jax.experimental import pallas as pl
from jax.experimental.pallas import tpu as pltpu
from jax.sharding import PartitionSpec as P

HDIM = 64
STEP = 10

NORM_EPSILON = 1e-05
BETA_ONE = 0.9
BETA_TWO = 0.999
ADAM_EPSILON = 1e-08
DECAY_RATE = 0.01
RATE_DENSE = 0.1
RATE_OUTER = 0.05
RATE_SMALL = 0.5
INV_ROOT_TWO = 0.7071067811865476
INV_ROOT_TAU = 0.3989422804014327
LOGIT_SCALE = 0.125
MASKED = -1e30
LANES = 128
VMEM_LIMIT = 60 * 2**20

F32 = jnp.float32
LOW = jnp.bfloat16


def adam_step(weight, gradient, first, second, rate):
    moment = BETA_ONE * first + (1.0 - BETA_ONE) * gradient
    square = BETA_TWO * second + (1.0 - BETA_TWO) * gradient * gradient
    moment_hat = moment / (1.0 - BETA_ONE**STEP)
    square_hat = square / (1.0 - BETA_TWO**STEP)
    updated = weight - rate * (
        moment_hat / (jnp.sqrt(square_hat) + ADAM_EPSILON) + DECAY_RATE * weight
    )
    return (moment, square, updated)


def product(left_side, right_side):
    return jnp.dot(left_side, right_side, preferred_element_type=F32)


def back_product(left_side, right_side):
    return lax.dot_general(
        left_side, right_side, (((1,), (1,)), ((), ())), preferred_element_type=F32
    )


def outer_sum(left_side, right_side):
    return lax.dot_general(
        left_side, right_side, (((0,), (0,)), ((), ())), preferred_element_type=F32
    )


def normalise(values_in):
    centred = values_in - jnp.mean(values_in, axis=-1, keepdims=True)
    scale_inv = lax.rsqrt(jnp.mean(centred * centred, axis=-1, keepdims=True) + NORM_EPSILON)
    return centred * scale_inv, scale_inv


def norm_backward(upstream, gain_row, normal, scale_inv):
    scaled = upstream * gain_row
    inside = (
        scaled
        - jnp.mean(scaled, axis=-1, keepdims=True)
        - normal * jnp.mean(scaled * normal, axis=-1, keepdims=True)
    )
    return (
        scale_inv * inside,
        jnp.sum(upstream * normal, axis=0, keepdims=True),
        jnp.sum(upstream, axis=0, keepdims=True),
    )


def run(kernel, name, steps, ins, outs, scratch, flops, after=(), scalar=None, reuse=()):
    in_arrays, in_specs = zip(*ins)
    out_shapes, out_specs = zip(*outs)
    moved = sum(a.size * a.dtype.itemsize for a in in_arrays)
    moved += sum(math.prod(s.shape) * s.dtype.itemsize for s in out_shapes)
    lead = 0 if scalar is None else 1

    spare = [*after, *reuse]
    aliases = {lead + len(ins) + len(after) + number: number for number in range(len(reuse))}

    def body(*refs):
        kernel(*refs[: lead + len(ins)], *refs[lead + len(ins) + len(spare) :])

    grid_spec = pltpu.PrefetchScalarGridSpec(
        num_scalar_prefetch=lead,
        grid=(steps,),
        in_specs=list(in_specs) + [pl.BlockSpec(memory_space=pl.ANY)] * len(spare),
        out_specs=list(out_specs),
        scratch_shapes=scratch,
    )
    return pl.pallas_call(
        body,
        grid_spec=grid_spec,
        out_shape=list(out_shapes),
        input_output_aliases=aliases,
        compiler_params=pltpu.CompilerParams(vmem_limit_bytes=VMEM_LIMIT),
        cost_estimate=pl.CostEstimate(flops=flops, bytes_accessed=moved, transcendentals=0),
        name=name,
    )(*(() if scalar is None else (scalar,)), *in_arrays, *spare)


def full(shape):
    return pl.BlockSpec(shape, lambda step, *_: (0,) * len(shape))


def scalars():
    return pl.BlockSpec(memory_space=pltpu.SMEM)


def unit_spec(chunk, block, unit_of):
    owners, _, width = chunk.shape
    return chunk, pl.BlockSpec((owners, block, width), lambda step, *_: (0, unit_of(step), 0))


def unit_of_ref(ref):
    return ref[...].reshape(-1, ref.shape[-1])


class Wide:
    def __init__(self, chunk, sent, info, block, units):
        self.chunk, self.sent, self.info = chunk, sent, info
        self.block, self.units = block, units
        self.held = units // 2 if sent else units
        self.mix_at = 2 * self.held
        self.thin_at = self.mix_at + 1

    def mix_spec(self):
        return unit_spec(self.chunk, self.block, lambda step: self.mix_at)

    def inner_specs(self, unit_of):
        arrays = (self.chunk, *self.sent[0]) if self.sent else (self.chunk,)
        return [
            unit_spec(array, self.block, lambda step: lax.rem(unit_of(step), self.held))
            for array in arrays
        ]

    def inner_scratch(self):
        owners, _, width = self.chunk.shape
        return [pltpu.VMEM((owners, self.block, width), LOW)] if self.sent else []

    def outer_specs(self, steps):
        owners, _, width = self.chunk.shape
        if owners == 1:
            return [unit_spec(self.chunk, self.block, lambda step: self.units + step)]
        shape = (owners // steps, self.held * self.block, width)
        specs = [(self.chunk, pl.BlockSpec(shape, lambda step, *_: (step, 1, 0)))]
        if self.sent:
            near = pl.BlockSpec(shape, lambda step, *_: (lax.rem(step, steps // 2), 0, 0))
            specs += [(array, near) for array in self.sent[1]]
        return specs

    def outer_scratch(self, steps):
        owners, _, width = self.chunk.shape
        shape = (owners // steps, self.units * self.block, width)
        return [pltpu.VMEM(shape, LOW)] if self.sent else []

    def count(self):
        return 3 if self.sent else 1


def inner_unit(info_ref, refs, held, half):
    if len(refs) == 1:
        return unit_of_ref(refs[0])
    mine_ref, near_ref, far_ref = refs
    count = near_ref.shape[0]

    @pl.when(info_ref[0] == half)
    def _():
        held[...] = mine_ref[...]

    for core in range(2):

        @pl.when((info_ref[0] != half) & (info_ref[1] == core))
        def _():
            held[core * count : (core + 1) * count] = near_ref[...]
            held[(1 - core) * count : (2 - core) * count] = far_ref[...]

    return unit_of_ref(held)


def outer_unit(info_ref, refs, held, step, steps):
    if len(refs) == 1:
        return unit_of_ref(refs[0])
    mine_ref, near_ref, far_ref = refs
    count = mine_ref.shape[1]
    is_near = step // (steps // 2) == info_ref[1]
    for rep in range(2):

        @pl.when(info_ref[0] == rep)
        def _():
            held[:, rep * count : (rep + 1) * count] = mine_ref[...]

        for ref, wanted in ((near_ref, is_near), (far_ref, jnp.logical_not(is_near))):

            @pl.when((info_ref[0] == rep) & wanted)
            def _():
                held[:, (1 - rep) * count : (2 - rep) * count] = ref[...]

    return unit_of_ref(held)


def project_kernel(hidden_ref, params_ref, unit_ref, normed_ref, q_ref, kv_ref):
    step = pl.program_id(0)

    @pl.when(step == 0)
    def _():
        normal, _ = normalise(hidden_ref[...])
        normed_ref[...] = (normal * params_ref[0:1] + params_ref[1:2]).astype(LOW)

    weights = unit_of_ref(unit_ref)
    added = jnp.where(step == 0, params_ref[2:3], params_ref[3:4])
    added = jnp.where(step == 1, jnp.zeros_like(added), added)
    result = (product(normed_ref[...], weights) + added).astype(LOW)

    @pl.when(step == 0)
    def _():
        q_ref[...] = result

    @pl.when(step > 0)
    def _():
        kv_ref[...] = result


def project(hidden, params, chunk, block, first, after):
    rows, width = hidden.shape
    return run(
        project_kernel,
        "project",
        3,
        [
            (hidden, full(hidden.shape)),
            (params, full(params.shape)),
            unit_spec(chunk, block, lambda step: first + step),
        ],
        [
            (jax.ShapeDtypeStruct((rows, width), LOW), full((rows, width))),
            (jax.ShapeDtypeStruct((rows, width), LOW), full((rows, width))),
            (
                jax.ShapeDtypeStruct((rows, 2 * width), LOW),
                pl.BlockSpec((rows, width), lambda step, *_: (0, jnp.maximum(step - 1, 0))),
            ),
        ],
        [],
        6 * rows * width * width,
        after,
    )


def inner_kernel(count, per_half, info_ref, hidden_ref, mixed_ref, params_ref, mix_ref, *refs):
    unit_refs, refs = refs[:count], refs[count:]
    middle_ref, second_ref, active_ref, slope_ref, *held = refs
    step = pl.program_id(0)

    @pl.when(step == 0)
    def _():
        middle = hidden_ref[...] + (product(mixed_ref[...], unit_of_ref(mix_ref)) + params_ref[4:5])
        middle_ref[...] = middle
        normal, _ = normalise(middle)
        second_ref[...] = (normal * params_ref[5:6] + params_ref[6:7]).astype(LOW)

    @pl.when(step > 0)
    def _():
        weights = inner_unit(info_ref, unit_refs, held[0] if held else None, (step - 1) // per_half)
        inner = product(second_ref[...], weights) + params_ref[pl.ds(step + 7, 1), :]
        cumulative = 0.5 * (1.0 + lax.erf(inner * INV_ROOT_TWO))
        active_ref[...] = (inner * cumulative).astype(LOW)
        slope = cumulative + inner * jnp.exp(-0.5 * inner * inner) * INV_ROOT_TAU
        slope_ref[...] = slope.astype(LOW)


def inner(hidden, mixed_out, params, wide, after):
    units = wide.units
    rows, width = hidden.shape
    spread = pl.BlockSpec((rows, width), lambda step, *_: (0, jnp.maximum(step - 1, 0)))
    return run(
        functools.partial(inner_kernel, wide.count(), max(units // 2, 1)),
        "inner",
        units + 1,
        [
            (wide.info, scalars()),
            (hidden, full(hidden.shape)),
            (mixed_out, full(mixed_out.shape)),
            (params, full(params.shape)),
            wide.mix_spec(),
        ]
        + wide.inner_specs(lambda step: jnp.maximum(step - 1, 0)),
        [
            (jax.ShapeDtypeStruct((rows, width), F32), full((rows, width))),
            (jax.ShapeDtypeStruct((rows, width), LOW), full((rows, width))),
            (jax.ShapeDtypeStruct((rows, units * width), LOW), spread),
            (jax.ShapeDtypeStruct((rows, units * width), LOW), spread),
        ],
        wide.inner_scratch(),
        2 * (units + 1) * rows * width * width,
        after,
    )


def outer_kernel(count, steps, info_ref, middle_ref, active_ref, params_ref, *refs):
    unit_refs, (out_ref, *held) = refs[:count], refs[count:]
    weights = outer_unit(
        info_ref, unit_refs, held[0] if held else None, pl.program_id(0), steps
    )
    term = product(active_ref[...], weights)

    @pl.when(pl.program_id(0) == 0)
    def _():
        out_ref[...] = middle_ref[...] + (term + params_ref[7:8])

    @pl.when(pl.program_id(0) > 0)
    def _():
        out_ref[...] += term


def outer(middle, active, params, wide, steps, after):
    units = wide.units
    rows, width = middle.shape
    return run(
        functools.partial(outer_kernel, wide.count(), steps),
        "outer",
        steps,
        [
            (wide.info, scalars()),
            (middle, full(middle.shape)),
            (active, pl.BlockSpec((rows, units * width // steps), lambda step, *_: (0, step))),
            (params, full(params.shape)),
        ]
        + wide.outer_specs(steps),
        [(jax.ShapeDtypeStruct((rows, width), F32), full((rows, width)))],
        wide.outer_scratch(steps),
        2 * units * rows * width * width,
        after,
    )[0]


def outer_back_kernel(count, steps, info_ref, upstream_ref, slope_ref, *refs):
    unit_refs, refs = refs[:count], refs[count:]
    low_ref, inner_ref, bias_inner_ref, bias_outer_ref, *held = refs
    weights = outer_unit(
        info_ref, unit_refs, held[0] if held else None, pl.program_id(0), steps
    )

    @pl.when(pl.program_id(0) == 0)
    def _():
        low = upstream_ref[...].astype(LOW)
        low_ref[...] = low
        bias_outer_ref[...] = jnp.sum(low.astype(F32), axis=0, keepdims=True)

    grad = (back_product(low_ref[...], weights) * slope_ref[...].astype(F32)).astype(LOW)
    inner_ref[...] = grad
    bias_inner_ref[...] = jnp.sum(grad.astype(F32), axis=0, keepdims=True)


def outer_back(upstream, slope, wide, steps, after):
    units = wide.units
    rows, width = upstream.shape
    share = units * width // steps
    return run(
        functools.partial(outer_back_kernel, wide.count(), steps),
        "outer_back",
        steps,
        [
            (wide.info, scalars()),
            (upstream, full(upstream.shape)),
            (slope, pl.BlockSpec((rows, share), lambda step, *_: (0, step))),
        ]
        + wide.outer_specs(steps),
        [
            (jax.ShapeDtypeStruct((rows, width), LOW), full((rows, width))),
            (
                jax.ShapeDtypeStruct((rows, units * width), LOW),
                pl.BlockSpec((rows, share), lambda step, *_: (0, step)),
            ),
            (
                jax.ShapeDtypeStruct((1, units * width), F32),
                pl.BlockSpec((1, share), lambda step, *_: (0, step)),
            ),
            (jax.ShapeDtypeStruct((1, width), F32), full((1, width))),
        ],
        wide.outer_scratch(steps),
        2 * units * rows * width * width,
        after,
    )


def inner_back_kernel(
    count, units, info_ref, inner_ref, upstream_ref, middle_ref, params_ref, mix_ref, *refs
):
    unit_refs, refs = refs[:count], refs[count:]
    middle_grad_ref, low_ref, mixed_grad_ref, sums_ref, total, *held = refs
    step = pl.program_id(0)

    @pl.when(step == 0)
    def _():
        total[...] = jnp.zeros_like(total)

    @pl.when(step < units)
    def _():
        weights = inner_unit(
            info_ref, unit_refs, held[0] if held else None, step // max(units // 2, 1)
        )
        total[...] += back_product(inner_ref[...], weights)

    @pl.when(step == units)
    def _():
        normal, scale_inv = normalise(middle_ref[...])
        lifted, gain, shift = norm_backward(total[...], params_ref[5:6], normal, scale_inv)
        middle_grad = upstream_ref[...] + lifted
        middle_grad_ref[...] = middle_grad
        low = middle_grad.astype(LOW)
        low_ref[...] = low
        sums_ref[0:1] = gain
        sums_ref[1:2] = shift
        sums_ref[2:3] = jnp.sum(low.astype(F32), axis=0, keepdims=True)
        sums_ref[3:8] = jnp.zeros((5, sums_ref.shape[1]), F32)
        mixed_grad_ref[...] = back_product(low, unit_of_ref(mix_ref)).astype(LOW)


def inner_back(inner_grad, upstream, middle, params, wide, after):
    units = wide.units
    rows, width = upstream.shape
    return run(
        functools.partial(inner_back_kernel, wide.count(), units),
        "inner_back",
        units + 1,
        [
            (wide.info, scalars()),
            (
                inner_grad,
                pl.BlockSpec((rows, width), lambda step, *_: (0, jnp.minimum(step, units - 1))),
            ),
            (upstream, full(upstream.shape)),
            (middle, full(middle.shape)),
            (params, full(params.shape)),
            wide.mix_spec(),
        ]
        + wide.inner_specs(lambda step: jnp.minimum(step, units - 1)),
        [
            (jax.ShapeDtypeStruct((rows, width), F32), full((rows, width))),
            (jax.ShapeDtypeStruct((rows, width), LOW), full((rows, width))),
            (jax.ShapeDtypeStruct((rows, width), LOW), full((rows, width))),
            (jax.ShapeDtypeStruct((8, width), F32), full((8, width))),
        ],
        [pltpu.VMEM((rows, width), F32)] + wide.inner_scratch(),
        2 * (units + 1) * rows * width * width,
        after,
    )


def joined(terms, groups):
    columns = []
    for group in range(groups):
        term = terms[group][...]
        if len(terms) > groups:
            others = terms[groups + group :: groups]
            term = sum([other[...].astype(F32) for other in others], term.astype(F32))
        columns.append(term.astype(LOW))
    return jnp.concatenate(columns, axis=1)


def split_terms(refs, counts):
    groups, parts = counts
    ends = (groups, groups * (parts + 1), groups * (2 * parts + 1))
    return [refs[: ends[0]], refs[ends[0] : ends[1]], refs[ends[1] : ends[2]]], refs[ends[2] :]


def project_back_kernel(counts, hidden_ref, middle_grad_ref, params_ref, *refs):
    terms, (unit_ref, out_ref, sums_ref, total) = split_terms(refs, counts)
    step = pl.program_id(0)
    weights = unit_of_ref(unit_ref)

    @pl.when(step == 0)
    def _():
        grad = joined(terms[0], counts[0])
        sums_ref[2:3] = jnp.sum(grad.astype(F32), axis=0, keepdims=True)
        total[...] = back_product(grad, weights)

    @pl.when(step == 1)
    def _():
        total[...] += back_product(joined(terms[1], counts[0]), weights)

    @pl.when(step == 2)
    def _():
        grad = joined(terms[2], counts[0])
        sums_ref[3:4] = jnp.sum(grad.astype(F32), axis=0, keepdims=True)
        first_grad = total[...] + back_product(grad, weights)
        normal, scale_inv = normalise(hidden_ref[...])
        lowered, gain, shift = norm_backward(first_grad, params_ref[0:1], normal, scale_inv)
        out_ref[...] = middle_grad_ref[...] + lowered
        sums_ref[0:1] = gain
        sums_ref[1:2] = shift
        sums_ref[4:8] = jnp.zeros((4, sums_ref.shape[1]), F32)


def project_back(hidden, middle_grad, params, terms, chunk, block, first, after):
    rows, width = hidden.shape
    whole = full((rows, width))
    counts = (len(terms[0]), len(terms[1]) // len(terms[0]))
    return run(
        functools.partial(project_back_kernel, counts),
        "project_back",
        3,
        [
            (hidden, whole),
            (middle_grad, whole),
            (params, full(params.shape)),
        ]
        + [(term, full(term.shape)) for some in terms for term in some]
        + [unit_spec(chunk, block, lambda step: first + step)],
        [
            (jax.ShapeDtypeStruct((rows, width), F32), whole),
            (jax.ShapeDtypeStruct((8, width), F32), full((8, width))),
        ],
        [pltpu.VMEM((rows, width), F32)],
        6 * rows * width * width,
        after,
    )


def grad_out(cut, units, width):
    if cut is None:
        shape, scratch = (units, width, width), []
        outs = [
            (
                jax.ShapeDtypeStruct(shape, LOW),
                pl.BlockSpec((1, width, width), lambda step, *_: (step, 0, 0)),
            )
        ]
    else:
        far, deep, block = cut
        shape = (far, deep, units, block, width)
        outs = [(jax.ShapeDtypeStruct(shape, LOW), full(shape))] * 2
        scratch = [pltpu.VMEM((deep, 2 * far, block, width), LOW)]
    return outs, scratch


def split_unit(targets_ref, result, refs, unit):
    if len(refs) == 1:
        refs[0][0] = result.astype(LOW)
        return
    keep_ref, give_ref, held = refs
    held[...] = result.astype(LOW).reshape(held.shape)
    far = keep_ref.shape[0]
    for near in range(far):
        keep_ref[near, :, unit] = held[:, targets_ref[near]]
        give_ref[near, :, unit] = held[:, targets_ref[far + near]]


def wide_grad_kernel(units, targets_ref, second_ref, inner_ref, active_ref, low_ref, *refs):
    step = pl.program_id(0)

    @pl.when(step < units)
    def _():
        split_unit(targets_ref, outer_sum(second_ref[...], inner_ref[...]), refs[:3], step)

    @pl.when(step >= units)
    def _():
        result = outer_sum(active_ref[...], low_ref[...])
        if len(refs) == 1:
            refs[0][0] = result.astype(LOW)
        else:
            keep_ref, give_ref, _, held = refs
            held[...] = result.astype(LOW).reshape(held.shape)
            far = keep_ref.shape[0]
            for near in range(far):
                keep_ref[near, step - units] = held[targets_ref[near]]
                give_ref[near, step - units] = held[targets_ref[far + near]]


def wide_weight_grad(cut, targets, second_low, inner_grad, active, outer_low, units, after):
    rows, width = second_low.shape
    outs, scratch = grad_out(cut, 2 * units, width)
    steps = units
    if cut is not None:
        far, steps, block = cut
        shape = (far, steps, 2 * units, block, width)
        spec = pl.BlockSpec(
            (far, steps, units, block, width),
            lambda step, *_: (0, 0, jnp.where(step < units, 0, 1), 0, 0),
        )
        outs = [(jax.ShapeDtypeStruct(shape, LOW), spec)] * 2
        scratch = scratch + [pltpu.VMEM((2 * far, units, block, width), LOW)]
    share = units * width // steps
    return run(
        functools.partial(wide_grad_kernel, units),
        "wide_weight_grad",
        units + steps,
        [
            (targets, scalars()),
            (second_low, full((rows, width))),
            (
                inner_grad,
                pl.BlockSpec((rows, width), lambda step, *_: (0, jnp.minimum(step, units - 1))),
            ),
            (
                active,
                pl.BlockSpec((rows, share), lambda step, *_: (0, jnp.maximum(step - units, 0))),
            ),
            (outer_low, full((rows, width))),
        ],
        outs,
        scratch,
        4 * units * rows * width * width,
        after,
    )


def thin_grad_kernel(counts, targets_ref, normed_ref, mixed_ref, low_ref, *refs):
    terms, refs = split_terms(refs, counts)
    step = pl.program_id(0)
    for number in range(3):

        @pl.when(step == number)
        def _():
            grad = joined(terms[number], counts[0])
            split_unit(targets_ref, outer_sum(normed_ref[...], grad), refs, step)

    @pl.when(step == 3)
    def _():
        split_unit(targets_ref, outer_sum(mixed_ref[...], low_ref[...]), refs, step)


def thin_weight_grad(cut, targets, normed_low, terms, mixed_out, branch_low, after):
    rows, width = normed_low.shape
    outs, scratch = grad_out(cut, 4, width)
    whole = full((rows, width))
    counts = (len(terms[0]), len(terms[1]) // len(terms[0]))
    return run(
        functools.partial(thin_grad_kernel, counts),
        "thin_weight_grad",
        4,
        [
            (targets, scalars()),
            (normed_low, whole),
            (mixed_out, whole),
            (branch_low, whole),
        ]
        + [(term, full(term.shape)) for some in terms for term in some],
        outs,
        scratch,
        8 * rows * width * width,
        after,
    )


def sum_along_kernel(keep_ref, taken_ref, out_ref):
    out_ref[...] = keep_ref[0] + taken_ref[0]


def sum_along(keep, taken, step_far, after):
    _, deep, units, block, width = keep.shape
    spec = pl.BlockSpec(
        (1, 1, units, block, width), lambda step, *_: (step_far, step, 0, 0, 0)
    )
    return run(
        sum_along_kernel,
        "sum_along",
        deep,
        [(keep, spec), (taken, spec)],
        [
            (
                jax.ShapeDtypeStruct((deep, units, block, width), LOW),
                pl.BlockSpec((1, units, block, width), lambda step, *_: (step, 0, 0, 0)),
            )
        ],
        [],
        2 * units * deep * block * width,
        after,
    )[0]


def sum_near_kernel(keep_ref, taken_ref, *refs):
    along, out_ref = refs[:-1], refs[-1]
    total = keep_ref[0].astype(F32) + taken_ref[0].astype(F32)
    for ref in along:
        total += ref[...].astype(F32)
    out_ref[...] = total.astype(LOW)


def sum_near(keep, taken, along, after):
    _, deep, units, block, width = keep.shape
    near = pl.BlockSpec((1, 1, units, block, width), lambda step, *_: (0, step, 0, 0, 0))
    spec = pl.BlockSpec((1, units, block, width), lambda step, *_: (step, 0, 0, 0))
    return run(
        sum_near_kernel,
        "sum_near",
        deep,
        [(keep, near), (taken, near)] + [(array, spec) for array in along],
        [(jax.ShapeDtypeStruct((deep, units, block, width), LOW), spec)],
        [],
        3 * units * deep * block * width,
        after,
    )[0]


def pack_kernel(units, halves, rep_ref, in_ref, rows_ref, *refs):
    out_ref = refs[-1]
    block, width = in_ref.shape[1], out_ref.shape[1]
    count = units // halves

    def column(unit):
        return in_ref[0, :, unit * width : (unit + 1) * width].astype(LOW)

    for half in range(halves):

        @pl.when((rep_ref[0] == half) | (halves == 1))
        def _():
            for unit in range(count):
                out_ref[unit * block : (unit + 1) * block] = column(4 + half * count + unit)
            rows = rows_ref[0, half * count * block : (half + 1) * count * block]
            out_ref[count * block : 2 * count * block] = rows.astype(LOW)

    for number, unit in enumerate((3, 0, 1, 2)):
        at = (2 * count + number) * block
        out_ref[at : at + block] = column(unit)
    if len(refs) > 1:
        out_ref[(2 * count + 4) * block :] = refs[0][...]


def pack(dense_in, dense_out, layer, units, halves, rep, extra, after):
    _, block, columns = dense_in.shape
    width = dense_out.shape[2]
    rows = (2 * units // halves + 4) * block
    ins = [
        (rep, scalars()),
        (dense_in, pl.BlockSpec((1, block, columns), lambda step, *_: (layer, 0, 0))),
        (
            dense_out,
            pl.BlockSpec((1,) + dense_out.shape[1:], lambda step, *_: (layer, 0, 0)),
        ),
    ]
    if extra is not None:
        ins.append((extra, full(extra.shape)))
        rows += extra.shape[0]
    return run(
        functools.partial(pack_kernel, units, halves),
        "pack",
        1,
        ins,
        [(jax.ShapeDtypeStruct((rows, width), LOW), full((rows, width)))],
        [],
        rows * width,
        after,
    )[0]


def small_cut_kernel(layers, block, targets_ref, *refs):
    keep_ref, give_ref, held = refs[-3:]
    _, deep, rows, _ = keep_ref.shape
    each = rows // layers
    keep_ref[...] = jnp.zeros_like(keep_ref)
    give_ref[...] = jnp.zeros_like(give_ref)
    for layer in range(layers):
        one, two, outer_sums, inner_sums = (ref[...] for ref in refs[4 * layer : 4 * layer + 4])
        width = one.shape[1]
        at = layer * each
        held[at : at + 4] = one[:4]
        held[at + 4 : at + 5] = two[2:3]
        held[at + 5 : at + 7] = two[:2]
        held[at + 7 : at + 8] = outer_sums
        for unit in range(each - 8):
            held[at + 8 + unit : at + 9 + unit] = inner_sums[:, unit * width : (unit + 1) * width]
    far = keep_ref.shape[0]
    for depth in range(deep):
        for near in range(far):
            for place in range(2 * far):
                start = (depth * 2 * far + place) * block

                @pl.when(targets_ref[near] == place)
                def _():
                    keep_ref[near, depth, :, :block] = held[:, start : start + block]

                @pl.when(targets_ref[far + near] == place)
                def _():
                    give_ref[near, depth, :, :block] = held[:, start : start + block]


def small_cut(cut, targets, parts, layers, after):
    far, deep, block = cut
    width = parts[0].shape[1]
    rows = layers * (8 + parts[3].shape[1] // width)
    shape = (far, deep, rows, LANES)
    return run(
        functools.partial(small_cut_kernel, layers, block),
        "small_cut",
        1,
        [(targets, scalars())] + [(part, full(part.shape)) for part in parts],
        [(jax.ShapeDtypeStruct(shape, F32), full(shape))] * 2,
        [pltpu.VMEM((rows, width), F32)],
        rows * width,
        after,
    )


def adam_kernel(usual, special, chosen, weight_ref, first_ref, second_ref, *refs):
    grads, (grad_ref, moment_ref, square_ref, updated_ref) = refs[:-4], refs[-4:]
    grad = sum([ref[0].astype(F32) for ref in grads[1:]], grads[0][0].astype(F32))
    grad = grad.reshape(weight_ref.shape)
    rate = jnp.where(pl.program_id(0) == chosen, special, usual)
    moment, square, updated = adam_step(weight_ref[...], grad, first_ref[...], second_ref[...], rate)
    grad_ref[...] = grad
    moment_ref[...] = moment
    square_ref[...] = square
    updated_ref[...] = updated


def adam(state, grads, layer, first, count, from_unit, rates, after, reuse):
    weight = state[0]
    block, width = grads[0].shape[1:]
    if weight.ndim == 3 and weight.shape[2] == width:
        spec = pl.BlockSpec((1, block, width), lambda step, *_: (layer, first + step, 0))
    elif weight.ndim == 3:
        spec = pl.BlockSpec((1, block, width), lambda step, *_: (layer, 0, first + step))
    else:
        spec = pl.BlockSpec((1, 1, block, width), lambda step, *_: (layer, first + step, 0, 0))
    usual, special, chosen = rates
    return run(
        functools.partial(adam_kernel, usual, special, chosen - first),
        "adam",
        count,
        [(array, spec) for array in state]
        + [
            (grad, pl.BlockSpec((1, block, width), lambda step, *_: (from_unit + step, 0, 0)))
            for grad in grads
        ],
        [(jax.ShapeDtypeStruct(weight.shape, F32), spec)] * 4,
        [],
        16 * count * block * width,
        after,
        None,
        reuse,
    )


def part_kernel(lower_ref, rows_ref, keep_ref, give_ref):
    count = keep_ref.shape[0]
    lower, upper = rows_ref[:count], rows_ref[count:]
    in_lower = lower_ref[0] != 0
    keep_ref[...] = jnp.where(in_lower, lower, upper).astype(keep_ref.dtype)
    give_ref[...] = jnp.where(in_lower, upper, lower).astype(LOW)


def part_clips(in_lower, rows, kind, after):
    count, width = rows.shape[0] // 2, rows.shape[1]
    return run(
        part_kernel,
        "part_clips",
        1,
        [(in_lower, scalars()), (rows, full(rows.shape))],
        [
            (jax.ShapeDtypeStruct((count, width), kind), full((count, width))),
            (jax.ShapeDtypeStruct((count, width), LOW), full((count, width))),
        ],
        [],
        rows.size,
        after,
    )


def query_block(rows):
    return next(size for size in (768, 384, 256, 128) if rows % size == 0)


def attend_kernel(parts, block, bias_ref, q_ref, *refs):
    k_refs, v_refs = refs[:parts], refs[parts : 2 * parts]
    o_ref, lse_ref = refs[2 * parts :]
    rows = q_ref.shape[0]
    q_side = (q_ref[...] * jnp.bfloat16(LOGIT_SCALE)).T
    ones = jnp.ones((16, rows), LOW)
    v_heads = []
    for ref in v_refs:
        side = ref[...].T
        v_heads.append(
            [jnp.concatenate([side[h * HDIM : (h + 1) * HDIM], ones]) for h in range(2)]
        )
    head_of = lax.broadcasted_iota(jnp.int32, (LANES, block), 0) // HDIM
    for start in range(0, rows, block):
        q_block = q_side[:, start : start + block]
        both = []
        for head in range(2):
            q_head = jnp.where(head_of == head, q_block, jnp.zeros_like(q_block))
            scores = []
            for part in range(parts):
                score = product(k_refs[part][...], q_head)
                lower, upper = score[: rows // 2], score[rows // 2 :]
                bias = jnp.tile(bias_ref[part], (1, block // LANES))
                scores.append(jnp.concatenate([lower, upper + bias], axis=0))
            top = functools.reduce(
                jnp.maximum, [jnp.max(score, axis=0, keepdims=True) for score in scores]
            )
            weights = [jnp.exp(score - top).astype(LOW) for score in scores]
            summed = sum(product(v_heads[part][head], weights[part]) for part in range(parts))
            total = summed[HDIM : HDIM + 1]
            both.append(summed[:HDIM] / total)
            lse_ref[0, head : head + 1, start : start + block] = top + jnp.log(total)
        o_ref[start : start + block, :] = jnp.concatenate(both, axis=0).T.astype(LOW)


def attend(queries, own, others, bias, after):
    rows, width = queries.shape
    pairs = width // LANES
    parts = len(others) + 1

    def columns(base):
        return pl.BlockSpec((rows, LANES), lambda pair, *_: (0, base * pairs + pair))

    return run(
        functools.partial(attend_kernel, parts, query_block(rows)),
        "attend",
        pairs,
        [(bias, full(bias.shape)), (queries, columns(0))]
        + [(array, columns(0)) for array in (own, *others)]
        + [(array, columns(1)) for array in (own, *others)],
        [
            (jax.ShapeDtypeStruct((rows, width), LOW), columns(0)),
            (
                jax.ShapeDtypeStruct((pairs, 2, rows), F32),
                pl.BlockSpec((1, 2, rows), lambda pair, *_: (pair, 0, 0)),
            ),
        ],
        [],
        16 * rows * rows * parts * width,
        after,
    )


def attend_back_kernel(parts, block, bias_ref, q_ref, *refs):
    k_refs, v_refs = refs[:parts], refs[parts : 2 * parts]
    o_ref, do_ref, lse_ref = refs[2 * parts : 2 * parts + 3]
    dq_ref = refs[2 * parts + 3]
    dk_refs = refs[2 * parts + 4 : 3 * parts + 4]
    dv_refs = refs[3 * parts + 4 :]
    rows = q_ref.shape[0]
    q_rows = q_ref[...] * jnp.bfloat16(LOGIT_SCALE)
    do_rows = do_ref[...]
    q_side, do_side = q_rows.T, do_rows.T
    shared = (do_rows.astype(F32) * o_ref[...].astype(F32)).T
    delta = [
        jnp.sum(shared[head * HDIM : (head + 1) * HDIM], axis=0, keepdims=True)
        for head in range(2)
    ]
    head_of = lax.broadcasted_iota(jnp.int32, (LANES, rows), 0) // HDIM
    zeros = jnp.zeros_like(q_side)
    q_heads = [jnp.where(head_of == head, q_side, zeros) for head in range(2)]
    do_heads = [jnp.where(head_of == head, do_side, zeros) for head in range(2)]
    lane = lax.broadcasted_iota(jnp.int32, (block, LANES), 1)
    dq_sides = [jnp.zeros((HDIM, rows), F32)] * 2
    for part in range(parts):
        for start in range(0, rows, block):
            here = slice(start, start + block)
            k_block, v_block = k_refs[part][here], v_refs[part][here]
            k_side = k_block.T
            dk_heads, dv_heads = [], []
            for head in range(2):
                score = product(k_block, q_heads[head])
                if start + block > rows // 2:
                    skip = max(rows // 2 - start, 0)
                    upper = bias_ref[part][start + skip - rows // 2 : start + block - rows // 2]
                    raised = score[skip:] + jnp.tile(upper, (1, rows // LANES))
                    score = jnp.concatenate([score[:skip], raised], axis=0) if skip else raised
                chances = jnp.exp(score - lse_ref[0, head : head + 1])
                chance_grad = product(v_block, do_heads[head])
                score_grad = (chances * (chance_grad - delta[head])).astype(LOW)
                dq_sides[head] = dq_sides[head] + product(
                    k_side[head * HDIM : (head + 1) * HDIM], score_grad
                )
                dk_heads.append(product(score_grad, q_rows))
                dv_heads.append(product(chances.astype(LOW), do_rows))
            dk_refs[part][here] = jnp.where(lane < HDIM, *dk_heads).astype(LOW)
            dv_refs[part][here] = jnp.where(lane < HDIM, *dv_heads).astype(LOW)
    dq_ref[...] = (jnp.concatenate(dq_sides, axis=0) * LOGIT_SCALE).T.astype(LOW)


def attend_back(queries, own, others, mixed_out, mixed_grad, log_total, bias, group, groups, after):
    rows, width = queries.shape
    pairs = width // LANES
    parts = len(others) + 1
    first = group * pairs // groups
    count = (group + 1) * pairs // groups - first

    def columns(base):
        return pl.BlockSpec((rows, LANES), lambda pair, *_: (0, base * pairs + first + pair))

    out = run(
        functools.partial(attend_back_kernel, parts, query_block(rows)),
        "attend_back",
        count,
        [(bias, full(bias.shape)), (queries, columns(0))]
        + [(array, columns(0)) for array in (own, *others)]
        + [(array, columns(1)) for array in (own, *others)]
        + [
            (mixed_out, columns(0)),
            (mixed_grad, columns(0)),
            (log_total, pl.BlockSpec((1, 2, rows), lambda pair, *_: (first + pair, 0, 0))),
        ],
        [
            (
                jax.ShapeDtypeStruct((rows, count * LANES), LOW),
                pl.BlockSpec((rows, LANES), lambda pair, *_: (0, pair)),
            )
        ]
        * (2 * parts + 1),
        [],
        40 * rows * rows * parts * count * LANES,
        after,
    )
    return out[0], out[1 : parts + 1], out[parts + 1 :]


def on_device(
    frames,
    lengths,
    cotangent,
    dense_in,
    dense_out,
    small_params,
    first_in,
    first_out,
    first_small,
    second_in,
    second_out,
    second_small,
):
    clip_count, local_frames, width = frames.shape
    layer_count, block, columns_in = dense_in.shape
    units = columns_in // width - 4
    seq, deep, reps = lax.axis_size("seq"), lax.axis_size("fsdp"), lax.axis_size("rep")
    half = seq // clip_count
    total_frames = local_frames * seq
    place, depth = lax.axis_index("seq"), lax.axis_index("fsdp")
    owners = seq * deep
    my_clip, my_member = place // half, place % half
    in_lower = my_clip == 0
    swap = [(source, (source + half) % seq) for source in range(seq)]
    far = seq // 2
    row, core = place // 2, place % 2
    cut = (far, deep, block) if block % 16 == 0 else None

    def turn(axis, step):
        size = lax.axis_size(axis)
        return [(source, (source + step) % size) for source in range(size)]

    over_core = [(source, source ^ 1) for source in range(seq)]

    def to_clips(arrays):
        whole = jnp.stack(arrays, axis=1)
        kept = lax.dynamic_index_in_dim(whole, my_clip, 0, keepdims=False)
        given = lax.dynamic_index_in_dim(whole, 1 - my_clip, 0, keepdims=False)
        taken = lax.ppermute(given, "seq", swap)
        lower, upper = jnp.where(in_lower, kept, taken), jnp.where(in_lower, taken, kept)
        return [
            jnp.concatenate([lower[number], upper[number]], axis=0).astype(F32)
            for number in range(len(arrays))
        ]

    def split_clips(rows):
        lower, upper = rows[:local_frames], rows[local_frames:]
        return jnp.where(in_lower, lower, upper), jnp.where(in_lower, upper, lower).astype(LOW)

    def from_clips(kept, given):
        taken = lax.ppermute(given, "seq", swap).astype(kept.dtype)
        return jnp.stack([jnp.where(in_lower, kept, taken), jnp.where(in_lower, taken, kept)])

    def around(step):
        return [
            (source, source - source % half + (source % half + step) % half)
            for source in range(seq)
        ]

    halves = 2 if reps == 2 and units % 2 == 0 and deep % 2 == 0 and cut is not None else 1
    info = jnp.stack([lax.axis_index("rep"), core])

    def gather(layer, extra, after):
        if cut is None:
            columns = dense_in[layer].astype(LOW).reshape(block, 4 + units, width)
            columns = columns.transpose(1, 0, 2)
            columns = lax.all_gather(columns, ("fsdp", "seq"), axis=1, tiled=True)
            rows = lax.all_gather(
                dense_out[layer].astype(LOW), ("fsdp", "seq"), axis=0, tiled=True
            )
            parts = [columns[4:].reshape(-1, width), rows, columns[3], *columns[:3]]
            return Wide(jnp.concatenate(parts)[None], None, info, width, units)
        own = pack(dense_in, dense_out, layer, units, halves, info, extra, after)
        chunk = lax.all_gather(own, ("fsdp", "seq"), axis=0)
        if halves == 1:
            return Wide(chunk, None, info, block, units)
        return Wide(chunk, [None, None], info, block, units)

    def share(wide, marker):
        wide.given = []
        if wide.sent:
            wide.chunk, marker = lax.optimization_barrier((wide.chunk, marker))
            rows = units // 2 * block
            shape = (owners // 2, rows, width)
            wide.given = [
                lax.dynamic_slice(wide.chunk, (core * (owners // 2), number * rows, 0), shape)
                for number in range(2)
            ]
            wide.near = [lax.ppermute(part, "rep", turn("rep", 1)) for part in wide.given]
        return marker

    def exchange(wide, number, marker):
        if wide.sent:
            near, marker = lax.optimization_barrier((wide.near[number], marker))
            wide.sent[number] = (near, lax.ppermute(near, "seq", over_core))
        return marker

    targets = jnp.stack(
        [
            (row + step) % far * 2 + (core + other) % 2
            for other in range(2)
            for step in range(far)
        ]
    )

    def start_core(parts):
        if cut is None:
            return parts, []
        return (parts[0], lax.ppermute(parts[1], "seq", over_core)), [parts[0]]

    def start_far(chunk, after):
        if cut is None:
            return chunk
        keep, taken = chunk[0]
        sums = [sum_along(keep, taken, step, after) for step in range(1, far)]
        moved = [
            lax.ppermute(part, "seq", turn("seq", 2 * step + 2)) for step, part in enumerate(sums)
        ]
        return (keep, taken, moved), sums

    def whole_deep(chunk, after):
        if cut is None:
            return chunk
        total = sum_near(*chunk[0], after)
        return lax.psum_scatter(total, "fsdp", scatter_dimension=0, tiled=True)[0], [total]

    def start_reps(chunk):
        if cut is None:
            result = chunk[0][0]
            owned = lax.psum_scatter(
                result[:units], ("fsdp", "seq"), scatter_dimension=1, tiled=True
            )
            if result.shape[0] > units:
                rows = lax.psum_scatter(
                    result[units:].reshape(units * width, width),
                    ("fsdp", "seq"),
                    scatter_dimension=0,
                    tiled=True,
                )
                owned = jnp.concatenate([owned, rows.reshape(units, block, width)])
        else:
            owned = chunk[0]
        return owned, [lax.ppermute(owned, "rep", turn("rep", step)) for step in range(1, reps)]

    def finish(state):
        owned, arrived = state
        return sum([part.astype(F32) for part in arrived], owned.astype(F32))

    length = lax.dynamic_index_in_dim(lengths, my_clip, 0, keepdims=False)
    bias = jnp.stack(
        [
            jnp.broadcast_to(
                jnp.where(
                    (half + (my_member - step) % half) * local_frames
                    + jnp.arange(local_frames, dtype=jnp.int32)
                    < length,
                    0.0,
                    MASKED,
                )[:, None],
                (local_frames, LANES),
            )
            for step in range(half)
        ]
    ).astype(F32)

    small_low = small_params.astype(LOW)
    extra = None
    if cut is not None:
        extra = jnp.pad(small_low.reshape(-1), (0, -small_low.size % (16 * width)))
        extra = extra.reshape(-1, width)
    wides = []
    for layer in range(layer_count):
        wides.append(gather(layer, extra if layer == 0 else None, []))
    if cut is None:
        params_all = lax.all_gather(small_low, ("fsdp", "seq"), axis=2, tiled=True)
    else:
        first_row = (wides[0].thin_at + 3) * block
        params_all = wides[0].chunk[:, first_row:].reshape(owners, -1)[:, : small_low.size]
        params_all = params_all.reshape((owners,) + small_low.shape).transpose(1, 2, 0, 3)
        params_all = params_all.reshape(layer_count, -1, width)
    params_all = params_all.astype(F32)

    row_steps = units if cut is None else deep
    hidden, upstream = to_clips([frames, cotangent])
    stored = []
    for layer_index in range(layer_count):
        params = params_all[layer_index]
        wide = wides[layer_index]
        normed_low, queries, own = project(
            hidden, params, wide.chunk, wide.block, wide.thin_at, []
        )
        own = share(wide, own)
        others = [lax.ppermute(own, "seq", around(step)) for step in range(1, half)]
        mixed_out, log_total = attend(queries, own, others, bias, wide.given)
        mixed_out = exchange(wide, 0, mixed_out)
        middle, second_low, active, slope = inner(hidden, mixed_out, params, wide, [])
        middle = exchange(wide, 1, middle)
        stored.append(
            (hidden, normed_low, queries, own, others, log_total, mixed_out)
            + (middle, second_low, active, slope)
        )
        if layer_index + 1 < layer_count:
            hidden = outer(middle, active, params, wide, row_steps, [])
    groups = 2 if width // LANES % 2 == 0 else 1
    def arrivals(number):
        return [
            part
            for layer in range(1, layer_count)
            for some in parts_out[layer][number : number + 1]
            for part in some[1]
        ]

    order = []
    waiting = None
    parts_out = {}
    done_in, done_out = (), ()
    rows_shape = (layer_count, units, block, width)
    states_in = (dense_in, first_in, second_in)
    states_out = (dense_out, first_out, second_out)
    if cut is None:
        states_out = [array.reshape(rows_shape) for array in states_out]
    rates_in = (RATE_DENSE, RATE_DENSE * math.sqrt(total_frames / 3.0), 3)
    rates_out = (RATE_OUTER, RATE_OUTER, 0)

    def flat(part):
        return [part[0]] + part[1]

    small_grads = []
    for layer_index in reversed(range(layer_count)):
        wide = wides[layer_index]
        params = params_all[layer_index]
        (
            hidden,
            normed_low,
            queries,
            own,
            others,
            log_total,
            mixed_out,
            middle,
            second_low,
            active,
            slope,
        ) = stored[layer_index]
        outer_low, inner_grad, bias_inner, bias_outer = outer_back(
            upstream, slope, wide, row_steps, order
        )
        order = [inner_grad]
        if waiting:
            waiting = start_far(waiting, order)
            order = order + waiting[1]
        wide_part = start_core(
            wide_weight_grad(
                cut, targets, second_low, inner_grad, active, outer_low, units, order
            )
        )
        middle_grad, branch_low, mixed_grad, sums_two = inner_back(
            inner_grad, upstream, middle, params, wide, wide_part[1]
        )
        order = [middle_grad]
        wide_part = start_far(wide_part, order)
        order = order + wide_part[1]
        q_terms, k_near, v_near, k_far, v_far = [], [], [], [], []
        for group in range(groups):
            q_term, k_terms, v_terms = attend_back(
                queries,
                own,
                others,
                mixed_out,
                mixed_grad,
                log_total,
                bias,
                group,
                groups,
                order,
            )
            q_terms.append(q_term)
            k_near.append(k_terms[0])
            v_near.append(v_terms[0])
            k_far.append(k_terms[1:])
            v_far.append(v_terms[1:])
            order = [q_term]
            if waiting and group == 0:
                waiting = whole_deep(waiting, order)
                order = order + waiting[1]

        def all_terms(near, terms):
            moved = [
                lax.ppermute(terms[group][step - 1], "seq", around(half - step))
                for step in range(1, half)
                for group in range(groups)
            ]
            return list(near) + moved

        terms = [q_terms, all_terms(k_near, k_far), all_terms(v_near, v_far)]
        order = [q_terms[-1]]

        if layer_index == 0:
            if waiting:
                waiting = start_reps(waiting)
                parts_out[1] += (waiting,)
            thin_part = start_core(
                thin_weight_grad(
                    cut, targets, normed_low, terms, mixed_out, branch_low, order
                )
            )
            wide_part = whole_deep(wide_part, thin_part[1] + arrivals(0))
            for layer in reversed(range(1, layer_count)):
                last = flat(parts_out[layer][0])
                done_out = adam(
                    states_out, last, layer, 0, units, units, rates_out, wide_part[1], done_out
                )
            thin_part = start_far(thin_part, list(done_out[:1]) + arrivals(1))
            order = thin_part[1]
        upstream, sums_one = project_back(
            hidden, middle_grad, params, terms, wide.chunk, wide.block, wide.thin_at, order
        )
        if layer_index > 0:
            if waiting:
                waiting = start_reps(waiting)
                parts_out[layer_index + 1] += (waiting,)
            wide_part = whole_deep(wide_part, [upstream])
            thin_part = start_core(
                thin_weight_grad(
                    cut,
                    targets,
                    normed_low,
                    terms,
                    mixed_out,
                    branch_low,
                    [upstream] + wide_part[1],
                )
            )
        waiting = thin_part
        order = waiting[1]
        parts_out[layer_index] = (start_reps(wide_part) if layer_index > 0 else wide_part,)
        small_grads = [sums_one, sums_two, bias_outer, bias_inner] + small_grads
    if cut is not None:
        keep, give = small_cut(cut, targets, small_grads, layer_count, [upstream])
        cuts = keep + lax.ppermute(give, "seq", over_core)
        along = [lax.ppermute(cuts[step], "seq", turn("seq", 2 * step)) for step in range(1, far)]

    middle, active = stored[-1][7], stored[-1][9]
    result = outer(middle, active, params_all[-1], wides[-1], row_steps, [upstream])
    for layer in reversed(range(1, layer_count)):
        last = flat(parts_out[layer][0])
        done_in = adam(states_in, last, layer, 4, units, 0, rates_in, [result], done_in)
    waiting = whole_deep(waiting, list(done_out[:1]) + list(done_in[:1]) + [result])
    order = waiting[1] or [upstream]
    ready = order + (along if cut else [])
    encoded = from_clips(*part_clips(in_lower.astype(jnp.int32).reshape(1), result, LOW, ready))
    for layer in reversed(range(1, layer_count)):
        last = flat(parts_out[layer][1])
        done_in = adam(states_in, last, layer, 0, 4, 0, rates_in, order, done_in)
    wide_part = parts_out[0][0]
    if cut is not None and done_in:
        mine, *done_in = lax.optimization_barrier((wide_part[0], *done_in))
        wide_part = (mine, wide_part[1])
    wide_part = start_reps(wide_part)
    ready = order + list(done_in[:1])
    frames_grad = from_clips(
        *part_clips(in_lower.astype(jnp.int32).reshape(1), upstream, F32, ready)
    )
    if cut is not None:
        total = sum(along, cuts[0])
        deeper = [
            lax.ppermute(
                lax.dynamic_index_in_dim(total, (depth + step) % deep, 0, keepdims=False),
                "fsdp",
                turn("fsdp", step),
            )
            for step in range(1, deep)
        ]
    done_in = adam(states_in, flat(wide_part), 0, 4, units, 0, rates_in, order, done_in)
    thin_part = start_reps(waiting)
    order = order + [done_in[0], thin_part[0]]
    done_out = adam(states_out, flat(wide_part), 0, 0, units, units, rates_out, order, done_out)
    if cut is None:
        small_all = jnp.stack(
            [
                jnp.concatenate([one[:4], two[2:3], two[:2], outer_sums])
                for one, two, outer_sums, _ in zip(*[iter(small_grads)] * 4)
            ]
        )
        inner_all = jnp.stack([part.reshape(units, width) for part in small_grads[3::4]])
        small_all = jnp.concatenate([small_all, inner_all], axis=1)
        small_all = small_all.reshape(layer_count, -1, owners, block).transpose(2, 0, 1, 3)
        owned_small = lax.psum_scatter(
            small_all, ("fsdp", "seq"), scatter_dimension=0, tiled=True
        )
    else:
        (total, *deeper, _) = lax.optimization_barrier((total, *deeper, done_in[0]))
        owned_small = lax.dynamic_index_in_dim(total, depth, 0, keepdims=False)
        owned_small = sum(deeper, owned_small)[:, :block]
    owned_small = owned_small.reshape(small_params.shape).astype(LOW)
    done_in = adam(states_in, flat(thin_part), 0, 0, 4, 0, rates_in, [done_out[0]], done_in)
    grad_in, moment_in, square_in, updated_in = done_in
    grad_out_rows, moment_out, square_out, updated_out = (
        array.reshape(dense_out.shape) for array in done_out
    )
    grad_small = finish(
        (owned_small, [lax.ppermute(owned_small, "rep", turn("rep", s)) for s in range(1, reps)])
    )
    moment_small, square_small, updated_small = adam_step(
        small_params, grad_small, first_small, second_small, RATE_SMALL
    )
    return (
        encoded,
        frames_grad,
        grad_in,
        grad_out_rows,
        grad_small,
        moment_in,
        moment_out,
        moment_small,
        square_in,
        square_out,
        square_small,
        updated_in,
        updated_out,
        updated_small,
    )


def solution(mesh):
    clips = P(("rep", "fsdp"), "seq", None)
    rows = P(None, ("fsdp", "seq"), None)
    lanes = P(None, None, ("fsdp", "seq"))
    return jax.shard_map(
        on_device,
        mesh=mesh,
        in_specs=(clips, P(("rep", "fsdp")), clips) + (rows, rows, lanes) * 3,
        out_specs=(clips, clips) + (rows, rows, lanes) * 4,
        check_vma=False,
    )
```
